32 devices in a mesh: dp: 8 (over y, x, core), mp: 4 (over z).
Axes of the slice: x: 2, y: 2, z: 4, core: 2. Of those that a mesh axis runs over, the one named last changes fastest.
Arguments:
- hidden_in: bfloat16 [8192, 2048], P('dp'), may hold values from -6 to 6
- cotangent: bfloat16 [8192, 2048], P('dp'), may hold values from -6 to 6
- doc_lengths: int32 [8, 8], replicated, may hold values from 1 to 256, 1024 in all within a row
- w_query: bfloat16 [2048, 2048], P('dp', 'mp'), may hold values from -0.125 to 0.125
- w_key: bfloat16 [2048, 1024], P('dp', 'mp'), may hold values from -0.125 to 0.125
- w_value: bfloat16 [2048, 1024], P('dp', 'mp'), may hold values from -0.125 to 0.125
- w_out: bfloat16 [2048, 2048], P('mp', 'dp'), may hold values from -1 to 1
- w_gate: bfloat16 [2048, 6144], P('dp', 'mp'), may hold values from -0.125 to 0.125
- w_up: bfloat16 [2048, 6144], P('dp', 'mp'), may hold values from -0.125 to 0.125
- w_down: bfloat16 [6144, 2048], P('mp', 'dp'), may hold values from -0.078125 to 0.078125
- norm_attn: bfloat16 [2048], P('dp'), may hold values from 0.099609375 to 1.8984375
- norm_mlp: bfloat16 [2048], P('dp'), may hold values from 0.099609375 to 1.8984375
- norm_query: bfloat16 [128], P('dp'), may hold values from 0.099609375 to 1.8984375
- norm_key: bfloat16 [128], P('dp'), may hold values from 0.099609375 to 1.8984375
Outputs:
- output: bfloat16 [8192, 2048], P('dp')
- grad_input: float32 [8192, 2048], P('dp')
- grad_query_w: float32 [2048, 2048], P('dp', 'mp')
- grad_key_w: float32 [2048, 1024], P('dp', 'mp')
- grad_value_w: float32 [2048, 1024], P('dp', 'mp')
- grad_out_w: float32 [2048, 2048], P('mp', 'dp')
- grad_gate_w: float32 [2048, 6144], P('dp', 'mp')
- grad_up_w: float32 [2048, 6144], P('dp', 'mp')
- grad_down_w: float32 [6144, 2048], P('mp', 'dp')
- grad_norm_attn: float32 [2048], P('dp')
- grad_norm_mlp: float32 [2048], P('dp')
- grad_norm_query: float32 [128], P('dp')
- grad_norm_key: float32 [128], P('dp')
The draws below stay inside these ranges and needn't reach their ends.
Inputs may be any that keep to these rules, and one draw needn't show every extreme that they name: Each row of doc_lengths sums to 1024 and its largest entry is 256.
All inputs are finite; a program needn't handle non-finite values.
Results may differ from the reference program's by a relative error of at most 0.015.
Values may be sent and summed in bfloat16 or wider, within the bound.
No kernel may reach another device: no remote copies, remote signals or barrier semaphores. Data moves between devices by JAX's collectives and lax.ppermute only.
A program may use at most 256 MiB of HBM per device.

```python
import math
import jax
import jax.numpy as jnp
import numpy as np
from jax import lax

D = 2048
HEADS = 16
KV = 8
HD = 128
FF = 6144
ROW = 1024
TOKENS = 8192
ROWS = 8
DOCS_ROW = 8
DOC_MOST = 256


def spiked(array, own_key, source, target, parts, factor):
    owner, partner = [(jnp.arange(array.shape[dim]) // (array.shape[dim] // parts)).reshape([-1 if axis == dim else 1 for axis in range(array.ndim)]) for dim in (source, target)]
    chosen = jax.random.permutation(own_key, parts)[partner]
    strong = (owner == chosen) | (owner == (partner + parts // 2) % parts)
    return jnp.where(strong, factor * array, array)


def steps_of(stream_key, shape, pieces, low, high):
    factor_of = 1.0
    for dim, blocks in pieces:
        steps = jax.random.uniform(jax.random.fold_in(jax.random.fold_in(stream_key, 6), dim), (blocks,), jnp.float32, low / len(pieces), high / len(pieces))
        factor_of = factor_of * jnp.repeat(jnp.exp(steps), shape[dim] // blocks).reshape((-1,) + (1,) * (len(shape) - 1 - dim))
    return factor_of


def length_profile(count, total, bound, skew):
    weights = [(1 << 20) // math.isqrt(rank ** skew) + 1 for rank in range(2, count + 1)]
    surplus, given = total - bound - (count - 1), [1] * (count - 1)
    while surplus > 0:
        candidates = [i for i in range(count - 1) if given[i] < bound]
        pool, left = sum([weights[i] for i in candidates]), surplus
        for i in candidates:
            more = min(bound - given[i], max(1, left * weights[i] // pool), surplus)
            given[i] = given[i] + more
            surplus = surplus - more
    return np.array([bound] + given)


def ragged_sizes(key, count, total, most, skew):
    if count == 2:
        one = jax.random.randint(key, (), max(1, total - most), min(most, total - 1) + 1)
        return jnp.stack([one, total - one])
    lengths = jnp.asarray(length_profile(count, total, most, skew), jnp.int32)
    couples = (count - 1) // 2
    source_of, sink = lengths[1:1 + 2 * couples:2], lengths[2:2 + 2 * couples:2]
    margin = jnp.minimum(source_of - 1, most - sink)
    passed = jax.random.randint(jax.random.fold_in(key, 1), (couples,), 0, 1 << 20) % (margin + 1)
    lengths = lengths.at[1:1 + 2 * couples:2].set(source_of - passed).at[2:2 + 2 * couples:2].set(sink + passed)
    return lengths[jax.random.permutation(jax.random.fold_in(key, 2), count)]


def centred(own_key, shape, scale, reach, split=(), kind=jnp.bfloat16):
    loudness = steps_of(own_key, shape, split, -0.22, 0.18) if split else 1.0
    result = jax.random.normal(own_key, shape, jnp.float32) * scale * loudness
    return jnp.minimum(jnp.maximum(result, -reach), reach).astype(kind)


def noise_with(rng, dims, deviation, reach, pieces, heavy, held_as=jnp.bfloat16):
    drawn = deviation * jax.random.normal(rng, dims, jnp.float32)
    if pieces:
        drawn = drawn * steps_of(rng, dims, pieces, -0.22, 0.18)
    return jnp.clip(spiked(drawn, jax.random.fold_in(rng, 3), *heavy), -reach, reach).astype(held_as)


def setup_inputs(seed: int = 0) -> dict:
    key_list = jax.random.split(jax.random.key(seed), 15)
    hidden_in = centred(key_list[0], (TOKENS, D), 1.0, 6.0, ((0, 8),))
    cotangent = noise_with(key_list[1], (TOKENS, D), 1.0, 6.0, ((0, 8),), (0, 1, 8, 2.0))
    doc_lengths = jax.vmap(lambda own: ragged_sizes(own, DOCS_ROW, ROW, DOC_MOST, 2))(jax.random.split(key_list[2], ROWS)).reshape((ROWS, DOCS_ROW)).astype(jnp.int32)
    w_query = centred(key_list[3], (D, HEADS * HD), D ** -0.5, 0.125, ((0, 8), (1, 4)))
    w_key = centred(key_list[4], (D, KV * HD), D ** -0.5, 0.125, ((0, 8), (1, 4)))
    w_value = centred(key_list[5], (D, KV * HD), D ** -0.5, 0.125, ((0, 8), (1, 4)))
    w_out = centred(key_list[6], (HEADS * HD, D), (HD // 4) ** -0.5, 1.0, ((0, 4), (1, 8)))
    w_gate = centred(key_list[7], (D, FF), D ** -0.5, 0.125, ((0, 8), (1, 4)))
    w_up = centred(key_list[8], (D, FF), D ** -0.5, 0.125, ((0, 8), (1, 4)))
    w_down = centred(key_list[9], (FF, D), FF ** -0.5, 0.078125, ((0, 4), (1, 8)))
    norm_attn = jnp.clip(1.0 + 0.18 * jax.random.normal(key_list[10], (D,), jnp.float32), 0.099609375, 1.8984375).astype(jnp.bfloat16)
    norm_mlp = jnp.clip(1.0 + 0.18 * jax.random.normal(key_list[11], (D,), jnp.float32), 0.099609375, 1.8984375).astype(jnp.bfloat16)
    norm_query = jnp.clip(1.0 + 0.18 * jax.random.normal(key_list[12], (HD,), jnp.float32), 0.099609375, 1.8984375).astype(jnp.bfloat16)
    norm_key = jnp.clip(1.0 + 0.18 * jax.random.normal(key_list[13], (HD,), jnp.float32), 0.099609375, 1.8984375).astype(jnp.bfloat16)
    return {"hidden_in": hidden_in, "cotangent": cotangent, "doc_lengths": doc_lengths, "w_query": w_query, "w_key": w_key, "w_value": w_value, "w_out": w_out, "w_gate": w_gate, "w_up": w_up, "w_down": w_down, "norm_attn": norm_attn, "norm_mlp": norm_mlp, "norm_query": norm_query, "norm_key": norm_key}


EPSILON = 1e-06
ROPE_BASE = 1000000.0
HIGHEST = lax.Precision.HIGHEST

@jax.custom_vjp
def low(v):
    return lax.optimization_barrier(v.astype(jnp.bfloat16)).astype(jnp.float32)

@jax.custom_vjp
def low_back(v):
    return v

def low_keep(v):
    return (low(v), None)

def low_pass(kept, grad):
    return (grad,)

def back_keep(v):
    return (v, None)

def back_low(kept, grad):
    return (low(grad),)
low.defvjp(low_keep, low_pass)
low_back.defvjp(back_keep, back_low)

def rms_scale(values, scale_gain):
    return values * lax.rsqrt(lax.optimization_barrier(jnp.mean(values * values, axis=-1, keepdims=True)) + EPSILON) * scale_gain

def rotate(values, position):
    half_dim = values.shape[-1] // 2
    inverse = ROPE_BASE ** (-(2.0 * jnp.arange(half_dim, dtype=jnp.float32)) / values.shape[-1])
    angles = position.astype(jnp.float32)[:, None] * inverse[None, :]
    cosine = jnp.cos(angles)[:, None, :]
    sine_part = jnp.sin(angles)[:, None, :]
    first_half = values[..., :half_dim]
    second_half = values[..., half_dim:]
    return jnp.concatenate([first_half * cosine - second_half * sine_part, second_half * cosine + first_half * sine_part], axis=-1)

def attend(queries, key_rows, value_rows):
    length = queries.shape[0]
    group_size = queries.shape[1] // key_rows.shape[1]
    keys_all = jnp.repeat(key_rows, group_size, axis=1)
    values_all = jnp.repeat(value_rows, group_size, axis=1)
    scores = jnp.einsum('qhd,khd->hqk', queries, keys_all, precision=HIGHEST) * queries.shape[-1] ** (-0.5)
    scores = low_back(scores)
    causal = jnp.arange(length, dtype=jnp.int32)[:, None] >= jnp.arange(length, dtype=jnp.int32)[None, :]
    scores = jnp.where(causal[None], scores, -1e+30)
    weights = jax.nn.softmax(scores, axis=-1)
    return jnp.einsum('hqk,khd->qhd', low(weights), values_all, precision=HIGHEST)

def reference(hidden_in, cotangent, doc_lengths, w_query, w_key, w_value, w_out, w_gate, w_up, w_down, norm_attn, norm_mlp, norm_query, norm_key):
    tokens = hidden_in.shape[0]
    doc_count = doc_lengths.shape[0] * doc_lengths.shape[1]
    starts = (jnp.cumsum(doc_lengths, axis=1) - doc_lengths).astype(jnp.int32)
    row_base = jnp.arange(doc_lengths.shape[0], dtype=jnp.int32)[:, None] * ROW
    doc_begin = (starts + row_base).reshape(-1).astype(jnp.int32)
    doc_finish = (doc_begin + doc_lengths.reshape(-1)).astype(jnp.int32)
    positions = jnp.arange(tokens, dtype=jnp.int32)
    member = (positions[:, None] >= doc_begin[None, :]) & (positions[:, None] < doc_finish[None, :])
    doc_index = lax.optimization_barrier(jnp.sum(jnp.where(member, jnp.arange(doc_count, dtype=jnp.int32)[None, :], 0), axis=1)).astype(jnp.int32)
    within = (positions - lax.optimization_barrier(jnp.sum(jnp.where(member, doc_begin[None, :], 0), axis=1))).astype(jnp.int32)
    token_rows = (doc_index * DOC_MOST + within).astype(jnp.int32)

    def slots(values):
        padded = jnp.concatenate([values, jnp.zeros((DOC_MOST,) + values.shape[1:], values.dtype)], axis=0)

        def take_doc(offset, amount):
            window = lax.dynamic_slice_in_dim(padded, offset.astype(jnp.int32), DOC_MOST, axis=0)
            inside = (jnp.arange(DOC_MOST, dtype=jnp.int32) < amount).astype(values.dtype)
            return window * inside[:, None, None]
        return jax.vmap(take_doc)(doc_begin, doc_finish - doc_begin)

    def forward(hidden, wq_full, wk_full, wv_full, wo_full, wg_full, wu_full, wd_full, gain_attn, gain_mlp, gain_query, gain_key):
        normed = low(rms_scale(hidden, gain_attn))
        queries = low_back(jnp.dot(normed, wq_full, precision=HIGHEST)).reshape(tokens, HEADS, HD)
        key_part = low_back(jnp.dot(normed, wk_full, precision=HIGHEST)).reshape(tokens, KV, HD)
        value_part = low_back(low(jnp.dot(normed, wv_full, precision=HIGHEST))).reshape(tokens, KV, HD)
        queries = low_back(low(rotate(rms_scale(queries, gain_query), within)))
        key_part = low_back(low(rotate(rms_scale(key_part, gain_key), within)))
        outputs = lax.map(jax.checkpoint(lambda triple: attend(triple[0], triple[1], triple[2])), (slots(queries), slots(key_part), slots(value_part)))
        flat_rows = outputs.reshape(doc_count * DOC_MOST, HEADS, HD)
        attended = jnp.take(flat_rows, token_rows, axis=0).reshape(tokens, HEADS * HD)
        attended = low_back(low(attended))
        branch = low_back(jnp.dot(attended, wo_full, precision=HIGHEST))
        middle = hidden + branch
        normed_two = low(rms_scale(middle, gain_mlp))
        gate_lin = low_back(jnp.dot(normed_two, wg_full, precision=HIGHEST))
        upward = low_back(jnp.dot(normed_two, wu_full, precision=HIGHEST))
        product = low(jax.nn.silu(gate_lin) * upward)
        return middle + low_back(jnp.dot(product, wd_full, precision=HIGHEST))
    primal = tuple((array_in.astype(jnp.float32) for array_in in (hidden_in, w_query, w_key, w_value, w_out, w_gate, w_up, w_down, norm_attn, norm_mlp, norm_query, norm_key)))
    output, pullback = jax.vjp(forward, *primal)
    gradients = pullback(cotangent.astype(jnp.float32))
    return (output.astype(jnp.bfloat16), gradients[0], gradients[1], gradients[2], gradients[3], gradients[4], gradients[5], gradients[6], gradients[7], gradients[8], gradients[9], gradients[10], gradients[11])
```

```python
import functools

import jax
import jax.numpy as jnp
from jax import lax
from jax.experimental import pallas as pl
from jax.experimental.pallas import tpu as pltpu
from jax.sharding import PartitionSpec as P

HD = 128
CHUNK = 256
EPSILON = 1e-06
ROPE_BASE = 1000000.0
SCALE = HD ** (-0.5)
BF = jnp.bfloat16
F32 = jnp.float32
VMEM_LIMIT = 56 * 1024 * 1024

NN = (((1,), (0,)), ((), ()))
NT = (((1,), (1,)), ((), ()))
TN = (((0,), (0,)), ((), ()))


def dot(a, b, dims=NN):
    return lax.dot_general(a, b, dims, preferred_element_type=F32)


def whole():
    return pl.BlockSpec(memory_space=pltpu.VMEM)


def smem():
    return pl.BlockSpec(memory_space=pltpu.SMEM)


def hbm():
    return pl.BlockSpec(memory_space=pl.ANY)


def params(**kw):
    return pltpu.CompilerParams(vmem_limit_bytes=VMEM_LIMIT, **kw)


def cost(flops, nbytes):
    return pl.CostEstimate(flops=int(flops), bytes_accessed=int(nbytes), transcendentals=0)


def rms_r(values):
    return lax.rsqrt(jnp.mean(values * values, axis=-1, keepdims=True) + EPSILON)


def qkv_kernel(nq, nk, pieces, x_ref, gain_ref, w_ref, cos_ref, sin_ref, gq_ref, gk_ref, normed_ref, lin_ref, rot_ref):
    x = x_ref[...].astype(F32)
    normed = (x * rms_r(x) * gain_ref[...]).astype(BF)
    normed_ref[...] = normed
    depth = x.shape[1] // pieces
    acc = jnp.zeros((x.shape[0], w_ref.shape[2]), F32)
    for p in range(pieces):
        acc = acc + dot(normed[:, p * depth : (p + 1) * depth], w_ref[p, :depth, :])
    cosine = cos_ref[...]
    sine = sin_ref[...]
    for h in range(nq + nk):
        v = acc[:, h * HD : (h + 1) * HD]
        gain = gq_ref[...] if h < nq else gk_ref[...]
        n = v * rms_r(v) * gain
        rot_ref[:, h * HD : (h + 1) * HD] = (n * cosine + pltpu.roll(n, HD // 2, 1) * sine).astype(BF)
    lin_ref[...] = acc[:, : (nq + nk) * HD]
    rot_ref[:, (nq + nk) * HD :] = acc[:, (nq + nk) * HD :].astype(BF)


def qkv_call(x, gain, w, cosine, sine, gq, gk, nq, nk):
    tok, d = x.shape
    pieces = w.shape[0]
    cols = w.shape[2]
    blk = lambda n: pl.BlockSpec((CHUNK, n), lambda i: (i, 0))
    full = lambda a: pl.BlockSpec(a.shape, lambda i: (0,) * a.ndim)
    lin = (nq + nk) * HD
    return pl.pallas_call(
        functools.partial(qkv_kernel, nq, nk, pieces),
        grid=(tok // CHUNK,),
        in_specs=[blk(d), full(gain), full(w), blk(HD), blk(HD), full(gq), full(gk)],
        out_specs=[blk(d), blk(lin), blk(cols)],
        out_shape=[
            jax.ShapeDtypeStruct((tok, d), BF),
            jax.ShapeDtypeStruct((tok, lin), F32),
            jax.ShapeDtypeStruct((tok, cols), BF),
        ],
        compiler_params=params(),
        cost_estimate=cost(2 * tok * d * cols * 1.5, 20e6),
    )(x, gain, w, cosine, sine, gq, gk)


def band(c):
    lo = max(c - 1, 0) * CHUNK
    return lo, (c + 1) * CHUNK - lo


def allowed(c, col_ref, row_ref):
    lo, width = band(c)
    same = col_ref[c * CHUNK : (c + 1) * CHUNK, :] == row_ref[:, lo : lo + width]
    t = lax.broadcasted_iota(jnp.int32, (CHUNK, width), 0) + c * CHUNK
    u = lax.broadcasted_iota(jnp.int32, (CHUNK, width), 1) + lo
    return same & (u <= t)


def attn_kernel(c, nq, nk, aliased, rot_ref, col_ref, row_ref, w_ref, *rest):
    att_ref, lse_ref, part_ref = rest[1:] if aliased else rest
    lo, width = band(c)
    mask = allowed(c, col_ref, row_ref)
    group = nq // nk
    heads = []
    lses = []
    for h in range(nq):
        q = rot_ref[c * CHUNK : (c + 1) * CHUNK, h * HD : (h + 1) * HD]
        j = h // group
        k = rot_ref[lo : lo + width, (nq + j) * HD : (nq + j + 1) * HD]
        v = rot_ref[lo : lo + width, (nq + nk + j) * HD : (nq + nk + j + 1) * HD]
        s = jnp.where(mask, dot(q, k, NT) * SCALE, -1e30)
        m = jnp.max(s, axis=-1, keepdims=True)
        e = jnp.exp(s - m)
        l = jnp.sum(e, axis=-1, keepdims=True)
        heads.append(dot((e / l).astype(BF), v).astype(BF))
        lses.append(m + jnp.log(l))
    att = jnp.concatenate(heads, axis=1)
    att_ref[...] = att
    lse_ref[...] = jnp.concatenate(lses, axis=1)
    pieces = w_ref.shape[0]
    width_d = w_ref.shape[2]
    for p in range(pieces):
        part_ref[:, p * width_d : (p + 1) * width_d] = dot(att, w_ref[p]).astype(BF)


def chunk_block(c, n):
    return pl.BlockSpec((CHUNK, n), lambda i: (c, 0))


def attn_call(c, rot, col, row, w_out, att, nq, nk):
    tok = rot.shape[0]
    d = w_out.shape[0] * w_out.shape[2]
    first = att is None
    args = [rot, col, row, w_out] + ([] if first else [att])
    full = lambda a: pl.BlockSpec(a.shape, lambda i: (0,) * a.ndim)
    return pl.pallas_call(
        functools.partial(attn_kernel, c, nq, nk, not first),
        grid=(1,),
        in_specs=[full(a) for a in args[:4]] + ([] if first else [hbm()]),
        out_specs=[
            chunk_block(c, nq * HD),
            pl.BlockSpec((CHUNK, nq), lambda i: (0, 0)),
            pl.BlockSpec((CHUNK, d), lambda i: (0, 0)),
        ],
        out_shape=[
            jax.ShapeDtypeStruct((tok, nq * HD), BF),
            jax.ShapeDtypeStruct((CHUNK, nq), F32),
            jax.ShapeDtypeStruct((CHUNK, d), BF),
        ],
        input_output_aliases={} if first else {4: 0},
        compiler_params=params(),
        cost_estimate=cost(2e9, 6e6),
    )(*args)


def mlp_kernel(
    pieces,
    n_alias,
    flag_ref,
    x_ref,
    t_ref,
    r_ref,
    cot_ref,
    gain_ref,
    wg_ref,
    wu_ref,
    wd_ref,
    *rest,
):
    mid_ref, n2_ref, prod_ref, gg_ref, gu_ref, down_ref, gnt_ref, acc_d, acc_g, n2 = rest[n_alias:]
    j = pl.program_id(0)
    wide = wd_ref.shape[2]

    @pl.when(j == 0)
    def _():
        branch = jnp.where(flag_ref[0] == 1, r_ref[...], t_ref[...]).astype(F32)
        mid = x_ref[...].astype(F32) + branch
        mid_ref[...] = mid
        n = (mid * rms_r(mid) * gain_ref[...]).astype(BF)
        n2[...] = n
        n2_ref[...] = n
        acc_d[...] = jnp.zeros_like(acc_d)
        acc_g[...] = jnp.zeros_like(acc_g)

    g = dot(n2[...], wg_ref[...])
    u = dot(n2[...], wu_ref[...])
    gp = jnp.zeros_like(g)
    for p in range(pieces):
        gp = gp + dot(cot_ref[:, p * wide : (p + 1) * wide], wd_ref[p], NT)
    s = 1.0 / (1.0 + jnp.exp(-g))
    prod = (g * s * u).astype(BF)
    prod_ref[...] = prod
    gg = (gp * u * s * (1.0 + g * (1.0 - s))).astype(BF)
    gu = (gp * g * s).astype(BF)
    gg_ref[...] = gg
    gu_ref[...] = gu
    acc_g[...] += dot(gg, wg_ref[...], NT) + dot(gu, wu_ref[...], NT)
    for p in range(pieces):
        acc_d[:, p * wide : (p + 1) * wide] += dot(prod, wd_ref[p])

    @pl.when(j == pl.num_programs(0) - 1)
    def _():
        down_ref[...] = acc_d[...].astype(BF)
        gnt_ref[...] = acc_g[...].astype(BF)


def mlp_call(c, flag, x, t, r, cot, gain, wg, wu, wd, kept):
    tok, d = x.shape
    ff = wg.shape[1]
    tile = 512 if ff % 512 == 0 else 256
    pieces = wd.shape[0]
    first = kept is None
    blk = chunk_block(c, d)
    own = pl.BlockSpec((CHUNK, d), lambda j: (0, 0))
    ffblk = pl.BlockSpec((CHUNK, tile), lambda j: (c, j))
    full = lambda a: pl.BlockSpec(a.shape, lambda j: (0,) * a.ndim)
    n_alias = 0 if first else 4
    out = pl.pallas_call(
        functools.partial(mlp_kernel, pieces, n_alias),
        grid=(ff // tile,),
        in_specs=[
            smem(),
            blk,
            own,
            own,
            blk,
            full(gain),
            pl.BlockSpec((d, tile), lambda j: (0, j)),
            pl.BlockSpec((d, tile), lambda j: (0, j)),
            pl.BlockSpec((pieces, tile, wd.shape[2]), lambda j: (0, j, 0)),
        ]
        + [hbm()] * n_alias,
        out_specs=[own, blk, ffblk, ffblk, ffblk, own, own],
        out_shape=[
            jax.ShapeDtypeStruct((CHUNK, d), F32),
            jax.ShapeDtypeStruct((tok, d), BF),
            jax.ShapeDtypeStruct((tok, ff), BF),
            jax.ShapeDtypeStruct((tok, ff), BF),
            jax.ShapeDtypeStruct((tok, ff), BF),
            jax.ShapeDtypeStruct((CHUNK, d), BF),
            jax.ShapeDtypeStruct((CHUNK, d), BF),
        ],
        scratch_shapes=[
            pltpu.VMEM((CHUNK, d), F32),
            pltpu.VMEM((CHUNK, d), F32),
            pltpu.VMEM((CHUNK, d), BF),
        ],
        input_output_aliases={} if first else {9: 1, 10: 2, 11: 3, 12: 4},
        compiler_params=params(),
        cost_estimate=cost(12 * CHUNK * d * ff * 1.3, 30e6),
    )(flag, x, t, r, cot, gain, wg, wu, wd, *([] if first else kept))
    return out[0], out[1:5], out[5], out[6]


def back_kernel(
    c,
    nq,
    nk,
    first,
    last,
    flag_ref,
    mid_ref,
    t_ref,
    r_ref,
    cot_ref,
    gain_ref,
    wo_ref,
    rot_ref,
    col_ref,
    row_ref,
    lse_ref,
    lin_ref,
    cos_ref,
    sin_ref,
    gq_ref,
    gk_ref,
    w_ref,
    *rest,
):
    if not first:
        carry_ref, rest = rest[0], rest[3:]
    gm_ref, gb_ref, gqkv_ref, part_ref, gain_out, head_out, carry_out = rest
    gnt = jnp.where(flag_ref[0] == 1, r_ref[...], t_ref[...]).astype(F32)
    mid = mid_ref[...]
    r2 = rms_r(mid)
    h = gnt * gain_ref[...]
    gm = (
        cot_ref[...].astype(F32)
        + r2 * h
        - mid * (r2 * r2 * r2 * jnp.mean(h * mid, axis=-1, keepdims=True))
    )
    gain_out[...] = jnp.sum(gnt * mid * r2, axis=0, keepdims=True)
    gm_ref[...] = gm
    gb = gm.astype(BF)
    gb_ref[...] = gb
    pieces = wo_ref.shape[0]
    wide = wo_ref.shape[2]
    ga = jnp.zeros((CHUNK, nq * HD), F32)
    for p in range(pieces):
        ga = ga + dot(gb[:, p * wide : (p + 1) * wide], wo_ref[p], NT)
    ga = ga.astype(BF)
    lo, width = band(c)
    mask = allowed(c, col_ref, row_ref)
    group = nq // nk
    cosine = cos_ref[...]
    sine = -sin_ref[...]

    def unrope(grad, lin, gain):
        gr = grad * cosine + pltpu.roll(grad, HD // 2, 1) * sine
        rr = rms_r(lin)
        hh = gr * gain
        out = rr * hh - lin * (rr * rr * rr * jnp.mean(hh * lin, axis=-1, keepdims=True))
        return out.astype(BF), jnp.sum(gr * lin * rr, axis=0, keepdims=True)

    sum_q = jnp.zeros((1, HD), F32)
    sum_k = jnp.zeros((1, HD), F32)
    outs = [None] * (nq + 2 * nk)
    for j in range(nk):
        k = rot_ref[lo : lo + width, (nq + j) * HD : (nq + j + 1) * HD]
        v = rot_ref[lo : lo + width, (nq + nk + j) * HD : (nq + nk + j + 1) * HD]
        dk = jnp.zeros((width, HD), F32)
        dv = jnp.zeros((width, HD), F32)
        for g in range(group):
            i = j * group + g
            q = rot_ref[c * CHUNK : (c + 1) * CHUNK, i * HD : (i + 1) * HD]
            gah = ga[:, i * HD : (i + 1) * HD]
            s = jnp.where(mask, dot(q, k, NT) * SCALE, -1e30)
            w = jnp.exp(s - lse_ref[:, i : i + 1])
            gw = dot(gah, v, NT)
            delta = jnp.sum(w * gw, axis=-1, keepdims=True)
            gs = (w * (gw - delta)).astype(BF)
            dq = (dot(gs, k) * SCALE).astype(BF).astype(F32)
            dk = dk + dot(gs, q, TN)
            dv = dv + dot(w.astype(BF), gah, TN)
            outs[i], part = unrope(dq, lin_ref[:, i * HD : (i + 1) * HD], gq_ref[...])
            sum_q = sum_q + part
        dk_own, dv_own = dk[width - CHUNK :], dv[width - CHUNK :]
        if not first:
            dk_own = dk_own + carry_ref[:, j * HD : (j + 1) * HD]
            dv_own = dv_own + carry_ref[:, (nk + j) * HD : (nk + j + 1) * HD]
        carry_out[:, j * HD : (j + 1) * HD] = dk[:CHUNK]
        carry_out[:, (nk + j) * HD : (nk + j + 1) * HD] = dv[:CHUNK]
        dk_own = (dk_own * SCALE).astype(BF).astype(F32)
        outs[nq + j], part = unrope(dk_own, lin_ref[:, (nq + j) * HD : (nq + j + 1) * HD], gk_ref[...])
        sum_k = sum_k + part
        outs[nq + nk + j] = dv_own.astype(BF)
    gqkv = jnp.concatenate(outs, axis=1)
    gqkv_ref[...] = gqkv
    head_out[0:1, :] = sum_q
    head_out[1:2, :] = sum_k
    depth = gb.shape[1] // w_ref.shape[0]
    for p in range(w_ref.shape[0]):
        part_ref[:, p * depth : (p + 1) * depth] = dot(gqkv, w_ref[p, :depth, :], NT).astype(BF)


def back_call(c, flag, mid, t, r, cot, gain, wo, rot, col, row, lse, lin, cosine, sine, gq, gk, w, kept, carry, nq, nk, last):
    tok, d = cot.shape
    first = carry is None
    full = lambda a: pl.BlockSpec(a.shape, lambda i: (0,) * a.ndim)
    args = [flag, mid, t, r, cot, gain, wo, rot, col, row, lse, lin, cosine, sine, gq, gk, w]
    specs = [smem()] + [full(a) for a in args[1:]]
    specs[4] = chunk_block(c, d)
    specs[11] = chunk_block(c, lin.shape[1])
    specs[12] = chunk_block(c, HD)
    specs[13] = chunk_block(c, HD)
    if not first:
        args += [carry, *kept]
        specs += [full(carry), hbm(), hbm()]
    own = lambda n: pl.BlockSpec((CHUNK, n), lambda i: (0, 0))
    cols = (nq + 2 * nk) * HD
    out = pl.pallas_call(
        functools.partial(back_kernel, c, nq, nk, first, last),
        grid=(1,),
        in_specs=specs,
        out_specs=[
            own(d),
            chunk_block(c, d),
            chunk_block(c, cols),
            own(d),
            pl.BlockSpec((1, d), lambda i: (0, 0)),
            pl.BlockSpec((2, HD), lambda i: (0, 0)),
            own(2 * nk * HD),
        ],
        out_shape=[
            jax.ShapeDtypeStruct((CHUNK, d), F32),
            jax.ShapeDtypeStruct((tok, d), BF),
            jax.ShapeDtypeStruct((tok, cols), BF),
            jax.ShapeDtypeStruct((CHUNK, d), BF),
            jax.ShapeDtypeStruct((1, d), F32),
            jax.ShapeDtypeStruct((2, HD), F32),
            jax.ShapeDtypeStruct((CHUNK, 2 * nk * HD), F32),
        ],
        input_output_aliases={} if first else {18: 1, 19: 2},
        compiler_params=params(),
        cost_estimate=cost(6e9, 20e6),
    )(*args)
    return out[0], out[1:3], out[3], out[4], out[5], out[6]


def input_kernel(aliased, flag_ref, x_ref, t_ref, r_ref, gm_ref, gain_ref, *rest):
    out_ref, gain_out = rest[1:] if aliased else rest
    gn = jnp.where(flag_ref[0] == 1, r_ref[...], t_ref[...]).astype(F32)
    x = x_ref[...].astype(F32)
    r1 = rms_r(x)
    h = gn * gain_ref[...]
    out_ref[...] = gm_ref[...] + r1 * h - x * (r1 * r1 * r1 * jnp.mean(h * x, axis=-1, keepdims=True))
    gain_out[...] = jnp.sum(gn * x * r1, axis=0, keepdims=True)


def input_call(c, flag, x, t, r, gm, gain, kept):
    tok, d = x.shape
    own = pl.BlockSpec((CHUNK, d), lambda i: (0, 0))
    first = kept is None
    return pl.pallas_call(
        functools.partial(input_kernel, not first),
        grid=(1,),
        in_specs=[smem(), chunk_block(c, d), own, own, own, pl.BlockSpec((1, d), lambda i: (0, 0))]
        + ([] if first else [hbm()]),
        out_specs=[chunk_block(c, d), pl.BlockSpec((1, d), lambda i: (0, 0))],
        out_shape=[jax.ShapeDtypeStruct((tok, d), F32), jax.ShapeDtypeStruct((1, d), F32)],
        input_output_aliases={} if first else {6: 0},
        compiler_params=params(),
        cost_estimate=cost(1e6, 8e6),
    )(flag, x, t, r, gm, gain, *([] if first else [kept]))


def output_kernel(aliased, flag_ref, mid_ref, t_ref, r_ref, *rest):
    out_ref = rest[-1]
    down = jnp.where(flag_ref[0] == 1, r_ref[...], t_ref[...]).astype(F32)
    out_ref[...] = (mid_ref[...] + down).astype(BF)


def output_call(c, flag, mid, t, r, kept, tok):
    d = mid.shape[1]
    own = pl.BlockSpec((CHUNK, d), lambda i: (0, 0))
    first = kept is None
    return pl.pallas_call(
        functools.partial(output_kernel, not first),
        grid=(1,),
        in_specs=[smem(), own, own, own] + ([] if first else [hbm()]),
        out_specs=chunk_block(c, d),
        out_shape=jax.ShapeDtypeStruct((tok, d), BF),
        input_output_aliases={} if first else {4: 0},
        compiler_params=params(),
        cost_estimate=cost(1e6, 5e6),
    )(flag, mid, t, r, *([] if first else [kept]))


def line_sum(x):
    n = lax.axis_size("mp")
    me = lax.axis_index("mp")
    half = n // 2
    for h in range(half - 1):
        x = x + lax.ppermute(x, "mp", [(h, h + 1), (n - 1 - h, n - 2 - h)])
    x = x + lax.ppermute(x, "mp", [(half - 1, half), (half, half - 1)])
    r = x
    for h in reversed(range(half - 1)):
        r = lax.ppermute(x, "mp", [(h + 1, h), (n - 2 - h, n - 1 - h)])
        if h:
            x = jnp.where((me == h) | (me == n - 1 - h), r, x)
    return x, r


def swap_sum(x, axis):
    n = lax.axis_size(axis)
    step = 1
    while step < n:
        x = x + lax.ppermute(x, axis, [(i, i ^ step) for i in range(n)])
        step *= 2
    return x


def own_sum(rows, axis):
    n = lax.axis_size(axis)
    me = lax.axis_index(axis)
    total = lax.dynamic_index_in_dim(rows, me, 0)
    for step in range(1, n):
        part = lax.dynamic_index_in_dim(rows, me ^ step, 0)
        total = total + lax.ppermute(part, axis, [(i, i ^ step) for i in range(n)])
    return total[0]


def on_device(
    hidden_in,
    cotangent,
    doc_lengths,
    w_query,
    w_key,
    w_value,
    w_out,
    w_gate,
    w_up,
    w_down,
    norm_attn,
    norm_mlp,
    norm_query,
    norm_key,
):
    n_dp = lax.axis_size("dp")
    dp = lax.axis_index("dp")
    mp = lax.axis_index("mp")
    n_mp = lax.axis_size("mp")
    tok, d = hidden_in.shape
    nq = w_query.shape[1] // HD
    nk = w_key.shape[1] // HD
    depth = w_query.shape[0]
    cols = (nq + 2 * nk) * HD
    small = norm_query.shape[0]
    flag = ((mp == 0) | (mp == n_mp - 1)).astype(jnp.int32).reshape(1)

    gains = jnp.concatenate([norm_attn, norm_mlp, norm_query, norm_key])
    per_row = cols
    n_rows = -(-gains.shape[0] // per_row)
    gain_rows = jnp.pad(gains, (0, 16 * per_row * -(-n_rows // 16) - gains.shape[0])).reshape(-1, per_row)
    w_qkv = jnp.concatenate([jnp.concatenate([w_query, w_key, w_value], axis=1), gain_rows], axis=0)
    w_qkv = lax.all_gather(w_qkv, "dp", axis=0)
    w_out = lax.all_gather(w_out, "dp", axis=0)
    w_gate = lax.all_gather(w_gate, "dp", axis=0, tiled=True)
    w_up = lax.all_gather(w_up, "dp", axis=0, tiled=True)
    w_down = lax.all_gather(w_down, "dp", axis=0)
    flat = w_qkv[:, depth:, :].reshape(n_dp, -1)[:, : gains.shape[0]].astype(F32)
    gain_attn = flat[:, :depth].reshape(1, d)
    gain_mlp = flat[:, depth : 2 * depth].reshape(1, d)
    gain_query = flat[:, 2 * depth : 2 * depth + small].reshape(1, HD)
    gain_key = flat[:, 2 * depth + small :].reshape(1, HD)

    lengths = lax.dynamic_index_in_dim(doc_lengths, dp, 0, keepdims=False)
    ends = jnp.cumsum(lengths)
    token = jnp.arange(tok, dtype=jnp.int32)
    passed = token[:, None] >= ends[None, :]
    doc = jnp.sum(passed.astype(jnp.int32), axis=1)
    position = token - jnp.sum(jnp.where(passed, lengths[None, :], 0), axis=1)
    inverse = ROPE_BASE ** (-(2.0 * jnp.arange(HD // 2, dtype=F32)) / HD)
    angles = position.astype(F32)[:, None] * inverse[None, :]
    cosine = jnp.cos(angles)
    sine = jnp.sin(angles)
    cosine = jnp.concatenate([cosine, cosine], axis=1)
    sine = jnp.concatenate([-sine, sine], axis=1)
    col = doc[:, None]
    row = doc[None, :]

    normed, lin, rot = qkv_call(hidden_in, gain_attn, w_qkv, cosine, sine, gain_query, gain_key, nq, nk)

    order = list(reversed(range(tok // CHUNK)))
    att = None
    lse, branch, mid, down, gnt = {}, {}, {}, {}, {}
    for c in order:
        att, lse[c], part = attn_call(c, rot, col, row, w_out, att, nq, nk)
        branch[c] = line_sum(part)
    kept = None
    for c in order:
        t, r = branch[c]
        mid[c], kept, down_part, gnt_part = mlp_call(
            c, flag, hidden_in, t, r, cotangent, gain_mlp, w_gate, w_up, w_down, kept
        )
        gnt[c] = line_sum(gnt_part)
        down[c] = line_sum(down_part)
    n2, prod, gg, gu = kept

    def scatter(a, b):
        g = lax.dot_general(a, b, TN, preferred_element_type=F32).astype(BF)
        return lax.psum_scatter(g, "dp", scatter_dimension=0, tiled=True).astype(F32)

    grad_gate_w = scatter(n2, gg)
    grad_up_w = scatter(n2, gu)
    grad_down_w = scatter(cotangent, prod).T

    kept, carry = None, None
    gm, gn = {}, {}
    sum_mlp = jnp.zeros((1, d), F32)
    sum_head = jnp.zeros((2, HD), F32)
    for c in order:
        t, r = gnt[c]
        gm[c], kept, part, g_mlp, g_head, carry = back_call(
            c, flag, mid[c], t, r, cotangent, gain_mlp, w_out, rot, col, row, lse[c], lin, cosine, sine,
            gain_query, gain_key, w_qkv, kept, carry, nq, nk, c == order[-1],
        )
        gn[c] = line_sum(part)
        sum_mlp = sum_mlp + g_mlp
        sum_head = sum_head + g_head
    gb, gqkv = kept
    grad_qkv_w = scatter(normed, gqkv)
    grad_out_w = scatter(gb, att).T

    output, grad_input = None, None
    sum_attn = jnp.zeros((1, d), F32)
    for c in order:
        output = output_call(c, flag, mid[c], *down[c], output, tok)
    for c in order:
        grad_input, g_attn = input_call(c, flag, hidden_in, *gn[c], gm[c], gain_attn, grad_input)
        sum_attn = sum_attn + g_attn
    sum_head = swap_sum(sum_head, "mp")
    early = own_sum(
        jnp.concatenate(
            [sum_mlp.reshape(n_dp, depth), sum_head[0].reshape(n_dp, small), sum_head[1].reshape(n_dp, small)], axis=1
        ),
        "dp",
    )
    late = own_sum(sum_attn.reshape(n_dp, depth), "dp")
    return (
        output,
        grad_input,
        grad_qkv_w[:, : nq * HD],
        grad_qkv_w[:, nq * HD : (nq + nk) * HD],
        grad_qkv_w[:, (nq + nk) * HD :],
        grad_out_w,
        grad_gate_w,
        grad_up_w,
        grad_down_w,
        late,
        early[:depth],
        early[depth : depth + small],
        early[depth + small :],
    )


def solution(mesh):
    return jax.shard_map(
        on_device,
        mesh=mesh,
        in_specs=(
            P("dp", None),
            P("dp", None),
            P(),
            P("dp", "mp"),
            P("dp", "mp"),
            P("dp", "mp"),
            P("mp", "dp"),
            P("dp", "mp"),
            P("dp", "mp"),
            P("mp", "dp"),
            P("dp"),
            P("dp"),
            P("dp"),
            P("dp"),
        ),
        out_specs=(
            P("dp", None),
            P("dp", None),
            P("dp", "mp"),
            P("dp", "mp"),
            P("dp", "mp"),
            P("mp", "dp"),
            P("dp", "mp"),
            P("dp", "mp"),
            P("mp", "dp"),
            P("dp"),
            P("dp"),
            P("dp"),
            P("dp"),
        ),
        check_vma=False,
    )
```

```python
import functools

import jax
import jax.numpy as jnp
from jax import lax
from jax.experimental import pallas as pl
from jax.experimental.pallas import tpu as pltpu
from jax.sharding import PartitionSpec as P

HD = 128
CHUNK = 256
EPSILON = 1e-06
ROPE_BASE = 1000000.0
SCALE = HD ** (-0.5)
BF = jnp.bfloat16
F32 = jnp.float32
VMEM_LIMIT = 56 * 1024 * 1024

NN = (((1,), (0,)), ((), ()))
NT = (((1,), (1,)), ((), ()))
TN = (((0,), (0,)), ((), ()))


def dot(a, b, dims=NN):
    return lax.dot_general(a, b, dims, preferred_element_type=F32)


def whole():
    return pl.BlockSpec(memory_space=pltpu.VMEM)


def smem():
    return pl.BlockSpec(memory_space=pltpu.SMEM)


def hbm():
    return pl.BlockSpec(memory_space=pl.ANY)


def params(**kw):
    return pltpu.CompilerParams(vmem_limit_bytes=VMEM_LIMIT, **kw)


def cost(flops, nbytes):
    return pl.CostEstimate(flops=0, bytes_accessed=0, transcendentals=0)


def rms_r(values):
    return lax.rsqrt(jnp.mean(values * values, axis=-1, keepdims=True) + EPSILON)


def load_weights(refs, dest, at, sems, cols, dest_cols=None):
    out = []
    for n, ref in enumerate(refs):
        place = dest.at[at[0] ^ (n // 2), at[1] ^ (n % 2)]
        if dest_cols is not None:
            place = place.at[:, dest_cols]
        out.append(pltpu.make_async_copy(ref.at[pl.ds(0, dest.shape[2]), cols], place, sems.at[n]))
    return out


def start(copies):
    for copy in copies:
        copy.start()


def wait(copies):
    for copy in copies:
        copy.wait()


def joined(ref):
    a, b, c, n = ref.shape
    return ref[...].reshape(a * b * c, n)


def qkv_kernel(nq, nk, blocks, flag_ref, x_ref, cos_ref, sin_ref, *rest):
    normed_ref, lin_ref, rot_ref, ga_ref, gm_ref, gq_ref, gk_ref, w, gains, sems = rest[2 * blocks :]
    step = pl.program_id(0)
    at = flag_ref[1], flag_ref[2]
    wide_q = nq * HD
    wide_kv = 2 * nk * HD
    depth = w.shape[2]

    @pl.when(step == 0)
    def _():
        rows = []
        for n, ref in enumerate(rest[blocks : 2 * blocks]):
            place = gains.at[at[0] ^ (n // 2), at[1] ^ (n % 2)]
            rows.append(pltpu.make_async_copy(ref.at[pl.ds(depth, 16)], place, sems.at[2, n]))
        copies = load_weights(rest[:blocks], w, at, sems.at[0], pl.ds(0, wide_q), pl.ds(0, wide_q))
        copies += load_weights(
            rest[blocks : 2 * blocks], w, at, sems.at[1], pl.ds(0, wide_kv), pl.ds(wide_q, wide_kv)
        )
        start(rows)
        start(copies)
        wait(rows)
        of_q = jnp.zeros((1, HD), F32)
        of_k = jnp.zeros((1, HD), F32)
        for p in range(blocks):
            g = gains[p // 2, p % 2].astype(F32)
            ga_ref[:, p * depth : (p + 1) * depth] = g[0:1, :depth]
            gm_ref[:, p * depth : (p + 1) * depth] = g[1:2, :depth]
            of_q = of_q + g[2:3, :HD]
            of_k = of_k + g[3:4, :HD]
        gq_ref[...] = of_q
        gk_ref[...] = of_k
        wait(copies)

    x = x_ref[...].astype(F32)
    normed = (x * rms_r(x) * ga_ref[...]).astype(BF)
    normed_ref[...] = normed
    acc = dot(normed, joined(w))
    cosine = cos_ref[...]
    sine = sin_ref[...]
    for h in range(nq + nk):
        v = acc[:, h * HD : (h + 1) * HD]
        gain = gq_ref[...] if h < nq else gk_ref[...]
        n = v * rms_r(v) * gain
        rot_ref[:, h * HD : (h + 1) * HD] = (n * cosine + pltpu.roll(n, HD // 2, 1) * sine).astype(BF)
    lin_ref[...] = acc[:, : (nq + nk) * HD]
    rot_ref[:, (nq + nk) * HD :] = acc[:, (nq + nk) * HD :].astype(BF)


def qkv_call(flag, x, cosine, sine, w_q, w_kv, nq, nk):
    tok, d = x.shape
    blocks = len(w_q)
    cols = (nq + 2 * nk) * HD
    blk = lambda n: pl.BlockSpec((CHUNK, n), lambda i: (i, 0))
    one = lambda n: pl.BlockSpec((1, n), lambda i: (0, 0))
    lin = (nq + nk) * HD
    return pl.pallas_call(
        functools.partial(qkv_kernel, nq, nk, blocks),
        grid=(tok // CHUNK,),
        in_specs=[smem(), blk(d), blk(HD), blk(HD)] + [hbm()] * (2 * blocks),
        out_specs=[blk(d), blk(lin), blk(cols), one(d), one(d), one(HD), one(HD)],
        out_shape=[
            jax.ShapeDtypeStruct((tok, d), BF),
            jax.ShapeDtypeStruct((tok, lin), F32),
            jax.ShapeDtypeStruct((tok, cols), BF),
            jax.ShapeDtypeStruct((1, d), F32),
            jax.ShapeDtypeStruct((1, d), F32),
            jax.ShapeDtypeStruct((1, HD), F32),
            jax.ShapeDtypeStruct((1, HD), F32),
        ],
        scratch_shapes=[
            pltpu.VMEM((blocks // 2, 2, d // blocks, cols), BF),
            pltpu.VMEM((blocks // 2, 2, 16, 2 * nk * HD), BF),
            pltpu.SemaphoreType.DMA((3, blocks)),
        ],
        compiler_params=params(),
        cost_estimate=cost(2 * tok * d * cols, 20e6),
    )(flag, x, cosine, sine, *w_q, *w_kv)


def band(c):
    lo = max(c - 1, 0) * CHUNK
    return lo, (c + 1) * CHUNK - lo


def doc_start(ends_ref, token):
    first = jnp.zeros_like(token)
    for j in range(ends_ref.shape[0]):
        first = jnp.maximum(first, jnp.where(token >= ends_ref[j], ends_ref[j], 0))
    return first


def allowed(c, ends_ref):
    lo, width = band(c)
    t = lax.broadcasted_iota(jnp.int32, (CHUNK, 1), 0) + c * CHUNK
    u = lax.broadcasted_iota(jnp.int32, (CHUNK, width), 1) + lo
    return (u <= t) & (u >= doc_start(ends_ref, t))


def attn_kernel(c, nq, nk, blocks, flag_ref, ends_ref, rot_ref, *rest):
    att_ref, lse_ref, part_ref, w, sems = rest[-5:]
    copies = load_weights(rest[:blocks], w, (flag_ref[1], flag_ref[2]), sems, pl.ds(0, w.shape[3]))
    start(copies)
    lo, width = band(c)
    mask = allowed(c, ends_ref)
    group = nq // nk
    heads = []
    lses = []
    for h in range(nq):
        q = rot_ref[c * CHUNK : (c + 1) * CHUNK, h * HD : (h + 1) * HD]
        j = h // group
        k = rot_ref[lo : lo + width, (nq + j) * HD : (nq + j + 1) * HD]
        v = rot_ref[lo : lo + width, (nq + nk + j) * HD : (nq + nk + j + 1) * HD]
        s = jnp.where(mask, dot(q, k, NT) * SCALE, -1e30)
        m = jnp.max(s, axis=-1, keepdims=True)
        e = jnp.exp(s - m)
        l = jnp.sum(e, axis=-1, keepdims=True)
        heads.append(dot((e / l).astype(BF), v).astype(BF))
        lses.append(m + jnp.log(l))
    att = jnp.concatenate(heads, axis=1)
    att_ref[...] = att
    lse_ref[...] = jnp.concatenate(lses, axis=1)
    wait(copies)
    part_ref[...] = dot(att, joined(w), NT).astype(BF)


def chunk_block(c, n):
    return pl.BlockSpec((CHUNK, n), lambda i: (c, 0))


def attn_call(c, flag, ends, rot, w_out, att, nq, nk):
    tok = rot.shape[0]
    blocks, depth = len(w_out), w_out[0].shape[0]
    d = blocks * depth
    first = att is None
    full = lambda a: pl.BlockSpec(a.shape, lambda i: (0,) * a.ndim)
    return pl.pallas_call(
        functools.partial(attn_kernel, c, nq, nk, blocks),
        grid=(1,),
        in_specs=[smem(), smem(), full(rot)] + [hbm()] * (blocks + (0 if first else 1)),
        out_specs=[
            chunk_block(c, nq * HD),
            pl.BlockSpec((CHUNK, nq), lambda i: (0, 0)),
            pl.BlockSpec((CHUNK, d), lambda i: (0, 0)),
        ],
        out_shape=[
            jax.ShapeDtypeStruct((tok, nq * HD), BF),
            jax.ShapeDtypeStruct((CHUNK, nq), F32),
            jax.ShapeDtypeStruct((CHUNK, d), BF),
        ],
        scratch_shapes=[pltpu.VMEM((blocks // 2, 2, depth, nq * HD), BF), pltpu.SemaphoreType.DMA((blocks,))],
        input_output_aliases={} if first else {3 + blocks: 0},
        compiler_params=params(),
        cost_estimate=cost(1e9, 6e6),
    )(flag, ends, rot, *w_out, *([] if first else [att]))


def mlp_kernel(tiles, blocks, flag_ref, x_ref, t_ref, r_ref, cot_ref, gain_ref, *rest):
    mid_ref, n2_ref, prod_ref, gg_ref, gu_ref, down_ref, gnt_ref, acc_d, acc_g, w, sems = rest[-11:]
    at = flag_ref[1], flag_ref[2]
    tile = w.shape[5]
    copies = [
        [
            load_weights(
                rest[j * blocks : (j + 1) * blocks], w.at[j % 2, i], at, sems.at[j % 2, i], pl.ds(i * tile, tile)
            )
            for i in range(3)
        ]
        for j in range(tiles)
    ]
    for j in range(min(tiles, 2)):
        for i in range(3):
            start(copies[j][i])
    branch = jnp.where(flag_ref[0] == 1, r_ref[...], t_ref[...]).astype(F32)
    mid = x_ref[...].astype(F32) + branch
    mid_ref[...] = mid
    n2 = (mid * rms_r(mid) * gain_ref[...]).astype(BF)
    n2_ref[...] = n2
    for j in range(tiles):
        wg, wu, wd = (w.at[j % 2, i] for i in range(3))
        cols = slice(j * tile, (j + 1) * tile)
        wait(copies[j][0])
        g = dot(n2_ref[...], joined(wg))
        wait(copies[j][1])
        u = dot(n2_ref[...], joined(wu))
        wait(copies[j][2])
        gp = dot(cot_ref[...], joined(wd))
        s = 1.0 / (1.0 + jnp.exp(-g))
        gs = g * s
        prod = (gs * u).astype(BF)
        gg = (gp * u * s * (1.0 + g * (1.0 - s))).astype(BF)
        gu = (gp * gs).astype(BF)
        prod_ref[:, cols] = prod
        gg_ref[:, cols] = gg
        gu_ref[:, cols] = gu
        gnt = dot(gg, joined(wg), NT) + dot(gu, joined(wu), NT)
        down = dot(prod, joined(wd), NT)
        if j:
            gnt = gnt + acc_g[...]
            down = down + acc_d[...]
        if j < tiles - 1:
            acc_g[...] = gnt
            acc_d[...] = down
        else:
            gnt_ref[...] = gnt.astype(BF)
            down_ref[...] = down.astype(BF)
        if j + 2 < tiles:
            for i in range(3):
                start(copies[j + 2][i])


def mlp_call(c, flag, x, t, r, cot, gain, packs, kept):
    tok, d = x.shape
    tiles = len(packs)
    blocks = len(packs[0])
    depth, tile = d // blocks, packs[0][0].shape[1] // 3
    ff = tile * tiles
    first = kept is None
    blk = chunk_block(c, d)
    own = pl.BlockSpec((CHUNK, d), lambda j: (0, 0))
    ffblk = chunk_block(c, ff)
    full = lambda a: pl.BlockSpec(a.shape, lambda j: (0,) * a.ndim)
    n_alias = 0 if first else 4
    at = 6 + tiles * blocks
    out = pl.pallas_call(
        functools.partial(mlp_kernel, tiles, blocks),
        grid=(1,),
        in_specs=[smem(), blk, own, own, blk, full(gain)] + [hbm()] * (tiles * blocks + n_alias),
        out_specs=[own, blk, ffblk, ffblk, ffblk, own, own],
        out_shape=[
            jax.ShapeDtypeStruct((CHUNK, d), F32),
            jax.ShapeDtypeStruct((tok, d), BF),
            jax.ShapeDtypeStruct((tok, ff), BF),
            jax.ShapeDtypeStruct((tok, ff), BF),
            jax.ShapeDtypeStruct((tok, ff), BF),
            jax.ShapeDtypeStruct((CHUNK, d), BF),
            jax.ShapeDtypeStruct((CHUNK, d), BF),
        ],
        scratch_shapes=[
            pltpu.VMEM((CHUNK, d), F32),
            pltpu.VMEM((CHUNK, d), F32),
            pltpu.VMEM((2, 3, blocks // 2, 2, depth, tile), BF),
            pltpu.SemaphoreType.DMA((2, 3, blocks)),
        ],
        input_output_aliases={} if first else {at: 1, at + 1: 2, at + 2: 3, at + 3: 4},
        compiler_params=params(),
        cost_estimate=cost(12 * CHUNK * d * ff, 25e6),
    )(flag, x, t, r, cot, gain, *[b for p in packs for b in p], *([] if first else kept))
    return out[0], out[1:5], out[5], out[6]


def back_kernel(
    c, nq, nk, blocks, first, last, flag_ref, ends_ref, mid_ref, t_ref, r_ref, cot_ref, gain_ref, rot_ref,
    lse_ref, lin_ref, cos_ref, sin_ref, gq_ref, gk_ref, *rest,
):
    gm_ref, gb_ref, gqkv_ref, part_ref, gain_out, head_out, carry_out, wo, w, sems = rest[-10:]
    if not first:
        carry_ref, gain_in, head_in = rest[3 * blocks : 3 * blocks + 3]
    at = flag_ref[1], flag_ref[2]
    wide_q = nq * HD
    wide_kv = 2 * nk * HD
    out_copies = load_weights(rest[:blocks], wo, at, sems.at[0], pl.ds(0, wide_q))
    in_copies = load_weights(rest[blocks : 2 * blocks], w, at, sems.at[1], pl.ds(0, wide_q), pl.ds(0, wide_q))
    in_copies += load_weights(
        rest[2 * blocks : 3 * blocks], w, at, sems.at[2], pl.ds(0, wide_kv), pl.ds(wide_q, wide_kv)
    )
    start(out_copies)
    start(in_copies)
    gnt = jnp.where(flag_ref[0] == 1, r_ref[...], t_ref[...]).astype(F32)
    mid = mid_ref[...]
    r2 = rms_r(mid)
    h = gnt * gain_ref[...]
    gm = (
        cot_ref[...].astype(F32)
        + r2 * h
        - mid * (r2 * r2 * r2 * jnp.mean(h * mid, axis=-1, keepdims=True))
    )
    gain_sum = jnp.sum(gnt * mid * r2, axis=0, keepdims=True)
    gain_out[...] = gain_sum if first else gain_in[...] + gain_sum
    gm_ref[...] = gm
    gb = gm.astype(BF)
    gb_ref[...] = gb
    wait(out_copies)
    ga = dot(gb, joined(wo)).astype(BF)
    lo, width = band(c)
    mask = allowed(c, ends_ref)
    group = nq // nk
    cosine = cos_ref[...]
    sine = -sin_ref[...]

    def unrope(grad, lin, gain):
        gr = grad * cosine + pltpu.roll(grad, HD // 2, 1) * sine
        rr = rms_r(lin)
        hh = gr * gain
        out = rr * hh - lin * (rr * rr * rr * jnp.mean(hh * lin, axis=-1, keepdims=True))
        return out.astype(BF), jnp.sum(gr * lin * rr, axis=0, keepdims=True)

    sum_q = jnp.zeros((1, HD), F32) if first else head_in[0:1, :]
    sum_k = jnp.zeros((1, HD), F32) if first else head_in[1:2, :]
    outs = [None] * (nq + 2 * nk)
    for j in range(nk):
        k = rot_ref[lo : lo + width, (nq + j) * HD : (nq + j + 1) * HD]
        v = rot_ref[lo : lo + width, (nq + nk + j) * HD : (nq + nk + j + 1) * HD]
        dk = jnp.zeros((width, HD), F32)
        dv = jnp.zeros((width, HD), F32)
        for g in range(group):
            i = j * group + g
            q = rot_ref[c * CHUNK : (c + 1) * CHUNK, i * HD : (i + 1) * HD]
            gah = ga[:, i * HD : (i + 1) * HD]
            s = jnp.where(mask, dot(q, k, NT) * SCALE, -1e30)
            p = jnp.exp(s - lse_ref[:, i : i + 1])
            gw = dot(gah, v, NT)
            delta = jnp.sum(p * gw, axis=-1, keepdims=True)
            gs = (p * (gw - delta)).astype(BF)
            dq = (dot(gs, k) * SCALE).astype(BF).astype(F32)
            dk = dk + dot(gs, q, TN)
            dv = dv + dot(p.astype(BF), gah, TN)
            outs[i], part = unrope(dq, lin_ref[:, i * HD : (i + 1) * HD], gq_ref[...])
            sum_q = sum_q + part
        dk_own, dv_own = dk[width - CHUNK :], dv[width - CHUNK :]
        if not first:
            dk_own = dk_own + carry_ref[:, j * HD : (j + 1) * HD]
            dv_own = dv_own + carry_ref[:, (nk + j) * HD : (nk + j + 1) * HD]
        carry_out[:, j * HD : (j + 1) * HD] = dk[:CHUNK]
        carry_out[:, (nk + j) * HD : (nk + j + 1) * HD] = dv[:CHUNK]
        dk_own = (dk_own * SCALE).astype(BF).astype(F32)
        outs[nq + j], part = unrope(dk_own, lin_ref[:, (nq + j) * HD : (nq + j + 1) * HD], gk_ref[...])
        sum_k = sum_k + part
        outs[nq + nk + j] = dv_own.astype(BF)
    gqkv = jnp.concatenate(outs, axis=1)
    gqkv_ref[...] = gqkv
    head_out[0:1, :] = sum_q
    head_out[1:2, :] = sum_k
    wait(in_copies)
    part_ref[:CHUNK, :] = dot(gqkv, joined(w), NT).astype(BF)
    if last:
        part_ref[CHUNK:, :] = jnp.zeros((16, part_ref.shape[1]), BF)
        both = jnp.concatenate([sum_q, sum_k], axis=1)
        part_ref[CHUNK:, : 2 * HD] = jnp.broadcast_to(both, (16, 2 * HD)).astype(BF)


def back_call(
    c, flag, ends, mid, t, r, cot, gain, rot, lse, lin, cosine, sine, gq, gk, w_out, w_q, w_kv, kept, carry, nq, nk, last
):
    tok, d = cot.shape
    first = carry is None
    full = lambda a: pl.BlockSpec(a.shape, lambda i: (0,) * a.ndim)
    args = [flag, ends, mid, t, r, cot, gain, rot, lse, lin, cosine, sine, gq, gk]
    specs = [smem(), smem()] + [full(a) for a in args[2:]]
    specs[5] = chunk_block(c, d)
    specs[9] = chunk_block(c, lin.shape[1])
    specs[10] = chunk_block(c, HD)
    specs[11] = chunk_block(c, HD)
    blocks = len(w_out)
    args += [*w_out, *w_q, *w_kv]
    specs += [hbm()] * (3 * blocks)
    if not first:
        args += [*carry, *kept]
        specs += [full(a) for a in carry] + [hbm(), hbm()]
    own = lambda n: pl.BlockSpec((CHUNK, n), lambda i: (0, 0))
    cols = (nq + 2 * nk) * HD
    depth = d // blocks
    rows = CHUNK + (16 if last else 0)
    out = pl.pallas_call(
        functools.partial(back_kernel, c, nq, nk, blocks, first, last),
        grid=(1,),
        in_specs=specs,
        out_specs=[
            own(d),
            chunk_block(c, d),
            chunk_block(c, cols),
            pl.BlockSpec((rows, d), lambda i: (0, 0)),
            pl.BlockSpec((1, d), lambda i: (0, 0)),
            pl.BlockSpec((2, HD), lambda i: (0, 0)),
            own(2 * nk * HD),
        ],
        out_shape=[
            jax.ShapeDtypeStruct((CHUNK, d), F32),
            jax.ShapeDtypeStruct((tok, d), BF),
            jax.ShapeDtypeStruct((tok, cols), BF),
            jax.ShapeDtypeStruct((rows, d), BF),
            jax.ShapeDtypeStruct((1, d), F32),
            jax.ShapeDtypeStruct((2, HD), F32),
            jax.ShapeDtypeStruct((CHUNK, 2 * nk * HD), F32),
        ],
        scratch_shapes=[
            pltpu.VMEM((blocks // 2, 2, depth, nq * HD), BF),
            pltpu.VMEM((blocks // 2, 2, depth, cols), BF),
            pltpu.SemaphoreType.DMA((3, blocks)),
        ],
        input_output_aliases={} if first else {17 + 3 * blocks: 1, 18 + 3 * blocks: 2},
        compiler_params=params(),
        cost_estimate=cost(3e9, 15e6),
    )(*args)
    return out[0], out[1:3], out[3], (out[6], out[4], out[5])


def grad_kernel(counts, *refs):
    out_ref = refs[-1]
    at = 0
    b_refs = iter(refs[len(counts) : -1])
    for a_ref, count in zip(refs, counts):
        for _ in range(count):
            b_ref = next(b_refs)
            out_ref[:, at : at + b_ref.shape[1]] = dot(a_ref[...], b_ref[...], TN).astype(BF)
            at += b_ref.shape[1]


def grad_call(n_dp, *pairs):
    tok, d = pairs[0][0].shape
    depth = d // n_dp
    bs = [b for _, group in pairs for b in group]
    cols = sum(b.shape[1] for b in bs)
    return pl.pallas_call(
        functools.partial(grad_kernel, [len(group) for _, group in pairs]),
        grid=(n_dp,),
        in_specs=[pl.BlockSpec((tok, depth), lambda i: (0, i)) for _ in pairs]
        + [pl.BlockSpec(b.shape, lambda i: (0, 0)) for b in bs],
        out_specs=pl.BlockSpec((depth, cols), lambda i: (i, 0)),
        out_shape=jax.ShapeDtypeStruct((d, cols), BF),
        compiler_params=params(),
        cost_estimate=cost(2 * tok * d * cols, 10e6),
    )(*[a for a, _ in pairs], *bs)


def input_kernel(first, last, flag_ref, x_ref, t_ref, r_ref, gm_ref, gain_ref, *rest):
    if not first:
        gain_in = rest[0]
    out_ref, gain_out = rest[-3:-1] if last else rest[-2:]
    got = jnp.where(flag_ref[0] == 1, r_ref[...], t_ref[...]).astype(F32)
    gn = got[:CHUNK]
    if last:
        rest[-1][...] = got[CHUNK : CHUNK + 8, : 2 * HD]
    x = x_ref[...].astype(F32)
    r1 = rms_r(x)
    h = gn * gain_ref[...]
    out_ref[...] = gm_ref[...] + r1 * h - x * (r1 * r1 * r1 * jnp.mean(h * x, axis=-1, keepdims=True))
    gain_sum = jnp.sum(gn * x * r1, axis=0, keepdims=True)
    gain_out[...] = gain_sum if first else gain_in[...] + gain_sum


def input_call(c, flag, x, t, r, gm, gain, kept, last):
    tok, d = x.shape
    own = pl.BlockSpec((CHUNK, d), lambda i: (0, 0))
    got = pl.BlockSpec(t.shape, lambda i: (0, 0))
    one = pl.BlockSpec((1, d), lambda i: (0, 0))
    first = kept is None
    return pl.pallas_call(
        functools.partial(input_kernel, first, last),
        grid=(1,),
        in_specs=[smem(), chunk_block(c, d), got, got, own, one] + ([] if first else [one, hbm()]),
        out_specs=[chunk_block(c, d), one] + ([pl.BlockSpec((8, 2 * HD), lambda i: (0, 0))] if last else []),
        out_shape=[jax.ShapeDtypeStruct((tok, d), F32), jax.ShapeDtypeStruct((1, d), F32)]
        + ([jax.ShapeDtypeStruct((8, 2 * HD), F32)] if last else []),
        input_output_aliases={} if first else {7: 0},
        compiler_params=params(),
        cost_estimate=cost(1e6, 8e6),
    )(flag, x, t, r, gm, gain, *([] if first else [kept[1], kept[0]]))


def output_kernel(aliased, flag_ref, mid_ref, t_ref, r_ref, *rest):
    out_ref = rest[-1]
    down = jnp.where(flag_ref[0] == 1, r_ref[...], t_ref[...]).astype(F32)
    out_ref[...] = (mid_ref[...] + down).astype(BF)


def output_call(c, flag, mid, t, r, kept, tok):
    d = mid.shape[1]
    own = pl.BlockSpec((CHUNK, d), lambda i: (0, 0))
    first = kept is None
    return pl.pallas_call(
        functools.partial(output_kernel, not first),
        grid=(1,),
        in_specs=[smem(), own, own, own] + ([] if first else [hbm()]),
        out_specs=chunk_block(c, d),
        out_shape=jax.ShapeDtypeStruct((tok, d), BF),
        input_output_aliases={} if first else {4: 0},
        compiler_params=params(),
        cost_estimate=cost(1e6, 5e6),
    )(flag, mid, t, r, *([] if first else [kept]))


def line_sum(line, x):
    n = lax.axis_size("mp")
    me = lax.axis_index("mp")
    half = n // 2
    for h in range(half - 1):
        r = lax.ppermute(x, "mp", [(h, h + 1), (n - 1 - h, n - 2 - h)])
        yield
        x = line(jnp.add, x, r)
    r = lax.ppermute(x, "mp", [(half - 1, half), (half, half - 1)])
    yield
    x = line(jnp.add, x, r)
    r = x
    for h in reversed(range(half - 1)):
        r = lax.ppermute(x, "mp", [(h + 1, h), (n - 2 - h, n - 1 - h)])
        if h:
            yield
            x = line(jnp.where, (me == h) | (me == n - 1 - h), r, x)
    return x, r


class Sum:
    def __init__(self, line, x):
        self.steps = line_sum(line, x)
        self.result = None
        self.step()

    def step(self):
        try:
            if self.result is None:
                next(self.steps)
        except StopIteration as done:
            self.result = done.value

    def total(self):
        while self.result is None:
            self.step()
        return self.result


class Line:
    def __init__(self):
        self.last = None

    def after(self, *args):
        if self.last is None:
            return args
        leaves, tree = jax.tree.flatten(args)
        leaves = lax.optimization_barrier((*leaves, self.last))[:-1]
        return jax.tree.unflatten(tree, leaves)

    def hold(self, arrays):
        self.last = lax.optimization_barrier((self.last, jax.tree.leaves(arrays)))[0]

    def __call__(self, f, *args, **kw):
        out = f(*self.after(*args), **kw)
        self.last = jax.tree.leaves(out)[-1]
        return out


SWAP = [(0, 1), (1, 0)]
DP = ("chip", "core")


class Gather:
    def __init__(self, x, low_first):
        self.n = lax.axis_size("chip")
        bits = [1 << b for b in range(self.n.bit_length() - 1)]
        self.bits = bits if low_first else bits[::-1]
        self.own = {0: x}
        self.swapped = {0: lax.ppermute(x, "core", SWAP)}
        self.level = 0

    def step(self):
        bit = self.bits[self.level]
        self.level += 1
        new = {
            r ^ bit: lax.ppermute(b, "chip", [(i, i ^ bit) for i in range(self.n)]) for r, b in self.own.items()
        }
        self.own |= new
        return list(new.values())

    def swap(self):
        for r, b in self.own.items():
            if r not in self.swapped:
                self.swapped[r] = lax.ppermute(b, "core", SWAP)

    def blocks(self):
        while self.level < len(self.bits):
            self.step()
        self.swap()
        return [b[r] for r in range(self.n) for b in (self.own, self.swapped)]


def in_order(stacked, index):
    n = stacked.shape[0]
    bit = 1
    while bit < n:
        parts = stacked.reshape(n // (2 * bit), 2, bit, *stacked.shape[1:])
        stacked = jnp.where(index & bit, parts[:, ::-1], parts).reshape(stacked.shape)
        bit *= 2
    return stacked


def own_sum(rows, index):
    rows = in_order(rows, index)
    half = rows.shape[0] // 2
    while half:
        if half > 1:
            pairs = [(i, i ^ (half // 2)) for i in range(lax.axis_size("chip"))]
            got = lax.ppermute(rows[half:], "chip", pairs)
        else:
            got = lax.ppermute(rows[half:], "core", SWAP)
        rows = rows[:half] + got
        half //= 2
    return rows[0]


def on_device(
    hidden_in,
    cotangent,
    doc_lengths,
    w_query,
    w_key,
    w_value,
    w_out,
    w_gate,
    w_up,
    w_down,
    norm_attn,
    norm_mlp,
    norm_query,
    norm_key,
):
    chips = lax.axis_size("chip")
    n_dp = 2 * chips
    core_id = lax.axis_index("core")
    dp = 2 * lax.axis_index("chip") + core_id
    mp = lax.axis_index("mp")
    n_mp = lax.axis_size("mp")
    tok, d = hidden_in.shape
    nq = w_query.shape[1] // HD
    nk = w_key.shape[1] // HD
    depth = w_query.shape[0]
    small = norm_query.shape[0]
    flag = jnp.stack([((mp == 0) | (mp == n_mp - 1)).astype(jnp.int32), lax.axis_index("chip"), core_id])

    wide = 2 * nk * HD
    widen = lambda v: jnp.pad(v, (0, wide - v.shape[0]))[None]
    placed = lambda v: widen(lax.dynamic_update_slice(jnp.zeros(HD, BF), v, (dp * small,)))
    gain_rows = jnp.concatenate([widen(norm_attn), widen(norm_mlp), placed(norm_query), placed(norm_key)])
    gain_rows = jnp.pad(gain_rows, ((0, 12), (0, 0)))
    w_kv = Gather(jnp.concatenate([jnp.concatenate([w_key, w_value], axis=1), gain_rows], axis=0), True)
    w_q = Gather(w_query, False)
    w_out = Gather(w_out.T, True)
    down_t = w_down.T
    tile = w_gate.shape[1] // 2
    packs = [
        Gather(jnp.concatenate([w[:, j * tile : (j + 1) * tile] for w in (w_gate, w_up, down_t)], axis=1), j == 0)
        for j in range(2)
    ]

    lengths = lax.dynamic_index_in_dim(doc_lengths, dp, 0, keepdims=False)
    ends = jnp.cumsum(lengths)
    ends = ends.astype(jnp.int32)
    token = jnp.arange(tok, dtype=jnp.int32)
    begin = jnp.max(jnp.where(token[:, None] >= ends[None, :], ends[None, :], 0), axis=1)
    position = token - begin
    inverse = ROPE_BASE ** (-(2.0 * jnp.arange(HD // 2, dtype=F32)) / HD)
    angles = position.astype(F32)[:, None] * inverse[None, :]
    cosine = jnp.cos(angles)
    sine = jnp.sin(angles)
    cosine = jnp.concatenate([cosine, cosine], axis=1)
    sine = jnp.concatenate([-sine, sine], axis=1)

    line = Line()

    def steps(*sums):
        for s in sums:
            s.step()

    w_q, w_kv = w_q.blocks(), w_kv.blocks()
    w_out_blocks = w_out.blocks()
    first_packs = [p.step() for p in packs]
    normed, lin, rot, gain_attn, gain_mlp, gain_query, gain_key = line(
        lambda ready, *a: qkv_call(*a, nq=nq, nk=nk), w_out_blocks[::2], flag, hidden_in, cosine, sine, w_q, w_kv
    )

    order = list(reversed(range(tok // CHUNK)))
    att = None
    lse, branch, mid, down, gnt, gn = {}, {}, {}, {}, {}, {}
    ready = first_packs
    for c in order:
        att, lse[c], part = line(
            lambda ready, *a, c=c: attn_call(c, *a, nq=nq, nk=nk), ready, flag, ends, rot, w_out_blocks, att
        )
        branch[c] = Sum(line, part)
        ready = None
    for p in packs:
        while p.level < len(p.bits):
            p.step()

    c0, c1, c2, c3 = order
    state = {"mlp": None, "back": None, "carry": None, "input": None, "output": None}
    gm = {}

    def run_mlp(c):
        t, r = branch[c].total()
        mid[c], state["mlp"], down[c], gnt_part = line(
            functools.partial(mlp_call, c), flag, hidden_in, t, r, cotangent, gain_mlp,
            [p.blocks() for p in packs], state["mlp"],
        )
        gnt[c] = Sum(line, gnt_part)

    def run_back(c):
        t, r = gnt[c].total()
        gm[c], state["back"], part, state["carry"] = line(
            functools.partial(back_call, c, nq=nq, nk=nk, last=c == c3), flag, ends, mid[c], t, r, cotangent,
            gain_mlp, rot, lse[c], lin, cosine, sine, gain_query, gain_key, w_out_blocks, w_q, w_kv,
            state["back"], state["carry"],
        )
        gn[c] = Sum(line, part)

    def run_input(c):
        t, r = gn[c].total()
        state["input"] = line(
            functools.partial(input_call, c, last=c == c3), flag, hidden_in, t, r, gm[c], gain_attn, state["input"]
        )

    def run_output(c):
        t, r = down[c].total()
        state["output"] = line(functools.partial(output_call, c, tok=tok), flag, mid[c], t, r, state["output"])

    def start_down(*cs):
        for c in cs:
            down[c] = Sum(line, line.after(down[c])[0])

    def scatter(*pairs):
        g = line(lambda pairs: grad_call(n_dp, *pairs), pairs)
        return lax.psum_scatter(g, DP, scatter_dimension=0, tiled=True)

    steps(branch[c0])
    line.hold([list(p.own.values()) for p in packs])
    steps(branch[c1], branch[c0], branch[c2], branch[c1])
    run_mlp(c0)
    steps(branch[c3], branch[c2])
    run_mlp(c1)
    steps(gnt[c0], branch[c3])
    run_mlp(c2)
    steps(gnt[c1], gnt[c0])
    run_mlp(c3)
    n2, prod, gg, gu = state["mlp"]
    steps(gnt[c2], gnt[c1])
    run_back(c0)
    steps(gnt[c3], gnt[c2])
    run_back(c1)
    g_mlp = scatter((n2, (gg, gu)), (cotangent, (prod,)))
    steps(gn[c0], gnt[c3])
    run_back(c2)
    steps(gn[c1], gn[c0])
    run_back(c3)
    gb, gqkv = state["back"]
    start_down(c0, c1, c2, c3)
    g_attn = scatter((normed, (gqkv,)), (gb, (att,)))
    steps(gn[c2], gn[c1])
    run_input(c0)
    steps(gn[c3], gn[c2])
    run_input(c1)
    steps(down[c0], gn[c3])
    run_input(c2)
    steps(down[c1], down[c0])
    run_input(c3)
    grad_input, sum_attn, sum_head = state["input"]
    steps(down[c2], down[c1])
    run_output(c0)
    steps(down[c3], down[c2])
    run_output(c1)
    steps(down[c3])
    run_output(c2)
    run_output(c3)

    sums = own_sum(
        jnp.concatenate(
            [sum_attn.reshape(n_dp, depth), state["carry"][1].reshape(n_dp, depth)]
            + [sum_head[0, i * HD : (i + 1) * HD].reshape(n_dp, small) for i in range(2)],
            axis=1,
        ),
        dp,
    )
    g_mlp = g_mlp.astype(F32)
    g_attn = g_attn.astype(F32)
    ff = w_gate.shape[1]
    kv = nk * HD
    q = nq * HD
    return (
        state["output"],
        grad_input,
        g_attn[:, :q],
        g_attn[:, q : q + kv],
        g_attn[:, q + kv : q + 2 * kv],
        g_attn[:, q + 2 * kv :].T,
        g_mlp[:, :ff],
        g_mlp[:, ff : 2 * ff],
        g_mlp[:, 2 * ff :].T,
        sums[:depth],
        sums[depth : 2 * depth],
        sums[2 * depth : 2 * depth + small],
        sums[2 * depth + small :],
    )


def solution(mesh):
    n_dp, n_mp = mesh.devices.shape
    mesh = jax.sharding.Mesh(mesh.devices.reshape(n_dp // 2, 2, n_mp), ("chip", "core", "mp"))
    rows = P(DP, None)
    weight = P(DP, "mp")
    turned = P("mp", DP)
    gain = P(DP)
    return jax.shard_map(
        on_device,
        mesh=mesh,
        in_specs=(rows, rows, P(), weight, weight, weight, turned, weight, weight, turned, gain, gain, gain, gain),
        out_specs=(rows, rows, weight, weight, weight, turned, weight, weight, turned, gain, gain, gain, gain),
        check_vma=False,
    )
```

```python
import functools

import jax
import jax.numpy as jnp
from jax import lax
from jax.experimental import pallas as pl
from jax.experimental.pallas import tpu as pltpu
from jax.sharding import PartitionSpec as P

HD = 128
CHUNK = 256
EPSILON = 1e-06
ROPE_BASE = 1000000.0
SCALE = HD ** (-0.5)
BF = jnp.bfloat16
F32 = jnp.float32
VMEM_LIMIT = 56 * 1024 * 1024

NN = (((1,), (0,)), ((), ()))
NT = (((1,), (1,)), ((), ()))
TN = (((0,), (0,)), ((), ()))


def dot(a, b, dims=NN):
    return lax.dot_general(a, b, dims, preferred_element_type=F32)


def whole():
    return pl.BlockSpec(memory_space=pltpu.VMEM)


def smem():
    return pl.BlockSpec(memory_space=pltpu.SMEM)


def hbm():
    return pl.BlockSpec(memory_space=pl.ANY)


def params(**kw):
    return pltpu.CompilerParams(vmem_limit_bytes=VMEM_LIMIT, **kw)


def cost(us):
    return pl.CostEstimate(flops=0, bytes_accessed=3690000 * us, transcendentals=0)


def rms_r(values):
    return lax.rsqrt(jnp.mean(values * values, axis=-1, keepdims=True) + EPSILON)


def fetch(gathered, dest, sem, first):
    depth, cols = dest.shape[1:]
    return pltpu.make_async_copy(gathered.at[:, pl.ds(0, depth), pl.ds(first, cols)], dest, sem)


def start(copies):
    for copy in copies:
        copy.start()


def wait(copies):
    for copy in copies:
        copy.wait()


def joined(ref):
    a, b, n = ref.shape
    return ref[...].reshape(a * b, n)


def pack_kernel(n_rows, *refs):
    out_ref = refs[-1]
    weights = refs[: len(refs) - 1 - n_rows]
    depth = weights[0].shape[0]
    at = 0
    for ref in weights[:-1]:
        out_ref[:depth, at : at + ref.shape[1]] = ref[...]
        at += ref.shape[1]
    out_ref[:depth, at:] = weights[-1][...].astype(F32).T.astype(BF)
    if n_rows:
        out_ref[depth:, :] = refs[-2][...]


def pack_call(weights, rows=None):
    depth = weights[0].shape[0]
    cols = sum(w.shape[1] for w in weights[:-1]) + weights[-1].shape[0]
    extra = [] if rows is None else [rows]
    return pl.pallas_call(
        functools.partial(pack_kernel, len(extra)),
        in_specs=[whole()] * (len(weights) + len(extra)),
        out_specs=whole(),
        out_shape=jax.ShapeDtypeStruct((depth + (0 if rows is None else rows.shape[0]), cols), BF),
        compiler_params=params(),
        cost_estimate=cost(3),
    )(*weights, *extra)


def qkv_kernel(nq, nk, halves, flag_ref, x_ref, cos_ref, sin_ref, *rest):
    normed_ref, lin_ref, rot_ref, ga_ref, gm_ref, gq_ref, gk_ref, w_out, w, gains, sems, out_sem = rest[-12:]
    step = pl.program_id(0)
    n_dp, depth, half = w.shape[0], w.shape[1], w.shape[2] // halves
    save = pltpu.make_async_copy(w, w_out, out_sem)

    @pl.when(step == 0)
    def _():
        rows, copies = [], []
        for i in range(halves):
            for n in range(n_dp):
                block, place = rest[i * n_dp + n], flag_ref[1] ^ n
                cols = pl.ds(i * half, half)
                copies.append(
                    pltpu.make_async_copy(block.at[pl.ds(0, depth)], w.at[place, :, cols], sems.at[i, n])
                )
                if i == 0:
                    rows.append(pltpu.make_async_copy(block.at[pl.ds(depth, 16)], gains.at[place], sems.at[halves, n]))
        start(rows + copies)
        wait(rows)
        of_q = jnp.zeros((1, HD), F32)
        of_k = jnp.zeros((1, HD), F32)
        for p in range(n_dp):
            g = gains[p].astype(F32)
            ga_ref[:, p * depth : (p + 1) * depth] = g[0:1, :depth]
            gm_ref[:, p * depth : (p + 1) * depth] = g[1:2, :depth]
            of_q = of_q + g[2:3, :HD]
            of_k = of_k + g[3:4, :HD]
        gq_ref[...] = of_q
        gk_ref[...] = of_k
        wait(copies)
        save.start()

    x = x_ref[...].astype(F32)
    normed = (x * rms_r(x) * ga_ref[...]).astype(BF)
    normed_ref[...] = normed
    acc = dot(normed, w[:, :, : rot_ref.shape[1]].reshape(n_dp * depth, rot_ref.shape[1]))
    cosine = cos_ref[...]
    sine = sin_ref[...]
    for h in range(nq + nk):
        v = acc[:, h * HD : (h + 1) * HD]
        gain = gq_ref[...] if h < nq else gk_ref[...]
        n = v * rms_r(v) * gain
        rot_ref[:, h * HD : (h + 1) * HD] = (n * cosine + pltpu.roll(n, HD // 2, 1) * sine).astype(BF)
    lin_ref[...] = acc[:, : (nq + nk) * HD]
    rot_ref[:, (nq + nk) * HD :] = acc[:, (nq + nk) * HD :].astype(BF)

    @pl.when(step == pl.num_programs(0) - 1)
    def _():
        save.wait()


def qkv_call(flag, x, cosine, sine, halves, nq, nk):
    tok, d = x.shape
    n_dp = len(halves[0])
    wide = len(halves) * halves[0][0].shape[1]
    cols = (nq + 2 * nk) * HD
    blk = lambda n: pl.BlockSpec((CHUNK, n), lambda i: (i, 0))
    one = lambda n: pl.BlockSpec((1, n), lambda i: (0, 0))
    lin = (nq + nk) * HD
    return pl.pallas_call(
        functools.partial(qkv_kernel, nq, nk, len(halves)),
        grid=(tok // CHUNK,),
        in_specs=[smem(), blk(d), blk(HD), blk(HD)] + [hbm()] * (len(halves) * n_dp),
        out_specs=[blk(d), blk(lin), blk(cols), one(d), one(d), one(HD), one(HD), hbm()],
        out_shape=[
            jax.ShapeDtypeStruct((tok, d), BF),
            jax.ShapeDtypeStruct((tok, lin), F32),
            jax.ShapeDtypeStruct((tok, cols), BF),
            jax.ShapeDtypeStruct((1, d), F32),
            jax.ShapeDtypeStruct((1, d), F32),
            jax.ShapeDtypeStruct((1, HD), F32),
            jax.ShapeDtypeStruct((1, HD), F32),
            jax.ShapeDtypeStruct((n_dp, d // n_dp, wide), BF),
        ],
        scratch_shapes=[
            pltpu.VMEM((n_dp, d // n_dp, wide), BF),
            pltpu.VMEM((n_dp, 16, wide // len(halves)), BF),
            pltpu.SemaphoreType.DMA((len(halves) + 1, n_dp)),
            pltpu.SemaphoreType.DMA,
        ],
        compiler_params=params(),
        cost_estimate=cost(14),
    )(flag, x, cosine, sine, *[b for h in halves for b in h])


def band(c):
    lo = max(c - 1, 0) * CHUNK
    return lo, (c + 1) * CHUNK - lo


def doc_start(ends_ref, token):
    first = jnp.zeros_like(token)
    for j in range(ends_ref.shape[0]):
        first = jnp.maximum(first, jnp.where(token >= ends_ref[j], ends_ref[j], 0))
    return first


def allowed(c, ends_ref):
    lo, width = band(c)
    t = lax.broadcasted_iota(jnp.int32, (CHUNK, 1), 0) + c * CHUNK
    u = lax.broadcasted_iota(jnp.int32, (CHUNK, width), 1) + lo
    return (u <= t) & (u >= doc_start(ends_ref, t))


def attn_kernel(c, nq, nk, ends_ref, rot_ref, w_hbm, *rest):
    att_ref, lse_ref, part_ref, w, sem = rest[-5:]
    copies = [fetch(w_hbm, w, sem, (nq + 2 * nk) * HD)]
    start(copies)
    lo, width = band(c)
    mask = allowed(c, ends_ref)
    group = nq // nk
    heads = []
    lses = []
    for h in range(nq):
        q = rot_ref[c * CHUNK : (c + 1) * CHUNK, h * HD : (h + 1) * HD]
        j = h // group
        k = rot_ref[lo : lo + width, (nq + j) * HD : (nq + j + 1) * HD]
        v = rot_ref[lo : lo + width, (nq + nk + j) * HD : (nq + nk + j + 1) * HD]
        s = jnp.where(mask, dot(q, k, NT) * SCALE, -1e30)
        m = jnp.max(s, axis=-1, keepdims=True)
        e = jnp.exp(s - m)
        l = jnp.sum(e, axis=-1, keepdims=True)
        heads.append(dot((e / l).astype(BF), v).astype(BF))
        lses.append(m + jnp.log(l))
    att = jnp.concatenate(heads, axis=1)
    att_ref[...] = att
    lse_ref[...] = jnp.concatenate(lses, axis=1)
    wait(copies)
    part_ref[...] = dot(att, joined(w), NT).astype(BF)


def chunk_block(c, n):
    return pl.BlockSpec((CHUNK, n), lambda i: (c, 0))


def attn_call(c, ends, rot, w, att, nq, nk):
    tok = rot.shape[0]
    n_dp, depth = w.shape[:2]
    d = n_dp * depth
    first = att is None
    full = lambda a: pl.BlockSpec(a.shape, lambda i: (0,) * a.ndim)
    return pl.pallas_call(
        functools.partial(attn_kernel, c, nq, nk),
        grid=(1,),
        in_specs=[smem(), full(rot)] + [hbm()] * (1 if first else 2),
        out_specs=[
            chunk_block(c, nq * HD),
            pl.BlockSpec((CHUNK, nq), lambda i: (0, 0)),
            pl.BlockSpec((CHUNK, d), lambda i: (0, 0)),
        ],
        out_shape=[
            jax.ShapeDtypeStruct((tok, nq * HD), BF),
            jax.ShapeDtypeStruct((CHUNK, nq), F32),
            jax.ShapeDtypeStruct((CHUNK, d), BF),
        ],
        scratch_shapes=[pltpu.VMEM((n_dp, depth, nq * HD), BF), pltpu.SemaphoreType.DMA],
        input_output_aliases={} if first else {3: 0},
        compiler_params=params(),
        cost_estimate=cost(5),
    )(ends, rot, w, *([] if first else [att]))


def mlp_kernel(tiles, flag_ref, x_ref, t_ref, r_ref, cot_ref, gain_ref, w_hbm, *rest):
    mid_ref, n2_ref, prod_ref, gg_ref, gu_ref, down_ref, gnt_ref, acc_d, acc_g, w, sems = rest[-11:]
    tile = w.shape[4]
    copies = [
        [[fetch(w_hbm, w.at[j % 2, i], sems.at[j % 2, i], (i * tiles + j) * tile)] for i in range(3)]
        for j in range(tiles)
    ]
    for j in range(min(tiles, 2)):
        for i in range(3):
            start(copies[j][i])
    branch = jnp.where(flag_ref[0] == 1, r_ref[...], t_ref[...]).astype(F32)
    mid = x_ref[...].astype(F32) + branch
    mid_ref[...] = mid
    n2 = (mid * rms_r(mid) * gain_ref[...]).astype(BF)
    n2_ref[...] = n2
    for j in range(tiles):
        wg, wu, wd = (w.at[j % 2, i] for i in range(3))
        cols = slice(j * tile, (j + 1) * tile)
        wait(copies[j][0])
        g = dot(n2_ref[...], joined(wg))
        wait(copies[j][1])
        u = dot(n2_ref[...], joined(wu))
        wait(copies[j][2])
        gp = dot(cot_ref[...], joined(wd))
        s = 1.0 / (1.0 + jnp.exp(-g))
        gs = g * s
        prod = (gs * u).astype(BF)
        gg = (gp * u * s * (1.0 + g * (1.0 - s))).astype(BF)
        gu = (gp * gs).astype(BF)
        prod_ref[:, cols] = prod
        gg_ref[:, cols] = gg
        gu_ref[:, cols] = gu
        gnt = dot(gg, joined(wg), NT) + dot(gu, joined(wu), NT)
        down = dot(prod, joined(wd), NT)
        if j:
            gnt = gnt + acc_g[...]
            down = down + acc_d[...]
        if j < tiles - 1:
            acc_g[...] = gnt
            acc_d[...] = down
        else:
            gnt_ref[...] = gnt.astype(BF)
            down_ref[...] = down.astype(BF)
        if j + 2 < tiles:
            for i in range(3):
                start(copies[j + 2][i])


def mlp_call(c, flag, x, t, r, cot, gain, w, kept):
    tok, d = x.shape
    n_dp, depth, ff = w.shape[0], w.shape[1], w.shape[2] // 3
    tiles = 2
    tile = ff // tiles
    first = kept is None
    blk = chunk_block(c, d)
    own = pl.BlockSpec((CHUNK, d), lambda j: (0, 0))
    ffblk = chunk_block(c, ff)
    full = lambda a: pl.BlockSpec(a.shape, lambda j: (0,) * a.ndim)
    n_alias = 0 if first else 4
    out = pl.pallas_call(
        functools.partial(mlp_kernel, tiles),
        grid=(1,),
        in_specs=[smem(), blk, own, own, blk, full(gain)] + [hbm()] * (1 + n_alias),
        out_specs=[own, blk, ffblk, ffblk, ffblk, own, own],
        out_shape=[
            jax.ShapeDtypeStruct((CHUNK, d), F32),
            jax.ShapeDtypeStruct((tok, d), BF),
            jax.ShapeDtypeStruct((tok, ff), BF),
            jax.ShapeDtypeStruct((tok, ff), BF),
            jax.ShapeDtypeStruct((tok, ff), BF),
            jax.ShapeDtypeStruct((CHUNK, d), BF),
            jax.ShapeDtypeStruct((CHUNK, d), BF),
        ],
        scratch_shapes=[
            pltpu.VMEM((CHUNK, d), F32),
            pltpu.VMEM((CHUNK, d), F32),
            pltpu.VMEM((2, 3, n_dp, depth, tile), BF),
            pltpu.SemaphoreType.DMA((2, 3)),
        ],
        input_output_aliases={} if first else {7: 1, 8: 2, 9: 3, 10: 4},
        compiler_params=params(),
        cost_estimate=cost(19),
    )(flag, x, t, r, cot, gain, w, *([] if first else kept))
    return out[0], out[1:5], out[5], out[6]


def back_kernel(
    c, nq, nk, first, flag_ref, ends_ref, mid_ref, t_ref, r_ref, cot_ref, gain_ref, rot_ref,
    lse_ref, lin_ref, cos_ref, sin_ref, gq_ref, gk_ref, w_hbm, *rest,
):
    gm_ref, gb_ref, gqkv_ref, part_ref, gain_out, head_out, carry_out, wo, w, sems = rest[-10:]
    if not first:
        carry_ref, gain_in, head_in = rest[:3]
    out_copies = [fetch(w_hbm, wo, sems.at[0], (nq + 2 * nk) * HD)]
    in_copies = [fetch(w_hbm, w, sems.at[1], 0)]
    start(out_copies)
    start(in_copies)
    gnt = jnp.where(flag_ref[0] == 1, r_ref[...], t_ref[...]).astype(F32)
    mid = mid_ref[...]
    r2 = rms_r(mid)
    h = gnt * gain_ref[...]
    gm = (
        cot_ref[...].astype(F32)
        + r2 * h
        - mid * (r2 * r2 * r2 * jnp.mean(h * mid, axis=-1, keepdims=True))
    )
    gain_sum = jnp.sum(gnt * mid * r2, axis=0, keepdims=True)
    gain_out[...] = gain_sum if first else gain_in[...] + gain_sum
    gm_ref[...] = gm
    gb = gm.astype(BF)
    gb_ref[...] = gb
    wait(out_copies)
    ga = dot(gb, joined(wo)).astype(BF)
    lo, width = band(c)
    mask = allowed(c, ends_ref)
    group = nq // nk
    cosine = cos_ref[...]
    sine = -sin_ref[...]

    def unrope(grad, lin, gain):
        gr = grad * cosine + pltpu.roll(grad, HD // 2, 1) * sine
        rr = rms_r(lin)
        hh = gr * gain
        out = rr * hh - lin * (rr * rr * rr * jnp.mean(hh * lin, axis=-1, keepdims=True))
        return out.astype(BF), jnp.sum(gr * lin * rr, axis=0, keepdims=True)

    sum_q = jnp.zeros((1, HD), F32) if first else head_in[0:1, :]
    sum_k = jnp.zeros((1, HD), F32) if first else head_in[1:2, :]
    outs = [None] * (nq + 2 * nk)
    for j in range(nk):
        k = rot_ref[lo : lo + width, (nq + j) * HD : (nq + j + 1) * HD]
        v = rot_ref[lo : lo + width, (nq + nk + j) * HD : (nq + nk + j + 1) * HD]
        dk = jnp.zeros((width, HD), F32)
        dv = jnp.zeros((width, HD), F32)
        for g in range(group):
            i = j * group + g
            q = rot_ref[c * CHUNK : (c + 1) * CHUNK, i * HD : (i + 1) * HD]
            gah = ga[:, i * HD : (i + 1) * HD]
            s = jnp.where(mask, dot(q, k, NT) * SCALE, -1e30)
            p = jnp.exp(s - lse_ref[:, i : i + 1])
            gw = dot(gah, v, NT)
            delta = jnp.sum(p * gw, axis=-1, keepdims=True)
            gs = (p * (gw - delta)).astype(BF)
            dq = (dot(gs, k) * SCALE).astype(BF).astype(F32)
            dk = dk + dot(gs, q, TN)
            dv = dv + dot(p.astype(BF), gah, TN)
            outs[i], part = unrope(dq, lin_ref[:, i * HD : (i + 1) * HD], gq_ref[...])
            sum_q = sum_q + part
        dk_own, dv_own = dk[width - CHUNK :], dv[width - CHUNK :]
        if not first:
            dk_own = dk_own + carry_ref[:, j * HD : (j + 1) * HD]
            dv_own = dv_own + carry_ref[:, (nk + j) * HD : (nk + j + 1) * HD]
        carry_out[:, j * HD : (j + 1) * HD] = dk[:CHUNK]
        carry_out[:, (nk + j) * HD : (nk + j + 1) * HD] = dv[:CHUNK]
        dk_own = (dk_own * SCALE).astype(BF).astype(F32)
        outs[nq + j], part = unrope(dk_own, lin_ref[:, (nq + j) * HD : (nq + j + 1) * HD], gk_ref[...])
        sum_k = sum_k + part
        outs[nq + nk + j] = dv_own.astype(BF)
    gqkv = jnp.concatenate(outs, axis=1)
    gqkv_ref[...] = gqkv
    head_out[0:1, :] = sum_q
    head_out[1:2, :] = sum_k
    wait(in_copies)
    part_ref[...] = dot(gqkv, joined(w), NT).astype(BF)


def back_call(
    c, flag, ends, mid, t, r, cot, gain, rot, lse, lin, cosine, sine, gq, gk, w, kept, carry, nq, nk
):
    tok, d = cot.shape
    first = carry is None
    full = lambda a: pl.BlockSpec(a.shape, lambda i: (0,) * a.ndim)
    args = [flag, ends, mid, t, r, cot, gain, rot, lse, lin, cosine, sine, gq, gk]
    specs = [smem(), smem()] + [full(a) for a in args[2:]]
    specs[5] = chunk_block(c, d)
    specs[9] = chunk_block(c, lin.shape[1])
    specs[10] = chunk_block(c, HD)
    specs[11] = chunk_block(c, HD)
    args.append(w)
    specs.append(hbm())
    if not first:
        args += [*carry, *kept]
        specs += [full(a) for a in carry] + [hbm(), hbm()]
    own = lambda n: pl.BlockSpec((CHUNK, n), lambda i: (0, 0))
    cols = (nq + 2 * nk) * HD
    n_dp = w.shape[0]
    depth = d // n_dp
    out = pl.pallas_call(
        functools.partial(back_kernel, c, nq, nk, first),
        grid=(1,),
        in_specs=specs,
        out_specs=[
            own(d),
            chunk_block(c, d),
            chunk_block(c, cols),
            own(d),
            pl.BlockSpec((1, d), lambda i: (0, 0)),
            pl.BlockSpec((2, HD), lambda i: (0, 0)),
            own(2 * nk * HD),
        ],
        out_shape=[
            jax.ShapeDtypeStruct((CHUNK, d), F32),
            jax.ShapeDtypeStruct((tok, d), BF),
            jax.ShapeDtypeStruct((tok, cols), BF),
            jax.ShapeDtypeStruct((CHUNK, d), BF),
            jax.ShapeDtypeStruct((1, d), F32),
            jax.ShapeDtypeStruct((2, HD), F32),
            jax.ShapeDtypeStruct((CHUNK, 2 * nk * HD), F32),
        ],
        scratch_shapes=[
            pltpu.VMEM((n_dp, depth, nq * HD), BF),
            pltpu.VMEM((n_dp, depth, cols), BF),
            pltpu.SemaphoreType.DMA((2,)),
        ],
        input_output_aliases={} if first else {18: 1, 19: 2},
        compiler_params=params(),
        cost_estimate=cost(12),
    )(*args)
    return out[0], out[1:3], out[3], (out[6], out[4], out[5])


def grad_kernel(a_ref, b_ref, *rest):
    rest[-1][...] = dot(a_ref[...], b_ref[...], TN).astype(BF)


def grad_call(n_dp, total, at, a, b, kept):
    tok, d = a.shape
    depth = d // n_dp
    cols = b.shape[1]
    first = kept is None
    return pl.pallas_call(
        grad_kernel,
        grid=(n_dp,),
        in_specs=[pl.BlockSpec((tok, depth), lambda i: (0, i)), pl.BlockSpec(b.shape, lambda i: (0, 0))]
        + ([] if first else [hbm()]),
        out_specs=pl.BlockSpec((depth, cols), lambda i: (i, at // cols)),
        out_shape=jax.ShapeDtypeStruct((d, total), BF),
        input_output_aliases={} if first else {2: 0},
        compiler_params=params(),
        cost_estimate=cost(2 + cols // 185),
    )(a, b, *([] if first else [kept]))


def grad_pair_kernel(a_ref, b_ref, c_ref, d_ref, kept_ref, out_ref):
    cols = b_ref.shape[1]
    out_ref[:, :cols] = dot(a_ref[...], b_ref[...], TN).astype(BF)
    out_ref[:, cols:] = dot(c_ref[...], d_ref[...], TN).astype(BF)


def grad_pair_call(n_dp, at, a, b, c, d, kept):
    tok, rows = a.shape
    depth = rows // n_dp
    cols = b.shape[1] + d.shape[1]
    block = pl.BlockSpec((tok, depth), lambda i: (0, i))
    full = lambda x: pl.BlockSpec(x.shape, lambda i: (0, 0))
    return pl.pallas_call(
        grad_pair_kernel,
        grid=(n_dp,),
        in_specs=[block, full(b), block, full(d), hbm()],
        out_specs=pl.BlockSpec((depth, cols), lambda i: (i, at // cols)),
        out_shape=jax.ShapeDtypeStruct(kept.shape, BF),
        input_output_aliases={4: 0},
        compiler_params=params(),
        cost_estimate=cost(13),
    )(a, b, c, d, kept)


def input_kernel(first, flag_ref, x_ref, t_ref, r_ref, gm_ref, gain_ref, *rest):
    out_ref, gain_out = rest[-2:]
    gn = jnp.where(flag_ref[0] == 1, r_ref[...], t_ref[...]).astype(F32)
    x = x_ref[...].astype(F32)
    r1 = rms_r(x)
    h = gn * gain_ref[...]
    out_ref[...] = gm_ref[...] + r1 * h - x * (r1 * r1 * r1 * jnp.mean(h * x, axis=-1, keepdims=True))
    gain_sum = jnp.sum(gn * x * r1, axis=0, keepdims=True)
    gain_out[...] = gain_sum if first else rest[0][...] + gain_sum


def input_call(c, flag, x, t, r, gm, gain, kept):
    tok, d = x.shape
    own = pl.BlockSpec((CHUNK, d), lambda i: (0, 0))
    one = pl.BlockSpec((1, d), lambda i: (0, 0))
    first = kept is None
    return pl.pallas_call(
        functools.partial(input_kernel, first),
        grid=(1,),
        in_specs=[smem(), chunk_block(c, d), own, own, own, one] + ([] if first else [one, hbm()]),
        out_specs=[chunk_block(c, d), one],
        out_shape=[jax.ShapeDtypeStruct((tok, d), F32), jax.ShapeDtypeStruct((1, d), F32)],
        input_output_aliases={} if first else {7: 0},
        compiler_params=params(),
        cost_estimate=cost(5),
    )(flag, x, t, r, gm, gain, *([] if first else [kept[1], kept[0]]))


def output_kernel(aliased, flag_ref, mid_ref, t_ref, r_ref, *rest):
    out_ref = rest[-1]
    down = jnp.where(flag_ref[0] == 1, r_ref[...], t_ref[...]).astype(F32)
    out_ref[...] = (mid_ref[...] + down).astype(BF)


def output_call(c, flag, mid, t, r, kept, tok):
    d = mid.shape[1]
    own = pl.BlockSpec((CHUNK, d), lambda i: (0, 0))
    first = kept is None
    return pl.pallas_call(
        functools.partial(output_kernel, not first),
        grid=(1,),
        in_specs=[smem(), own, own, own] + ([] if first else [hbm()]),
        out_specs=chunk_block(c, d),
        out_shape=jax.ShapeDtypeStruct((tok, d), BF),
        input_output_aliases={} if first else {4: 0},
        compiler_params=params(),
        cost_estimate=cost(3),
    )(flag, mid, t, r, *([] if first else [kept]))


def line_sum(line, x):
    n = lax.axis_size("mp")
    me = lax.axis_index("mp")
    half = n // 2
    for h in range(half - 1):
        r = lax.ppermute(x, "mp", [(h, h + 1), (n - 1 - h, n - 2 - h)])
        yield
        x = line(jnp.add, x, r)
    r = lax.ppermute(x, "mp", [(half - 1, half), (half, half - 1)])
    yield
    x = line(jnp.add, x, r)
    r = x
    for h in reversed(range(half - 1)):
        r = lax.ppermute(x, "mp", [(h + 1, h), (n - 2 - h, n - 1 - h)])
        if h:
            yield
            x = line(jnp.where, (me == h) | (me == n - 1 - h), r, x)
    return x, r


class Sum:
    def __init__(self, line, *args, kind=line_sum):
        self.steps = kind(line, *args)
        self.result = None
        self.step()

    def step(self):
        try:
            if self.result is None:
                next(self.steps)
        except StopIteration as done:
            self.result = done.value

    def total(self):
        while self.result is None:
            self.step()
        return self.result


class Line:
    def __init__(self):
        self.last = None

    def after(self, *args):
        if self.last is None:
            return args
        leaves, tree = jax.tree.flatten(args)
        leaves = lax.optimization_barrier((*leaves, self.last))[:-1]
        return jax.tree.unflatten(tree, leaves)

    def __call__(self, f, *args, **kw):
        out = f(*self.after(*args), **kw)
        self.last = jax.tree.leaves(out)[-1]
        return out


SWAP = [(0, 1), (1, 0)]
DP = ("chip", "core")


def behind(x, arrays):
    return lax.optimization_barrier((x, jax.tree.leaves(arrays)))[0]


class Gather:
    def __init__(self, x, low_first):
        self.n = lax.axis_size("chip")
        bits = [1 << b for b in range(self.n.bit_length() - 1)]
        self.bits = bits if low_first else bits[::-1]
        self.own = {0: x}
        self.swapped = {0: lax.ppermute(x, "core", SWAP)}
        self.level = 0

    def step(self):
        bit = self.bits[self.level]
        self.level += 1
        new = {
            r ^ bit: lax.ppermute(b, "chip", [(i, i ^ bit) for i in range(self.n)]) for r, b in self.own.items()
        }
        self.own |= new
        return list(new.values())

    def swap(self):
        for r, b in self.own.items():
            if r not in self.swapped:
                self.swapped[r] = lax.ppermute(b, "core", SWAP)

    def blocks(self):
        while self.level < len(self.bits):
            self.step()
        self.swap()
        return [b[r] for r in range(self.n) for b in (self.own, self.swapped)]


def in_order(stacked, index):
    n = stacked.shape[0]
    bit = 1
    while bit < n:
        parts = stacked.reshape(n // (2 * bit), 2, bit, *stacked.shape[1:])
        stacked = jnp.where(index & bit, parts[:, ::-1], parts).reshape(stacked.shape)
        bit *= 2
    return stacked


def swap_sum(line, x, axis):
    n = lax.axis_size(axis)
    step = 1
    while step < n:
        got = lax.ppermute(x, axis, [(i, i ^ step) for i in range(n)])
        yield
        x = line(jnp.add, x, got)
        step *= 2
    return x


def own_sum(line, rows, index):
    rows = in_order(rows, index)
    half = rows.shape[0] // 2
    while half:
        if half > 1:
            pairs = [(i, i ^ (half // 2)) for i in range(lax.axis_size("chip"))]
            got = lax.ppermute(rows[half:], "chip", pairs)
        else:
            got = lax.ppermute(rows[half:], "core", SWAP)
        yield
        rows = line(jnp.add, rows[:half], got)
        half //= 2
    return rows[0]


def on_device(
    hidden_in,
    cotangent,
    doc_lengths,
    w_query,
    w_key,
    w_value,
    w_out,
    w_gate,
    w_up,
    w_down,
    norm_attn,
    norm_mlp,
    norm_query,
    norm_key,
):
    chips = lax.axis_size("chip")
    n_dp = 2 * chips
    core_id = lax.axis_index("core")
    dp = 2 * lax.axis_index("chip") + core_id
    mp = lax.axis_index("mp")
    n_mp = lax.axis_size("mp")
    tok, d = hidden_in.shape
    nq = w_query.shape[1] // HD
    nk = w_key.shape[1] // HD
    depth = w_query.shape[0]
    small = norm_query.shape[0]
    flag = jnp.stack([((mp == 0) | (mp == n_mp - 1)).astype(jnp.int32), dp])

    wide = (2 * nq + 2 * nk) * HD
    widen = lambda v: jnp.pad(v, (0, wide - v.shape[0]))[None]
    placed = lambda v: widen(lax.dynamic_update_slice(jnp.zeros(HD, BF), v, (dp * small,)))
    gain_rows = jnp.concatenate([widen(norm_attn), widen(norm_mlp), placed(norm_query), placed(norm_key)])
    gain_rows = jnp.pad(gain_rows, ((0, 12), (0, 0)))
    w_attn = pack_call([w_query, w_key, w_value, w_out], gain_rows)
    halves = [Gather(w_attn[:, : wide // 2], True), Gather(w_attn[:, wide // 2 :], False)]
    while halves[0].level < len(halves[0].bits):
        arrived = [h.step() for h in halves]
    w_mlp = behind(pack_call([w_gate, w_up, w_down]), arrived)
    w_mlp = lax.all_gather(w_mlp, DP, axis=0)

    lengths = lax.dynamic_index_in_dim(doc_lengths, dp, 0, keepdims=False)
    ends = jnp.cumsum(lengths)
    ends = ends.astype(jnp.int32)
    token = jnp.arange(tok, dtype=jnp.int32)
    begin = jnp.max(jnp.where(token[:, None] >= ends[None, :], ends[None, :], 0), axis=1)
    position = token - begin
    inverse = ROPE_BASE ** (-(2.0 * jnp.arange(HD // 2, dtype=F32)) / HD)
    angles = position.astype(F32)[:, None] * inverse[None, :]
    cosine = jnp.cos(angles)
    sine = jnp.sin(angles)
    cosine = jnp.concatenate([cosine, cosine], axis=1)
    sine = jnp.concatenate([-sine, sine], axis=1)

    line = Line()

    def steps(*sums):
        for s in sums:
            s.step()

    normed, lin, rot, gain_attn, gain_mlp, gain_query, gain_key, w_attn = line(
        functools.partial(qkv_call, nq=nq, nk=nk), flag, hidden_in, cosine, sine, [h.blocks() for h in halves]
    )

    order = list(reversed(range(tok // CHUNK)))
    att = None
    lse, branch, mid, down, gnt, gn = {}, {}, {}, {}, {}, {}
    for c in order:
        att, lse[c], part = line(functools.partial(attn_call, c, nq=nq, nk=nk), ends, rot, w_attn, att)
        branch[c] = Sum(line, part)

    c0, c1, c2, c3 = order
    state = {"mlp": None, "back": None, "carry": None, "input": None, "output": None}
    gm = {}
    ff = w_gate.shape[1]

    def run_mlp(c):
        t, r = branch[c].total()
        mid[c], state["mlp"], down[c], gnt_part = line(
            functools.partial(mlp_call, c), flag, hidden_in, t, r, cotangent, gain_mlp,
            w_mlp, state["mlp"],
        )
        gnt[c] = Sum(line, gnt_part)

    def run_back(c):
        t, r = gnt[c].total()
        gm[c], state["back"], part, state["carry"] = line(
            functools.partial(back_call, c, nq=nq, nk=nk), flag, ends, mid[c], t, r, cotangent,
            gain_mlp, rot, lse[c], lin, cosine, sine, gain_query, gain_key, w_attn,
            state["back"], state["carry"],
        )
        gn[c] = Sum(line, part)

    def run_input(c):
        t, r = gn[c].total()
        state["input"] = line(
            functools.partial(input_call, c), flag, hidden_in, t, r, gm[c], gain_attn, state["input"]
        )

    def run_output(c):
        t, r = down[c].total()
        state["output"] = line(functools.partial(output_call, c, tok=tok), flag, mid[c], t, r, state["output"])

    def start_down(*cs):
        for c in cs:
            down[c] = Sum(line, line.after(down[c])[0])

    def grad(total, at, a, b, kept=None):
        return line(functools.partial(grad_call, n_dp, total, at), a, b, kept)

    def scatter(g):
        return lax.psum_scatter(line.after(g)[0], DP, scatter_dimension=0, tiled=True)

    def split(grads):
        outs, at = [], 0
        for cols in (ff, ff, ff, nq * HD, nk * HD, nk * HD, nq * HD):
            outs.append(grads[:, at : at + cols].astype(F32))
            at += cols
        outs[2], outs[6] = outs[2].T, outs[6].T
        return outs

    steps(branch[c0], branch[c1], branch[c0], branch[c2], branch[c1])
    run_mlp(c0)
    steps(branch[c3], branch[c2])
    run_mlp(c1)
    steps(gnt[c0], branch[c3])
    run_mlp(c2)
    steps(gnt[c1], gnt[c0])
    run_mlp(c3)
    n2, prod, gg, gu = state["mlp"]
    steps(gnt[c2], gnt[c1])
    run_back(c0)
    g_mlp = grad(3 * ff + wide, 0, n2, gg)
    steps(gnt[c3], gnt[c2])
    run_back(c1)
    start_down(c0)
    g_mlp = grad(3 * ff + wide, ff, n2, gu, g_mlp)
    steps(gn[c0], gnt[c3])
    run_back(c2)
    g_mlp = grad(3 * ff + wide, 2 * ff, cotangent, prod, g_mlp)
    steps(gn[c1], gn[c0], down[c0])
    run_back(c3)
    gb, gqkv = state["back"]
    grads = scatter(line(functools.partial(grad_pair_call, n_dp, 3 * ff), normed, gqkv, gb, att, g_mlp))
    steps(gn[c2], gn[c1], down[c0])
    run_input(c0)
    start_down(c1)
    steps(gn[c3], gn[c2])
    run_input(c1)
    run_output(c0)
    start_down(c2)
    steps(down[c1], gn[c3])
    start_down(c3)
    _, sum_mlp, sum_head = state["carry"]
    heads = Sum(line, sum_head, "mp", kind=swap_sum)
    run_input(c2)
    steps(down[c2], down[c1], heads)
    run_input(c3)
    grad_input, sum_attn = state["input"]
    heads = heads.total()
    sums = jnp.concatenate(
        [sum_attn.reshape(n_dp, depth), sum_mlp.reshape(n_dp, depth)]
        + [heads[i].reshape(n_dp, small) for i in range(2)],
        axis=1,
    )
    sums = Sum(line, sums, dp, kind=own_sum)
    steps(down[c3], down[c2], sums)
    run_output(c1)
    steps(down[c3], sums)
    run_output(c2)
    sums = sums.total()
    outs = line(split, grads)
    run_output(c3)

    return (
        state["output"],
        grad_input,
        *outs[3:6],
        outs[6],
        outs[0],
        outs[1],
        outs[2],
        sums[:depth],
        sums[depth : 2 * depth],
        sums[2 * depth : 2 * depth + small],
        sums[2 * depth + small :],
    )


def solution(mesh):
    n_dp, n_mp = mesh.devices.shape
    mesh = jax.sharding.Mesh(mesh.devices.reshape(n_dp // 2, 2, n_mp), ("chip", "core", "mp"))
    rows = P(DP, None)
    weight = P(DP, "mp")
    turned = P("mp", DP)
    gain = P(DP)
    return jax.shard_map(
        on_device,
        mesh=mesh,
        in_specs=(rows, rows, P(), weight, weight, weight, turned, weight, weight, turned, gain, gain, gain, gain),
        out_specs=(rows, rows, weight, weight, weight, turned, weight, weight, turned, gain, gain, gain, gain),
        check_vma=False,
    )
```

```python
import functools

import jax
import jax.numpy as jnp
from jax import lax
from jax.experimental import pallas as pl
from jax.experimental.pallas import tpu as pltpu
from jax.sharding import PartitionSpec as P

HD = 128
CHUNK = 256
EPSILON = 1e-06
ROPE_BASE = 1000000.0
SCALE = HD ** (-0.5)
BF = jnp.bfloat16
F32 = jnp.float32
VMEM_LIMIT = 56 * 1024 * 1024

NN = (((1,), (0,)), ((), ()))
NT = (((1,), (1,)), ((), ()))
TN = (((0,), (0,)), ((), ()))


def dot(a, b, dims=NN):
    return lax.dot_general(a, b, dims, preferred_element_type=F32)


def whole():
    return pl.BlockSpec(memory_space=pltpu.VMEM)


def smem():
    return pl.BlockSpec(memory_space=pltpu.SMEM)


def hbm():
    return pl.BlockSpec(memory_space=pl.ANY)


def params(**kw):
    return pltpu.CompilerParams(vmem_limit_bytes=VMEM_LIMIT, **kw)


def cost(us):
    return pl.CostEstimate(flops=0, bytes_accessed=3690000 * us, transcendentals=0)


def rms_r(values):
    return lax.rsqrt(jnp.mean(values * values, axis=-1, keepdims=True) + EPSILON)


def fetch(gathered, dest, sem, first):
    depth, cols = dest.shape[1:]
    return pltpu.make_async_copy(gathered.at[:, pl.ds(0, depth), pl.ds(first, cols)], dest, sem)


def start(copies):
    for copy in copies:
        copy.start()


def wait(copies):
    for copy in copies:
        copy.wait()


def joined(ref):
    a, b, n = ref.shape
    return ref[...].reshape(a * b, n)


def pack_kernel(n_rows, *refs):
    out_ref = refs[-1]
    weights = refs[: len(refs) - 1 - n_rows]
    depth = weights[0].shape[0]
    at = 0
    for ref in weights[:-1]:
        out_ref[:depth, at : at + ref.shape[1]] = ref[...]
        at += ref.shape[1]
    out_ref[:depth, at:] = weights[-1][...].astype(F32).T.astype(BF)
    if n_rows:
        out_ref[depth:, :] = refs[-2][...]


def pack_call(weights, rows=None):
    depth = weights[0].shape[0]
    cols = sum(w.shape[1] for w in weights[:-1]) + weights[-1].shape[0]
    extra = [] if rows is None else [rows]
    return pl.pallas_call(
        functools.partial(pack_kernel, len(extra)),
        in_specs=[whole()] * (len(weights) + len(extra)),
        out_specs=whole(),
        out_shape=jax.ShapeDtypeStruct((depth + (0 if rows is None else rows.shape[0]), cols), BF),
        compiler_params=params(),
        cost_estimate=cost(3),
    )(*weights, *extra)


def qkv_kernel(nq, nk, halves, flag_ref, x_ref, cos_ref, sin_ref, *rest):
    normed_ref, lin_ref, rot_ref, ga_ref, gm_ref, gq_ref, gk_ref, w_out, w, gains, sems, out_sem = rest[-12:]
    step = pl.program_id(0)
    n_dp, depth, half = w.shape[0], w.shape[1], w.shape[2] // halves
    save = pltpu.make_async_copy(w, w_out, out_sem)

    @pl.when(step == 0)
    def _():
        rows, copies = [], []
        for i in range(halves):
            for n in range(n_dp):
                block, place = rest[i * n_dp + n], flag_ref[1] ^ n
                cols = pl.ds(i * half, half)
                copies.append(
                    pltpu.make_async_copy(block.at[pl.ds(0, depth)], w.at[place, :, cols], sems.at[i, n])
                )
                if i == 0:
                    rows.append(pltpu.make_async_copy(block.at[pl.ds(depth, 16)], gains.at[place], sems.at[halves, n]))
        start(rows + copies)
        wait(rows)
        of_q = jnp.zeros((1, HD), F32)
        of_k = jnp.zeros((1, HD), F32)
        for p in range(n_dp):
            g = gains[p].astype(F32)
            ga_ref[:, p * depth : (p + 1) * depth] = g[0:1, :depth]
            gm_ref[:, p * depth : (p + 1) * depth] = g[1:2, :depth]
            of_q = of_q + g[2:3, :HD]
            of_k = of_k + g[3:4, :HD]
        gq_ref[...] = of_q
        gk_ref[...] = of_k
        wait(copies)
        save.start()

    x = x_ref[...].astype(F32)
    normed = (x * rms_r(x) * ga_ref[...]).astype(BF)
    normed_ref[...] = normed
    acc = dot(normed, w[:, :, : rot_ref.shape[1]].reshape(n_dp * depth, rot_ref.shape[1]))
    cosine = cos_ref[...]
    sine = sin_ref[...]
    for h in range(nq + nk):
        v = acc[:, h * HD : (h + 1) * HD]
        gain = gq_ref[...] if h < nq else gk_ref[...]
        n = v * rms_r(v) * gain
        rot_ref[:, h * HD : (h + 1) * HD] = (n * cosine + pltpu.roll(n, HD // 2, 1) * sine).astype(BF)
    lin_ref[...] = acc[:, : (nq + nk) * HD]
    rot_ref[:, (nq + nk) * HD :] = acc[:, (nq + nk) * HD :].astype(BF)

    @pl.when(step == pl.num_programs(0) - 1)
    def _():
        save.wait()


def qkv_call(flag, x, cosine, sine, halves, nq, nk):
    tok, d = x.shape
    n_dp = len(halves[0])
    wide = len(halves) * halves[0][0].shape[1]
    cols = (nq + 2 * nk) * HD
    blk = lambda n: pl.BlockSpec((CHUNK, n), lambda i: (i, 0))
    one = lambda n: pl.BlockSpec((1, n), lambda i: (0, 0))
    lin = (nq + nk) * HD
    return pl.pallas_call(
        functools.partial(qkv_kernel, nq, nk, len(halves)),
        grid=(tok // CHUNK,),
        in_specs=[smem(), blk(d), blk(HD), blk(HD)] + [hbm()] * (len(halves) * n_dp),
        out_specs=[blk(d), blk(lin), blk(cols), one(d), one(d), one(HD), one(HD), hbm()],
        out_shape=[
            jax.ShapeDtypeStruct((tok, d), BF),
            jax.ShapeDtypeStruct((tok, lin), F32),
            jax.ShapeDtypeStruct((tok, cols), BF),
            jax.ShapeDtypeStruct((1, d), F32),
            jax.ShapeDtypeStruct((1, d), F32),
            jax.ShapeDtypeStruct((1, HD), F32),
            jax.ShapeDtypeStruct((1, HD), F32),
            jax.ShapeDtypeStruct((n_dp, d // n_dp, wide), BF),
        ],
        scratch_shapes=[
            pltpu.VMEM((n_dp, d // n_dp, wide), BF),
            pltpu.VMEM((n_dp, 16, wide // len(halves)), BF),
            pltpu.SemaphoreType.DMA((len(halves) + 1, n_dp)),
            pltpu.SemaphoreType.DMA,
        ],
        compiler_params=params(),
        cost_estimate=cost(14),
    )(flag, x, cosine, sine, *[b for h in halves for b in h])


def band(c):
    lo = max(c - 1, 0) * CHUNK
    return lo, (c + 1) * CHUNK - lo


def doc_start(ends_ref, token):
    first = jnp.zeros_like(token)
    for j in range(ends_ref.shape[0]):
        first = jnp.maximum(first, jnp.where(token >= ends_ref[j], ends_ref[j], 0))
    return first


def allowed(c, ends_ref):
    lo, width = band(c)
    t = lax.broadcasted_iota(jnp.int32, (CHUNK, 1), 0) + c * CHUNK
    u = lax.broadcasted_iota(jnp.int32, (CHUNK, width), 1) + lo
    return (u <= t) & (u >= doc_start(ends_ref, t))


def attn_kernel(c, nq, nk, ends_ref, rot_ref, w_hbm, *rest):
    att_ref, lse_ref, part_ref, w, sem = rest[-5:]
    copies = [fetch(w_hbm, w, sem, (nq + 2 * nk) * HD)]
    start(copies)
    lo, width = band(c)
    mask = allowed(c, ends_ref)
    group = nq // nk
    heads = []
    lses = []
    for h in range(nq):
        q = rot_ref[c * CHUNK : (c + 1) * CHUNK, h * HD : (h + 1) * HD]
        j = h // group
        k = rot_ref[lo : lo + width, (nq + j) * HD : (nq + j + 1) * HD]
        v = rot_ref[lo : lo + width, (nq + nk + j) * HD : (nq + nk + j + 1) * HD]
        s = jnp.where(mask, dot(q, k, NT) * SCALE, -1e30)
        m = jnp.max(s, axis=-1, keepdims=True)
        e = jnp.exp(s - m)
        l = jnp.sum(e, axis=-1, keepdims=True)
        heads.append(dot((e / l).astype(BF), v).astype(BF))
        lses.append(m + jnp.log(l))
    att = jnp.concatenate(heads, axis=1)
    att_ref[...] = att
    lse_ref[...] = jnp.concatenate(lses, axis=1)
    wait(copies)
    part_ref[...] = dot(att, joined(w), NT).astype(BF)


def chunk_block(c, n):
    return pl.BlockSpec((CHUNK, n), lambda i: (c, 0))


def attn_call(c, ends, rot, w, att, nq, nk):
    tok = rot.shape[0]
    n_dp, depth = w.shape[:2]
    d = n_dp * depth
    first = att is None
    full = lambda a: pl.BlockSpec(a.shape, lambda i: (0,) * a.ndim)
    return pl.pallas_call(
        functools.partial(attn_kernel, c, nq, nk),
        grid=(1,),
        in_specs=[smem(), full(rot)] + [hbm()] * (1 if first else 2),
        out_specs=[
            chunk_block(c, nq * HD),
            pl.BlockSpec((CHUNK, nq), lambda i: (0, 0)),
            pl.BlockSpec((CHUNK, d), lambda i: (0, 0)),
        ],
        out_shape=[
            jax.ShapeDtypeStruct((tok, nq * HD), BF),
            jax.ShapeDtypeStruct((CHUNK, nq), F32),
            jax.ShapeDtypeStruct((CHUNK, d), BF),
        ],
        scratch_shapes=[pltpu.VMEM((n_dp, depth, nq * HD), BF), pltpu.SemaphoreType.DMA],
        input_output_aliases={} if first else {3: 0},
        compiler_params=params(),
        cost_estimate=cost(5),
    )(ends, rot, w, *([] if first else [att]))


def mlp_kernel(c, tiles, flag_ref, x_hbm, t_hbm, r_hbm, cot_hbm, gain_ref, w_hbm, *rest):
    outs, rest = rest[-22:-15], rest[-15:]
    x_ref, t_ref, r_ref, cot_ref, mid_ref, n2_ref, prod_ref, gg_ref, gu_ref, down_ref, gnt_ref, acc_d, acc_g, w, sems = rest
    mid_out, n2_out, prod_out, gg_out, gu_out, down_out, gnt_out = outs
    tile = w.shape[4]
    rows = pl.ds(c * CHUNK, CHUNK)
    copy = pltpu.make_async_copy
    first = [copy(t_hbm, t_ref, sems.at[0]), copy(r_hbm, r_ref, sems.at[1]), copy(x_hbm.at[rows], x_ref, sems.at[2])]
    cot_copy = [copy(cot_hbm.at[rows], cot_ref, sems.at[3])]
    copies = [
        [[fetch(w_hbm, w.at[j % 2, i], sems.at[4 + 3 * (j % 2) + i], (i * tiles + j) * tile)] for i in range(3)]
        for j in range(tiles)
    ]
    saves = [copy(mid_ref, mid_out, sems.at[10]), copy(n2_ref, n2_out.at[rows], sems.at[11])]
    start(first + copies[0][0] + copies[0][1] + cot_copy + copies[0][2])
    for j in range(1, min(tiles, 2)):
        for i in range(3):
            start(copies[j][i])
    wait(first)
    branch = jnp.where(flag_ref[0] == 1, r_ref[...], t_ref[...]).astype(F32)
    mid = x_ref[...].astype(F32) + branch
    mid_ref[...] = mid
    n2_ref[...] = (mid * rms_r(mid) * gain_ref[...]).astype(BF)
    start(saves)
    for j in range(tiles):
        wg, wu, wd = (w.at[j % 2, i] for i in range(3))
        cols = pl.ds(j * tile, tile)
        wait(copies[j][0])
        g = dot(n2_ref[...], joined(wg))
        wait(copies[j][1])
        u = dot(n2_ref[...], joined(wu))
        if j == 0:
            wait(cot_copy)
        wait(copies[j][2])
        gp = dot(cot_ref[...], joined(wd))
        s = 1.0 / (1.0 + jnp.exp(-g))
        gs = g * s
        prod = (gs * u).astype(BF)
        gg = (gp * u * s * (1.0 + g * (1.0 - s))).astype(BF)
        gu = (gp * gs).astype(BF)
        prod_ref[:, j * tile : (j + 1) * tile] = prod
        gg_ref[:, j * tile : (j + 1) * tile] = gg
        gu_ref[:, j * tile : (j + 1) * tile] = gu
        now = [
            copy(ref.at[:, cols], out.at[rows, cols], sems.at[12 + 3 * j + i])
            for i, (ref, out) in enumerate(((prod_ref, prod_out), (gg_ref, gg_out), (gu_ref, gu_out)))
        ]
        start(now)
        saves += now
        gnt = dot(gg, joined(wg), NT) + dot(gu, joined(wu), NT)
        if j:
            gnt = gnt + acc_g[...]
        if j < tiles - 1:
            acc_g[...] = gnt
        else:
            gnt_ref[...] = gnt.astype(BF)
            now = [copy(gnt_ref, gnt_out, sems.at[12 + 3 * tiles])]
            start(now)
            saves += now
        down = dot(prod, joined(wd), NT)
        if j:
            down = down + acc_d[...]
        if j < tiles - 1:
            acc_d[...] = down
        else:
            down_ref[...] = down.astype(BF)
            now = [copy(down_ref, down_out, sems.at[13 + 3 * tiles])]
            start(now)
            saves += now
        if j + 2 < tiles:
            for i in range(3):
                start(copies[j + 2][i])
    wait(saves)


MLP_TILES = 3


def mlp_call(c, flag, x, t, r, cot, gain, w, kept):
    tok, d = x.shape
    n_dp, depth, ff = w.shape[0], w.shape[1], w.shape[2] // 3
    tiles = MLP_TILES
    first = kept is None
    n_alias = 0 if first else 4
    chunk = lambda n, kind: pltpu.VMEM((CHUNK, n), kind)
    out = pl.pallas_call(
        functools.partial(mlp_kernel, c, tiles),
        in_specs=[smem(), hbm(), hbm(), hbm(), hbm(), whole(), hbm()] + [hbm()] * n_alias,
        out_specs=[hbm()] * 7,
        out_shape=[
            jax.ShapeDtypeStruct((CHUNK, d), F32),
            jax.ShapeDtypeStruct((tok, d), BF),
            jax.ShapeDtypeStruct((tok, ff), BF),
            jax.ShapeDtypeStruct((tok, ff), BF),
            jax.ShapeDtypeStruct((tok, ff), BF),
            jax.ShapeDtypeStruct((CHUNK, d), BF),
            jax.ShapeDtypeStruct((CHUNK, d), BF),
        ],
        scratch_shapes=[chunk(d, BF)] * 4
        + [chunk(d, F32), chunk(d, BF)]
        + [chunk(ff, BF)] * 3
        + [chunk(d, BF)] * 2
        + [chunk(d, F32)] * 2
        + [pltpu.VMEM((2, 3, n_dp, depth, ff // tiles), BF), pltpu.SemaphoreType.DMA((14 + 3 * tiles,))],
        input_output_aliases={} if first else {7: 1, 8: 2, 9: 3, 10: 4},
        compiler_params=params(),
        cost_estimate=cost(19),
    )(flag, x, t, r, cot, gain, w, *([] if first else kept))
    return out[0], out[1:5], out[5], out[6]


def back_kernel(
    c, nq, nk, first, flag_ref, ends_ref, mid_ref, t_ref, r_ref, cot_ref, gain_ref, rot_hbm,
    lse_ref, lin_hbm, cos_ref, sin_ref, gq_ref, gk_ref, w_hbm, *rest,
):
    gm_out, gb_out, gqkv_ref, part_ref, gain_out, head_out, carry_out = rest[-16:-9]
    gm_ref, gb_ref, rot_ref, lin_ref, wo, w, sems, late_sems, save_sems = rest[-9:]
    lo, width = band(c)
    rows = pl.ds(c * CHUNK, CHUNK)
    late = [
        pltpu.make_async_copy(rot_hbm.at[pl.ds(lo, width)], rot_ref, late_sems.at[0]),
        pltpu.make_async_copy(lin_hbm.at[rows], lin_ref, late_sems.at[1]),
    ]
    saves = [
        pltpu.make_async_copy(gm_ref, gm_out, save_sems.at[0]),
        pltpu.make_async_copy(gb_ref, gb_out.at[rows], save_sems.at[1]),
    ]
    if not first:
        carry_ref, gain_in, head_in = rest[:3]
    out_copies = [fetch(w_hbm, wo, sems.at[0], (nq + 2 * nk) * HD)]
    in_copies = [fetch(w_hbm, w, sems.at[1], 0)]
    start(out_copies + late + in_copies)
    gnt = jnp.where(flag_ref[0] == 1, r_ref[...], t_ref[...]).astype(F32)
    mid = mid_ref[...]
    r2 = rms_r(mid)
    h = gnt * gain_ref[...]
    gm = (
        cot_ref[...].astype(F32)
        + r2 * h
        - mid * (r2 * r2 * r2 * jnp.mean(h * mid, axis=-1, keepdims=True))
    )
    gain_sum = jnp.sum(gnt * mid * r2, axis=0, keepdims=True)
    gain_out[...] = gain_sum if first else gain_in[...] + gain_sum
    gm_ref[...] = gm
    gb = gm.astype(BF)
    gb_ref[...] = gb
    start(saves)
    wait(out_copies)
    ga = dot(gb, joined(wo)).astype(BF)
    wait(late)
    mask = allowed(c, ends_ref)
    group = nq // nk
    cosine = cos_ref[...]
    sine = -sin_ref[...]

    def unrope(grad, lin, gain):
        gr = grad * cosine + pltpu.roll(grad, HD // 2, 1) * sine
        rr = rms_r(lin)
        hh = gr * gain
        out = rr * hh - lin * (rr * rr * rr * jnp.mean(hh * lin, axis=-1, keepdims=True))
        return out.astype(BF), jnp.sum(gr * lin * rr, axis=0, keepdims=True)

    sum_q = jnp.zeros((1, HD), F32) if first else head_in[0:1, :]
    sum_k = jnp.zeros((1, HD), F32) if first else head_in[1:2, :]
    outs = [None] * (nq + 2 * nk)
    for j in range(nk):
        k = rot_ref[:, (nq + j) * HD : (nq + j + 1) * HD]
        v = rot_ref[:, (nq + nk + j) * HD : (nq + nk + j + 1) * HD]
        dk = jnp.zeros((width, HD), F32)
        dv = jnp.zeros((width, HD), F32)
        for g in range(group):
            i = j * group + g
            q = rot_ref[width - CHUNK :, i * HD : (i + 1) * HD]
            gah = ga[:, i * HD : (i + 1) * HD]
            s = jnp.where(mask, dot(q, k, NT) * SCALE, -1e30)
            p = jnp.exp(s - lse_ref[:, i : i + 1])
            gw = dot(gah, v, NT)
            delta = jnp.sum(p * gw, axis=-1, keepdims=True)
            gs = (p * (gw - delta)).astype(BF)
            dq = (dot(gs, k) * SCALE).astype(BF).astype(F32)
            dk = dk + dot(gs, q, TN)
            dv = dv + dot(p.astype(BF), gah, TN)
            outs[i], part = unrope(dq, lin_ref[:, i * HD : (i + 1) * HD], gq_ref[...])
            sum_q = sum_q + part
        dk_own, dv_own = dk[width - CHUNK :], dv[width - CHUNK :]
        if not first:
            dk_own = dk_own + carry_ref[:, j * HD : (j + 1) * HD]
            dv_own = dv_own + carry_ref[:, (nk + j) * HD : (nk + j + 1) * HD]
        carry_out[:, j * HD : (j + 1) * HD] = dk[:CHUNK]
        carry_out[:, (nk + j) * HD : (nk + j + 1) * HD] = dv[:CHUNK]
        dk_own = (dk_own * SCALE).astype(BF).astype(F32)
        outs[nq + j], part = unrope(dk_own, lin_ref[:, (nq + j) * HD : (nq + j + 1) * HD], gk_ref[...])
        sum_k = sum_k + part
        outs[nq + nk + j] = dv_own.astype(BF)
    gqkv = jnp.concatenate(outs, axis=1)
    gqkv_ref[...] = gqkv
    head_out[0:1, :] = sum_q
    head_out[1:2, :] = sum_k
    wait(in_copies)
    part_ref[...] = dot(gqkv, joined(w), NT).astype(BF)
    wait(saves)


def back_call(
    c, flag, ends, mid, t, r, cot, gain, rot, lse, lin, cosine, sine, gq, gk, w, kept, carry, nq, nk
):
    tok, d = cot.shape
    first = carry is None
    full = lambda a: pl.BlockSpec(a.shape, lambda i: (0,) * a.ndim)
    args = [flag, ends, mid, t, r, cot, gain, rot, lse, lin, cosine, sine, gq, gk]
    specs = [smem(), smem()] + [full(a) for a in args[2:]]
    specs[5] = chunk_block(c, d)
    specs[7] = hbm()
    specs[9] = hbm()
    specs[10] = chunk_block(c, HD)
    specs[11] = chunk_block(c, HD)
    args.append(w)
    specs.append(hbm())
    if not first:
        args += [*carry, *kept]
        specs += [full(a) for a in carry] + [hbm(), hbm()]
    own = lambda n: pl.BlockSpec((CHUNK, n), lambda i: (0, 0))
    cols = (nq + 2 * nk) * HD
    n_dp = w.shape[0]
    depth = d // n_dp
    out = pl.pallas_call(
        functools.partial(back_kernel, c, nq, nk, first),
        grid=(1,),
        in_specs=specs,
        out_specs=[
            hbm(),
            hbm(),
            chunk_block(c, cols),
            own(d),
            pl.BlockSpec((1, d), lambda i: (0, 0)),
            pl.BlockSpec((2, HD), lambda i: (0, 0)),
            own(2 * nk * HD),
        ],
        out_shape=[
            jax.ShapeDtypeStruct((CHUNK, d), F32),
            jax.ShapeDtypeStruct((tok, d), BF),
            jax.ShapeDtypeStruct((tok, cols), BF),
            jax.ShapeDtypeStruct((CHUNK, d), BF),
            jax.ShapeDtypeStruct((1, d), F32),
            jax.ShapeDtypeStruct((2, HD), F32),
            jax.ShapeDtypeStruct((CHUNK, 2 * nk * HD), F32),
        ],
        scratch_shapes=[
            pltpu.VMEM((CHUNK, d), F32),
            pltpu.VMEM((CHUNK, d), BF),
            pltpu.VMEM((band(c)[1], cols), BF),
            pltpu.VMEM((CHUNK, lin.shape[1]), F32),
            pltpu.VMEM((n_dp, depth, nq * HD), BF),
            pltpu.VMEM((n_dp, depth, cols), BF),
            pltpu.SemaphoreType.DMA((2,)),
            pltpu.SemaphoreType.DMA((2,)),
            pltpu.SemaphoreType.DMA((2,)),
        ],
        input_output_aliases={} if first else {18: 1, 19: 2},
        compiler_params=params(),
        cost_estimate=cost(12),
    )(*args)
    return out[0], out[1:3], out[3], (out[6], out[4], out[5])


def grad_kernel(a_ref, b_ref, *rest):
    rest[-1][...] = dot(a_ref[...], b_ref[...], TN).astype(BF)


def grad_call(n_dp, total, at, a, b, kept):
    tok, d = a.shape
    depth = d // n_dp
    cols = b.shape[1]
    first = kept is None
    return pl.pallas_call(
        grad_kernel,
        grid=(n_dp,),
        in_specs=[pl.BlockSpec((tok, depth), lambda i: (0, i)), pl.BlockSpec(b.shape, lambda i: (0, 0))]
        + ([] if first else [hbm()]),
        out_specs=pl.BlockSpec((depth, cols), lambda i: (i, at // cols)),
        out_shape=jax.ShapeDtypeStruct((d, total), BF),
        input_output_aliases={} if first else {2: 0},
        compiler_params=params(),
        cost_estimate=cost(2 + cols // 185),
    )(a, b, *([] if first else [kept]))


def grad_pair_kernel(a_ref, b_ref, c_ref, d_ref, kept_ref, out_ref):
    cols = b_ref.shape[1]
    out_ref[:, :cols] = dot(a_ref[...], b_ref[...], TN).astype(BF)
    out_ref[:, cols:] = dot(c_ref[...], d_ref[...], TN).astype(BF)


def grad_pair_call(n_dp, at, a, b, c, d, kept):
    tok, rows = a.shape
    depth = rows // n_dp
    cols = b.shape[1] + d.shape[1]
    block = pl.BlockSpec((tok, depth), lambda i: (0, i))
    full = lambda x: pl.BlockSpec(x.shape, lambda i: (0, 0))
    return pl.pallas_call(
        grad_pair_kernel,
        grid=(n_dp,),
        in_specs=[block, full(b), block, full(d), hbm()],
        out_specs=pl.BlockSpec((depth, cols), lambda i: (i, at // cols)),
        out_shape=jax.ShapeDtypeStruct(kept.shape, BF),
        input_output_aliases={4: 0},
        compiler_params=params(),
        cost_estimate=cost(13),
    )(a, b, c, d, kept)


def input_kernel(first, flag_ref, x_ref, t_ref, r_ref, gm_ref, gain_ref, *rest):
    out_ref, gain_out = rest[-2:]
    gn = jnp.where(flag_ref[0] == 1, r_ref[...], t_ref[...]).astype(F32)
    x = x_ref[...].astype(F32)
    r1 = rms_r(x)
    h = gn * gain_ref[...]
    out_ref[...] = gm_ref[...] + r1 * h - x * (r1 * r1 * r1 * jnp.mean(h * x, axis=-1, keepdims=True))
    gain_sum = jnp.sum(gn * x * r1, axis=0, keepdims=True)
    gain_out[...] = gain_sum if first else rest[0][...] + gain_sum


def input_call(c, flag, x, t, r, gm, gain, kept):
    tok, d = x.shape
    own = pl.BlockSpec((CHUNK, d), lambda i: (0, 0))
    one = pl.BlockSpec((1, d), lambda i: (0, 0))
    first = kept is None
    return pl.pallas_call(
        functools.partial(input_kernel, first),
        grid=(1,),
        in_specs=[smem(), chunk_block(c, d), own, own, own, one] + ([] if first else [one, hbm()]),
        out_specs=[chunk_block(c, d), one],
        out_shape=[jax.ShapeDtypeStruct((tok, d), F32), jax.ShapeDtypeStruct((1, d), F32)],
        input_output_aliases={} if first else {7: 0},
        compiler_params=params(),
        cost_estimate=cost(5),
    )(flag, x, t, r, gm, gain, *([] if first else [kept[1], kept[0]]))


def output_kernel(aliased, flag_ref, mid_ref, t_ref, r_ref, *rest):
    out_ref = rest[-1]
    down = jnp.where(flag_ref[0] == 1, r_ref[...], t_ref[...]).astype(F32)
    out_ref[...] = (mid_ref[...] + down).astype(BF)


def output_call(c, flag, mid, t, r, kept, tok):
    d = mid.shape[1]
    own = pl.BlockSpec((CHUNK, d), lambda i: (0, 0))
    first = kept is None
    return pl.pallas_call(
        functools.partial(output_kernel, not first),
        grid=(1,),
        in_specs=[smem(), own, own, own] + ([] if first else [hbm()]),
        out_specs=chunk_block(c, d),
        out_shape=jax.ShapeDtypeStruct((tok, d), BF),
        input_output_aliases={} if first else {4: 0},
        compiler_params=params(),
        cost_estimate=cost(3),
    )(flag, mid, t, r, *([] if first else [kept]))


def line_sum(line, x):
    n = lax.axis_size("mp")
    me = lax.axis_index("mp")
    half = n // 2
    for h in range(half - 1):
        r = lax.ppermute(x, "mp", [(h, h + 1), (n - 1 - h, n - 2 - h)])
        yield
        x = line(jnp.add, x, r)
    r = lax.ppermute(x, "mp", [(half - 1, half), (half, half - 1)])
    yield
    x = line(jnp.add, x, r)
    r = x
    for h in reversed(range(half - 1)):
        r = lax.ppermute(x, "mp", [(h + 1, h), (n - 2 - h, n - 1 - h)])
        if h:
            yield
            x = line(jnp.where, (me == h) | (me == n - 1 - h), r, x)
    return x, r


class Sum:
    def __init__(self, line, *args, kind=line_sum):
        self.steps = kind(line, *args)
        self.result = None
        self.step()

    def step(self):
        try:
            if self.result is None:
                next(self.steps)
        except StopIteration as done:
            self.result = done.value

    def total(self):
        while self.result is None:
            self.step()
        return self.result


class Stream:
    def __init__(self, line):
        self.line = line
        self.four = lax.axis_size("mp") == 4
        me = lax.axis_index("mp")
        self.end = (me == 0) | (me == 3)
        self.parts, self.sent, self.got, self.sums = [], [], [], {}

    def push(self, part=None):
        i = len(self.parts)
        self.parts.append(part)
        if not self.four:
            if part is not None:
                self.sums[i] = Sum(self.line, part).total()
            return i
        pairs = [(1, 0), (2, 3)] + ([] if part is None else [(0, 1), (3, 2)])
        if part is None:
            part = self.line(jnp.add, *self.sums[i - 2])
        elif i > 1:
            part = self.line(lambda end, p, a, b: jnp.where(end, p, a + b), self.end, part, *self.sums[i - 2])
        self.sent.append(part)
        self.got.append(lax.ppermute(part, "mp", pairs))
        return i

    def middle(self, i):
        if self.four:
            both = self.line(jnp.add, self.parts[i], self.got[i])
            self.sums[i] = both, lax.ppermute(both, "mp", [(1, 2), (2, 1)])

    def total(self, i):
        return (self.sent[i + 2], self.got[i + 2]) if self.four else self.sums[i]


class Line:
    def __init__(self):
        self.last = None

    def after(self, *args):
        if self.last is None:
            return args
        leaves, tree = jax.tree.flatten(args)
        leaves = lax.optimization_barrier((*leaves, self.last))[:-1]
        return jax.tree.unflatten(tree, leaves)

    def __call__(self, f, *args, **kw):
        out = f(*self.after(*args), **kw)
        self.last = jax.tree.leaves(out)[-1]
        return out


SWAP = [(0, 1), (1, 0)]
DP = ("chip", "core")


def behind(x, arrays):
    return lax.optimization_barrier((x, jax.tree.leaves(arrays)))[0]


class Gather:
    def __init__(self, x, low_first):
        self.n = lax.axis_size("chip")
        bits = [1 << b for b in range(self.n.bit_length() - 1)]
        self.bits = bits if low_first else bits[::-1]
        self.own = {0: x}
        self.swapped = {0: lax.ppermute(x, "core", SWAP)}
        self.level = 0

    def step(self):
        bit = self.bits[self.level]
        self.level += 1
        new = {
            r ^ bit: lax.ppermute(b, "chip", [(i, i ^ bit) for i in range(self.n)]) for r, b in self.own.items()
        }
        self.own |= new
        return list(new.values())

    def swap(self):
        for r, b in self.own.items():
            if r not in self.swapped:
                self.swapped[r] = lax.ppermute(b, "core", SWAP)

    def blocks(self):
        while self.level < len(self.bits):
            self.step()
        self.swap()
        return [b[r] for r in range(self.n) for b in (self.own, self.swapped)]


def in_order(stacked, index):
    n = stacked.shape[0]
    bit = 1
    while bit < n:
        parts = stacked.reshape(n // (2 * bit), 2, bit, *stacked.shape[1:])
        stacked = jnp.where(index & bit, parts[:, ::-1], parts).reshape(stacked.shape)
        bit *= 2
    return stacked


def swap_sum(line, x, axis):
    n = lax.axis_size(axis)
    step = 1
    while step < n:
        got = lax.ppermute(x, axis, [(i, i ^ step) for i in range(n)])
        yield
        x = line(jnp.add, x, got)
        step *= 2
    return x


def own_sum(line, rows, index):
    rows = in_order(rows, index)
    half = rows.shape[0] // 2
    while half:
        if half > 1:
            pairs = [(i, i ^ (half // 2)) for i in range(lax.axis_size("chip"))]
            got = lax.ppermute(rows[half:], "chip", pairs)
        else:
            got = lax.ppermute(rows[half:], "core", SWAP)
        yield
        rows = line(jnp.add, rows[:half], got)
        half //= 2
    return rows[0]


def on_device(
    hidden_in,
    cotangent,
    doc_lengths,
    w_query,
    w_key,
    w_value,
    w_out,
    w_gate,
    w_up,
    w_down,
    norm_attn,
    norm_mlp,
    norm_query,
    norm_key,
):
    chips = lax.axis_size("chip")
    n_dp = 2 * chips
    core_id = lax.axis_index("core")
    dp = 2 * lax.axis_index("chip") + core_id
    mp = lax.axis_index("mp")
    n_mp = lax.axis_size("mp")
    tok, d = hidden_in.shape
    nq = w_query.shape[1] // HD
    nk = w_key.shape[1] // HD
    depth = w_query.shape[0]
    small = norm_query.shape[0]
    flag = jnp.stack([((mp == 0) | (mp == n_mp - 1)).astype(jnp.int32), dp])

    wide = (2 * nq + 2 * nk) * HD
    widen = lambda v: jnp.pad(v, (0, wide - v.shape[0]))[None]
    placed = lambda v: widen(lax.dynamic_update_slice(jnp.zeros(HD, BF), v, (dp * small,)))
    gain_rows = jnp.concatenate([widen(norm_attn), widen(norm_mlp), placed(norm_query), placed(norm_key)])
    gain_rows = jnp.pad(gain_rows, ((0, 12), (0, 0)))
    w_attn = pack_call([w_query, w_key, w_value, w_out], gain_rows)
    halves = [Gather(w_attn[:, : wide // 2], True), Gather(w_attn[:, wide // 2 :], False)]
    while halves[0].level < len(halves[0].bits):
        arrived = [h.step() for h in halves]
    w_mlp = behind(pack_call([w_gate, w_up, w_down]), arrived)
    w_mlp = lax.all_gather(w_mlp, DP, axis=0)

    lengths = lax.dynamic_index_in_dim(doc_lengths, dp, 0, keepdims=False)
    ends = jnp.cumsum(lengths)
    ends = ends.astype(jnp.int32)
    token = jnp.arange(tok, dtype=jnp.int32)
    begin = jnp.max(jnp.where(token[:, None] >= ends[None, :], ends[None, :], 0), axis=1)
    position = token - begin
    inverse = ROPE_BASE ** (-(2.0 * jnp.arange(HD // 2, dtype=F32)) / HD)
    angles = position.astype(F32)[:, None] * inverse[None, :]
    cosine = jnp.cos(angles)
    sine = jnp.sin(angles)
    cosine = jnp.concatenate([cosine, cosine], axis=1)
    sine = jnp.concatenate([-sine, sine], axis=1)

    line = Line()

    normed, lin, rot, gain_attn, gain_mlp, gain_query, gain_key, w_attn = line(
        functools.partial(qkv_call, nq=nq, nk=nk), flag, hidden_in, cosine, sine, [h.blocks() for h in halves]
    )

    order = list(reversed(range(tok // CHUNK)))
    att = None
    lse, branch, mid, down, gnt, gn = {}, {}, {}, {}, {}, {}
    stream = Stream(line)
    for k, c in enumerate(order):
        att, lse[c], part = line(functools.partial(attn_call, c, nq=nq, nk=nk), ends, rot, w_attn, att)
        branch[c] = stream.push(part) if k < 2 else part

    c0, c1, c2, c3 = order
    state = {"mlp": None, "back": None, "carry": None, "input": None, "output": None}
    gm = {}
    ff = w_gate.shape[1]

    def run_mlp(c):
        t, r = stream.total(branch[c])
        mid[c], state["mlp"], down[c], gnt_part = line(
            functools.partial(mlp_call, c), flag, hidden_in, t, r, cotangent, gain_mlp,
            w_mlp, state["mlp"],
        )
        gnt[c] = gnt_part

    def run_back(c):
        t, r = stream.total(gnt[c])
        gm[c], state["back"], part, state["carry"] = line(
            functools.partial(back_call, c, nq=nq, nk=nk), flag, ends, mid[c], t, r, cotangent,
            gain_mlp, rot, lse[c], lin, cosine, sine, gain_query, gain_key, w_attn,
            state["back"], state["carry"],
        )
        gn[c] = part

    def run_input(c):
        t, r = stream.total(gn[c])
        state["input"] = line(
            functools.partial(input_call, c), flag, hidden_in, t, r, gm[c], gain_attn, state["input"]
        )

    def run_output(c):
        t, r = stream.total(down[c])
        state["output"] = line(functools.partial(output_call, c, tok=tok), flag, mid[c], t, r, state["output"])

    def push(of, c):
        of[c] = stream.push(line.after(of[c])[0])

    def grad(total, at, a, b, kept=None):
        return line(functools.partial(grad_call, n_dp, total, at), a, b, kept)

    def scatter(g):
        return lax.psum_scatter(line.after(g)[0], DP, scatter_dimension=0, tiled=True)

    def split(grads):
        outs, at = [], 0
        for cols in (ff, ff, ff, nq * HD, nk * HD, nk * HD, nq * HD):
            outs.append(grads[:, at : at + cols].astype(F32))
            at += cols
        outs[2], outs[6] = outs[2].T, outs[6].T
        return outs

    stream.middle(branch[c0])
    stream.middle(branch[c1])
    push(branch, c2)
    push(branch, c3)
    stream.middle(branch[c2])
    run_mlp(c0)
    stream.middle(branch[c3])
    push(gnt, c0)
    run_mlp(c1)
    push(gnt, c1)
    stream.middle(gnt[c0])
    run_mlp(c2)
    stream.middle(gnt[c1])
    push(gnt, c2)
    run_mlp(c3)
    n2, prod, gg, gu = state["mlp"]
    push(gnt, c3)
    stream.middle(gnt[c2])
    run_back(c0)
    g_mlp = grad(3 * ff + wide, 0, n2, gg)
    stream.middle(gnt[c3])
    push(gn, c0)
    run_back(c1)
    g_mlp = grad(3 * ff + wide, ff, n2, gu, g_mlp)
    push(down, c0)
    stream.middle(gn[c0])
    run_back(c2)
    g_mlp = grad(3 * ff + wide, 2 * ff, cotangent, prod, g_mlp)
    push(gn, c1)
    stream.middle(down[c0])
    run_back(c3)
    gb, gqkv = state["back"]
    grads = scatter(line(functools.partial(grad_pair_call, n_dp, 3 * ff), normed, gqkv, gb, att, g_mlp))
    push(gn, c2)
    stream.middle(gn[c1])
    run_input(c0)
    push(gn, c3)
    stream.middle(gn[c2])
    run_output(c0)
    push(down, c1)
    stream.middle(gn[c3])
    run_input(c1)
    _, sum_mlp, sum_head = state["carry"]
    heads = Sum(line, sum_head, "mp", kind=swap_sum)
    push(down, c2)
    stream.middle(down[c1])
    run_input(c2)
    heads.step()
    push(down, c3)
    stream.middle(down[c2])
    run_input(c3)
    grad_input, sum_attn = state["input"]
    heads = heads.total()
    sums = jnp.concatenate(
        [sum_attn.reshape(n_dp, depth), sum_mlp.reshape(n_dp, depth)]
        + [heads[i].reshape(n_dp, small) for i in range(2)],
        axis=1,
    )
    sums = Sum(line, sums, dp, kind=own_sum)
    stream.push()
    stream.middle(down[c3])
    sums.step()
    run_output(c1)
    sums.step()
    stream.push()
    run_output(c2)
    sums = sums.total()
    outs = line(split, grads)
    run_output(c3)

    return (
        state["output"],
        grad_input,
        *outs[3:6],
        outs[6],
        outs[0],
        outs[1],
        outs[2],
        sums[:depth],
        sums[depth : 2 * depth],
        sums[2 * depth : 2 * depth + small],
        sums[2 * depth + small :],
    )


def solution(mesh):
    n_dp, n_mp = mesh.devices.shape
    mesh = jax.sharding.Mesh(mesh.devices.reshape(n_dp // 2, 2, n_mp), ("chip", "core", "mp"))
    rows = P(DP, None)
    weight = P(DP, "mp")
    turned = P("mp", DP)
    gain = P(DP)
    return jax.shard_map(
        on_device,
        mesh=mesh,
        in_specs=(rows, rows, P(), weight, weight, weight, turned, weight, weight, turned, gain, gain, gain, gain),
        out_specs=(rows, rows, weight, weight, weight, turned, weight, weight, turned, gain, gain, gain, gain),
        check_vma=False,
    )
```

```python
import functools

import jax
import jax.numpy as jnp
from jax import lax
from jax.experimental import pallas as pl
from jax.experimental.pallas import tpu as pltpu
from jax.sharding import PartitionSpec as P

HD = 128
CHUNK = 256
EPSILON = 1e-06
ROPE_BASE = 1000000.0
SCALE = HD ** (-0.5)
BF = jnp.bfloat16
F32 = jnp.float32
VMEM_LIMIT = 56 * 1024 * 1024

NN = (((1,), (0,)), ((), ()))
NT = (((1,), (1,)), ((), ()))
TN = (((0,), (0,)), ((), ()))


def dot(a, b, dims=NN):
    return lax.dot_general(a, b, dims, preferred_element_type=F32)


def whole():
    return pl.BlockSpec(memory_space=pltpu.VMEM)


def smem():
    return pl.BlockSpec(memory_space=pltpu.SMEM)


def hbm():
    return pl.BlockSpec(memory_space=pl.ANY)


def params(**kw):
    return pltpu.CompilerParams(vmem_limit_bytes=VMEM_LIMIT, **kw)


def cost(us):
    return pl.CostEstimate(flops=0, bytes_accessed=3690000 * us, transcendentals=0)


def rms_r(values):
    return lax.rsqrt(jnp.mean(values * values, axis=-1, keepdims=True) + EPSILON)


def fetch(gathered, dest, sem, first):
    depth, cols = dest.shape[1:]
    return pltpu.make_async_copy(gathered.at[:, pl.ds(0, depth), pl.ds(first, cols)], dest, sem)


def start(copies):
    for copy in copies:
        copy.start()


def wait(copies):
    for copy in copies:
        copy.wait()


def joined(ref):
    a, b, n = ref.shape
    return ref[...].reshape(a * b, n)


def pack_kernel(n_rows, *refs):
    out_ref = refs[-1]
    weights = refs[: len(refs) - 1 - n_rows]
    depth = weights[0].shape[0]
    at = 0
    for ref in weights[:-1]:
        out_ref[:depth, at : at + ref.shape[1]] = ref[...]
        at += ref.shape[1]
    out_ref[:depth, at:] = weights[-1][...].astype(F32).T.astype(BF)
    if n_rows:
        out_ref[depth:, :] = refs[-2][...]


def pack_call(weights, rows=None):
    depth = weights[0].shape[0]
    cols = sum(w.shape[1] for w in weights[:-1]) + weights[-1].shape[0]
    extra = [] if rows is None else [rows]
    return pl.pallas_call(
        functools.partial(pack_kernel, len(extra)),
        in_specs=[whole()] * (len(weights) + len(extra)),
        out_specs=whole(),
        out_shape=jax.ShapeDtypeStruct((depth + (0 if rows is None else rows.shape[0]), cols), BF),
        compiler_params=params(),
        cost_estimate=cost(3),
    )(*weights, *extra)


def qkv_kernel(nq, nk, halves, flag_ref, x_ref, cos_ref, sin_ref, *rest):
    normed_ref, lin_ref, rot_ref, ga_ref, gm_ref, gq_ref, gk_ref, w_out, w, gains, sems, out_sem = rest[-12:]
    step = pl.program_id(0)
    n_dp, depth, half = w.shape[0], w.shape[1], w.shape[2] // halves
    save = pltpu.make_async_copy(w, w_out, out_sem)

    @pl.when(step == 0)
    def _():
        rows, copies = [], []
        for i in range(halves):
            for n in range(n_dp):
                block, place = rest[i * n_dp + n], flag_ref[1] ^ n
                cols = pl.ds(i * half, half)
                copies.append(
                    pltpu.make_async_copy(block.at[pl.ds(0, depth)], w.at[place, :, cols], sems.at[i, n])
                )
                if i == 0:
                    rows.append(pltpu.make_async_copy(block.at[pl.ds(depth, 16)], gains.at[place], sems.at[halves, n]))
        start(rows + copies)
        wait(rows)
        of_q = jnp.zeros((1, HD), F32)
        of_k = jnp.zeros((1, HD), F32)
        for p in range(n_dp):
            g = gains[p].astype(F32)
            ga_ref[:, p * depth : (p + 1) * depth] = g[0:1, :depth]
            gm_ref[:, p * depth : (p + 1) * depth] = g[1:2, :depth]
            of_q = of_q + g[2:3, :HD]
            of_k = of_k + g[3:4, :HD]
        gq_ref[...] = of_q
        gk_ref[...] = of_k
        wait(copies)
        save.start()

    x = x_ref[...].astype(F32)
    normed = (x * rms_r(x) * ga_ref[...]).astype(BF)
    normed_ref[...] = normed
    acc = dot(normed, w[:, :, : rot_ref.shape[1]].reshape(n_dp * depth, rot_ref.shape[1]))
    cosine = cos_ref[...]
    sine = sin_ref[...]
    for h in range(nq + nk):
        v = acc[:, h * HD : (h + 1) * HD]
        gain = gq_ref[...] if h < nq else gk_ref[...]
        n = v * rms_r(v) * gain
        rot_ref[:, h * HD : (h + 1) * HD] = (n * cosine + pltpu.roll(n, HD // 2, 1) * sine).astype(BF)
    lin_ref[...] = acc[:, : (nq + nk) * HD]
    rot_ref[:, (nq + nk) * HD :] = acc[:, (nq + nk) * HD :].astype(BF)

    @pl.when(step == pl.num_programs(0) - 1)
    def _():
        save.wait()


def qkv_call(flag, x, cosine, sine, halves, nq, nk):
    tok, d = x.shape
    n_dp = len(halves[0])
    wide = len(halves) * halves[0][0].shape[1]
    cols = (nq + 2 * nk) * HD
    blk = lambda n: pl.BlockSpec((CHUNK, n), lambda i: (i, 0))
    one = lambda n: pl.BlockSpec((1, n), lambda i: (0, 0))
    lin = (nq + nk) * HD
    return pl.pallas_call(
        functools.partial(qkv_kernel, nq, nk, len(halves)),
        grid=(tok // CHUNK,),
        in_specs=[smem(), blk(d), blk(HD), blk(HD)] + [hbm()] * (len(halves) * n_dp),
        out_specs=[blk(d), blk(lin), blk(cols), one(d), one(d), one(HD), one(HD), hbm()],
        out_shape=[
            jax.ShapeDtypeStruct((tok, d), BF),
            jax.ShapeDtypeStruct((tok, lin), F32),
            jax.ShapeDtypeStruct((tok, cols), BF),
            jax.ShapeDtypeStruct((1, d), F32),
            jax.ShapeDtypeStruct((1, d), F32),
            jax.ShapeDtypeStruct((1, HD), F32),
            jax.ShapeDtypeStruct((1, HD), F32),
            jax.ShapeDtypeStruct((n_dp, d // n_dp, wide), BF),
        ],
        scratch_shapes=[
            pltpu.VMEM((n_dp, d // n_dp, wide), BF),
            pltpu.VMEM((n_dp, 16, wide // len(halves)), BF),
            pltpu.SemaphoreType.DMA((len(halves) + 1, n_dp)),
            pltpu.SemaphoreType.DMA,
        ],
        compiler_params=params(),
        cost_estimate=cost(14),
    )(flag, x, cosine, sine, *[b for h in halves for b in h])


def band(c):
    lo = max(c - 1, 0) * CHUNK
    return lo, (c + 1) * CHUNK - lo


def doc_start(ends_ref, token):
    first = jnp.zeros_like(token)
    for j in range(ends_ref.shape[0]):
        first = jnp.maximum(first, jnp.where(token >= ends_ref[j], ends_ref[j], 0))
    return first


def allowed(c, ends_ref):
    lo, width = band(c)
    t = lax.broadcasted_iota(jnp.int32, (CHUNK, 1), 0) + c * CHUNK
    u = lax.broadcasted_iota(jnp.int32, (CHUNK, width), 1) + lo
    return (u <= t) & (u >= doc_start(ends_ref, t))


def attn_kernel(c, nq, nk, ends_ref, rot_ref, w_hbm, *rest):
    att_ref, lse_ref, part_ref, w, sem = rest[-5:]
    copies = [fetch(w_hbm, w, sem, (nq + 2 * nk) * HD)]
    start(copies)
    lo, width = band(c)
    mask = allowed(c, ends_ref)
    group = nq // nk
    heads = []
    lses = []
    for h in range(nq):
        q = rot_ref[c * CHUNK : (c + 1) * CHUNK, h * HD : (h + 1) * HD]
        j = h // group
        k = rot_ref[lo : lo + width, (nq + j) * HD : (nq + j + 1) * HD]
        v = rot_ref[lo : lo + width, (nq + nk + j) * HD : (nq + nk + j + 1) * HD]
        s = jnp.where(mask, dot(q, k, NT) * SCALE, -1e30)
        m = jnp.max(s, axis=-1, keepdims=True)
        e = jnp.exp(s - m)
        l = jnp.sum(e, axis=-1, keepdims=True)
        heads.append(dot((e / l).astype(BF), v).astype(BF))
        lses.append(m + jnp.log(l))
    att = jnp.concatenate(heads, axis=1)
    att_ref[...] = att
    lse_ref[...] = jnp.concatenate(lses, axis=1)
    wait(copies)
    part_ref[...] = dot(att, joined(w), NT).astype(BF)


def chunk_block(c, n):
    return pl.BlockSpec((CHUNK, n), lambda i: (c, 0))


def attn_call(c, ends, rot, w, att, nq, nk):
    tok = rot.shape[0]
    n_dp, depth = w.shape[:2]
    d = n_dp * depth
    first = att is None
    full = lambda a: pl.BlockSpec(a.shape, lambda i: (0,) * a.ndim)
    return pl.pallas_call(
        functools.partial(attn_kernel, c, nq, nk),
        grid=(1,),
        in_specs=[smem(), full(rot)] + [hbm()] * (1 if first else 2),
        out_specs=[
            chunk_block(c, nq * HD),
            pl.BlockSpec((CHUNK, nq), lambda i: (0, 0)),
            pl.BlockSpec((CHUNK, d), lambda i: (0, 0)),
        ],
        out_shape=[
            jax.ShapeDtypeStruct((tok, nq * HD), BF),
            jax.ShapeDtypeStruct((CHUNK, nq), F32),
            jax.ShapeDtypeStruct((CHUNK, d), BF),
        ],
        scratch_shapes=[pltpu.VMEM((n_dp, depth, nq * HD), BF), pltpu.SemaphoreType.DMA],
        input_output_aliases={} if first else {3: 0},
        compiler_params=params(),
        cost_estimate=cost(5),
    )(ends, rot, w, *([] if first else [att]))


def mlp_kernel(c, tiles, flag_ref, x_hbm, t_hbm, r_hbm, cot_hbm, gain_ref, w_hbm, *rest):
    outs, rest = rest[-22:-15], rest[-15:]
    x_ref, t_ref, r_ref, cot_ref, mid_ref, n2_ref, prod_ref, gg_ref, gu_ref, down_ref, gnt_ref, acc_d, acc_g, w, sems = rest
    mid_out, n2_out, prod_out, gg_out, gu_out, down_out, gnt_out = outs
    tile = w.shape[4]
    rows = pl.ds(c * CHUNK, CHUNK)
    copy = pltpu.make_async_copy
    first = [copy(t_hbm, t_ref, sems.at[0]), copy(r_hbm, r_ref, sems.at[1]), copy(x_hbm.at[rows], x_ref, sems.at[2])]
    cot_copy = [copy(cot_hbm.at[rows], cot_ref, sems.at[3])]
    copies = [
        [[fetch(w_hbm, w.at[j % 2, i], sems.at[4 + 3 * (j % 2) + i], (i * tiles + j) * tile)] for i in range(3)]
        for j in range(tiles)
    ]
    saves = [copy(mid_ref, mid_out, sems.at[10]), copy(n2_ref, n2_out.at[rows], sems.at[11])]
    start(first + copies[0][0] + copies[0][1] + cot_copy + copies[0][2])
    for j in range(1, min(tiles, 2)):
        for i in range(3):
            start(copies[j][i])
    wait(first)
    branch = jnp.where(flag_ref[0] == 1, r_ref[...], t_ref[...]).astype(F32)
    mid = x_ref[...].astype(F32) + branch
    mid_ref[...] = mid
    n2_ref[...] = (mid * rms_r(mid) * gain_ref[...]).astype(BF)
    start(saves)
    for j in range(tiles):
        wg, wu, wd = (w.at[j % 2, i] for i in range(3))
        cols = pl.ds(j * tile, tile)
        wait(copies[j][0])
        g = dot(n2_ref[...], joined(wg))
        wait(copies[j][1])
        u = dot(n2_ref[...], joined(wu))
        if j == 0:
            wait(cot_copy)
        wait(copies[j][2])
        gp = dot(cot_ref[...], joined(wd))
        s = 1.0 / (1.0 + jnp.exp(-g))
        gs = g * s
        prod = (gs * u).astype(BF)
        gg = (gp * u * s * (1.0 + g * (1.0 - s))).astype(BF)
        gu = (gp * gs).astype(BF)
        prod_ref[:, j * tile : (j + 1) * tile] = prod
        gg_ref[:, j * tile : (j + 1) * tile] = gg
        gu_ref[:, j * tile : (j + 1) * tile] = gu
        now = [
            copy(ref.at[:, cols], out.at[rows, cols], sems.at[12 + 3 * j + i])
            for i, (ref, out) in enumerate(((prod_ref, prod_out), (gg_ref, gg_out), (gu_ref, gu_out)))
        ]
        start(now)
        saves += now
        gnt = dot(gg, joined(wg), NT) + dot(gu, joined(wu), NT)
        if j:
            gnt = gnt + acc_g[...]
        if j < tiles - 1:
            acc_g[...] = gnt
        else:
            gnt_ref[...] = gnt.astype(BF)
            now = [copy(gnt_ref, gnt_out, sems.at[12 + 3 * tiles])]
            start(now)
            saves += now
        down = dot(prod, joined(wd), NT)
        if j:
            down = down + acc_d[...]
        if j < tiles - 1:
            acc_d[...] = down
        else:
            down_ref[...] = down.astype(BF)
            now = [copy(down_ref, down_out, sems.at[13 + 3 * tiles])]
            start(now)
            saves += now
        if j + 2 < tiles:
            for i in range(3):
                start(copies[j + 2][i])
    wait(saves)


MLP_TILES = 3


def mlp_call(c, flag, x, t, r, cot, gain, w, kept):
    tok, d = x.shape
    n_dp, depth, ff = w.shape[0], w.shape[1], w.shape[2] // 3
    tiles = MLP_TILES
    first = kept is None
    n_alias = 0 if first else 4
    chunk = lambda n, kind: pltpu.VMEM((CHUNK, n), kind)
    out = pl.pallas_call(
        functools.partial(mlp_kernel, c, tiles),
        in_specs=[smem(), hbm(), hbm(), hbm(), hbm(), whole(), hbm()] + [hbm()] * n_alias,
        out_specs=[hbm()] * 7,
        out_shape=[
            jax.ShapeDtypeStruct((CHUNK, d), F32),
            jax.ShapeDtypeStruct((tok, d), BF),
            jax.ShapeDtypeStruct((tok, ff), BF),
            jax.ShapeDtypeStruct((tok, ff), BF),
            jax.ShapeDtypeStruct((tok, ff), BF),
            jax.ShapeDtypeStruct((CHUNK, d), BF),
            jax.ShapeDtypeStruct((CHUNK, d), BF),
        ],
        scratch_shapes=[chunk(d, BF)] * 4
        + [chunk(d, F32), chunk(d, BF)]
        + [chunk(ff, BF)] * 3
        + [chunk(d, BF)] * 2
        + [chunk(d, F32)] * 2
        + [pltpu.VMEM((2, 3, n_dp, depth, ff // tiles), BF), pltpu.SemaphoreType.DMA((14 + 3 * tiles,))],
        input_output_aliases={} if first else {7: 1, 8: 2, 9: 3, 10: 4},
        compiler_params=params(),
        cost_estimate=cost(19),
    )(flag, x, t, r, cot, gain, w, *([] if first else kept))
    return out[0], out[1:5], out[5], out[6]


def back_kernel(
    c, nq, nk, first, flag_ref, ends_ref, mid_ref, t_ref, r_ref, cot_ref, gain_ref, rot_hbm,
    lse_ref, lin_hbm, cos_ref, sin_ref, gq_ref, gk_ref, w_hbm, *rest,
):
    gm_out, gb_out, gqkv_ref, part_ref, gain_out, head_out, carry_out = rest[-16:-9]
    gm_ref, gb_ref, rot_ref, lin_ref, wo, w, sems, late_sems, save_sems = rest[-9:]
    lo, width = band(c)
    rows = pl.ds(c * CHUNK, CHUNK)
    late = [
        pltpu.make_async_copy(rot_hbm.at[pl.ds(lo, width)], rot_ref, late_sems.at[0]),
        pltpu.make_async_copy(lin_hbm.at[rows], lin_ref, late_sems.at[1]),
    ]
    saves = [
        pltpu.make_async_copy(gm_ref, gm_out, save_sems.at[0]),
        pltpu.make_async_copy(gb_ref, gb_out.at[rows], save_sems.at[1]),
    ]
    if not first:
        carry_ref, gain_in, head_in = rest[:3]
    out_copies = [fetch(w_hbm, wo, sems.at[0], (nq + 2 * nk) * HD)]
    in_copies = [fetch(w_hbm, w, sems.at[1], 0)]
    start(out_copies + late + in_copies)
    gnt = jnp.where(flag_ref[0] == 1, r_ref[...], t_ref[...]).astype(F32)
    mid = mid_ref[...]
    r2 = rms_r(mid)
    h = gnt * gain_ref[...]
    gm = (
        cot_ref[...].astype(F32)
        + r2 * h
        - mid * (r2 * r2 * r2 * jnp.mean(h * mid, axis=-1, keepdims=True))
    )
    gain_sum = jnp.sum(gnt * mid * r2, axis=0, keepdims=True)
    gain_out[...] = gain_sum if first else gain_in[...] + gain_sum
    gm_ref[...] = gm
    gb = gm.astype(BF)
    gb_ref[...] = gb
    start(saves)
    wait(out_copies)
    ga = dot(gb, joined(wo)).astype(BF)
    wait(late)
    mask = allowed(c, ends_ref)
    group = nq // nk
    cosine = cos_ref[...]
    sine = -sin_ref[...]

    def unrope(grad, lin, gain):
        gr = grad * cosine + pltpu.roll(grad, HD // 2, 1) * sine
        rr = rms_r(lin)
        hh = gr * gain
        out = rr * hh - lin * (rr * rr * rr * jnp.mean(hh * lin, axis=-1, keepdims=True))
        return out.astype(BF), jnp.sum(gr * lin * rr, axis=0, keepdims=True)

    sum_q = jnp.zeros((1, HD), F32) if first else head_in[0:1, :]
    sum_k = jnp.zeros((1, HD), F32) if first else head_in[1:2, :]
    outs = [None] * (nq + 2 * nk)
    for j in range(nk):
        k = rot_ref[:, (nq + j) * HD : (nq + j + 1) * HD]
        v = rot_ref[:, (nq + nk + j) * HD : (nq + nk + j + 1) * HD]
        dk = jnp.zeros((width, HD), F32)
        dv = jnp.zeros((width, HD), F32)
        for g in range(group):
            i = j * group + g
            q = rot_ref[width - CHUNK :, i * HD : (i + 1) * HD]
            gah = ga[:, i * HD : (i + 1) * HD]
            s = jnp.where(mask, dot(q, k, NT) * SCALE, -1e30)
            p = jnp.exp(s - lse_ref[:, i : i + 1])
            gw = dot(gah, v, NT)
            delta = jnp.sum(p * gw, axis=-1, keepdims=True)
            gs = (p * (gw - delta)).astype(BF)
            dq = (dot(gs, k) * SCALE).astype(BF).astype(F32)
            dk = dk + dot(gs, q, TN)
            dv = dv + dot(p.astype(BF), gah, TN)
            outs[i], part = unrope(dq, lin_ref[:, i * HD : (i + 1) * HD], gq_ref[...])
            sum_q = sum_q + part
        dk_own, dv_own = dk[width - CHUNK :], dv[width - CHUNK :]
        if not first:
            dk_own = dk_own + carry_ref[:, j * HD : (j + 1) * HD]
            dv_own = dv_own + carry_ref[:, (nk + j) * HD : (nk + j + 1) * HD]
        carry_out[:, j * HD : (j + 1) * HD] = dk[:CHUNK]
        carry_out[:, (nk + j) * HD : (nk + j + 1) * HD] = dv[:CHUNK]
        dk_own = (dk_own * SCALE).astype(BF).astype(F32)
        outs[nq + j], part = unrope(dk_own, lin_ref[:, (nq + j) * HD : (nq + j + 1) * HD], gk_ref[...])
        sum_k = sum_k + part
        outs[nq + nk + j] = dv_own.astype(BF)
    gqkv = jnp.concatenate(outs, axis=1)
    gqkv_ref[...] = gqkv
    head_out[0:1, :] = sum_q
    head_out[1:2, :] = sum_k
    wait(in_copies)
    part_ref[...] = dot(gqkv, joined(w), NT).astype(BF)
    wait(saves)


def back_call(
    c, flag, ends, mid, t, r, cot, gain, rot, lse, lin, cosine, sine, gq, gk, w, kept, carry, nq, nk
):
    tok, d = cot.shape
    first = carry is None
    full = lambda a: pl.BlockSpec(a.shape, lambda i: (0,) * a.ndim)
    args = [flag, ends, mid, t, r, cot, gain, rot, lse, lin, cosine, sine, gq, gk]
    specs = [smem(), smem()] + [full(a) for a in args[2:]]
    specs[5] = chunk_block(c, d)
    specs[7] = hbm()
    specs[9] = hbm()
    specs[10] = chunk_block(c, HD)
    specs[11] = chunk_block(c, HD)
    args.append(w)
    specs.append(hbm())
    if not first:
        args += [*carry, *kept]
        specs += [full(a) for a in carry] + [hbm(), hbm()]
    own = lambda n: pl.BlockSpec((CHUNK, n), lambda i: (0, 0))
    cols = (nq + 2 * nk) * HD
    n_dp = w.shape[0]
    depth = d // n_dp
    out = pl.pallas_call(
        functools.partial(back_kernel, c, nq, nk, first),
        grid=(1,),
        in_specs=specs,
        out_specs=[
            hbm(),
            hbm(),
            chunk_block(c, cols),
            own(d),
            pl.BlockSpec((1, d), lambda i: (0, 0)),
            pl.BlockSpec((2, HD), lambda i: (0, 0)),
            own(2 * nk * HD),
        ],
        out_shape=[
            jax.ShapeDtypeStruct((CHUNK, d), F32),
            jax.ShapeDtypeStruct((tok, d), BF),
            jax.ShapeDtypeStruct((tok, cols), BF),
            jax.ShapeDtypeStruct((CHUNK, d), BF),
            jax.ShapeDtypeStruct((1, d), F32),
            jax.ShapeDtypeStruct((2, HD), F32),
            jax.ShapeDtypeStruct((CHUNK, 2 * nk * HD), F32),
        ],
        scratch_shapes=[
            pltpu.VMEM((CHUNK, d), F32),
            pltpu.VMEM((CHUNK, d), BF),
            pltpu.VMEM((band(c)[1], cols), BF),
            pltpu.VMEM((CHUNK, lin.shape[1]), F32),
            pltpu.VMEM((n_dp, depth, nq * HD), BF),
            pltpu.VMEM((n_dp, depth, cols), BF),
            pltpu.SemaphoreType.DMA((2,)),
            pltpu.SemaphoreType.DMA((2,)),
            pltpu.SemaphoreType.DMA((2,)),
        ],
        input_output_aliases={} if first else {18: 1, 19: 2},
        compiler_params=params(),
        cost_estimate=cost(12),
    )(*args)
    return out[0], out[1:3], out[3], (out[6], out[4], out[5])


def grad_kernel(a_ref, b_ref, *rest):
    rest[-1][...] = dot(a_ref[...], b_ref[...], TN).astype(BF)


def grad_call(n_dp, total, at, a, b, kept):
    tok, d = a.shape
    depth = d // n_dp
    cols = b.shape[1]
    first = kept is None
    return pl.pallas_call(
        grad_kernel,
        grid=(n_dp,),
        in_specs=[pl.BlockSpec((tok, depth), lambda i: (0, i)), pl.BlockSpec(b.shape, lambda i: (0, 0))]
        + ([] if first else [hbm()]),
        out_specs=pl.BlockSpec((depth, cols), lambda i: (i, at // cols)),
        out_shape=jax.ShapeDtypeStruct((d, total), BF),
        input_output_aliases={} if first else {2: 0},
        compiler_params=params(),
        cost_estimate=cost(2 + cols // 185),
    )(a, b, *([] if first else [kept]))


def grad_pair_kernel(a_ref, b_ref, c_ref, d_ref, kept_ref, out_ref):
    cols = b_ref.shape[1]
    out_ref[:, :cols] = dot(a_ref[...], b_ref[...], TN).astype(BF)
    out_ref[:, cols:] = dot(c_ref[...], d_ref[...], TN).astype(BF)


def grad_pair_call(n_dp, at, a, b, c, d, kept):
    tok, rows = a.shape
    depth = rows // n_dp
    cols = b.shape[1] + d.shape[1]
    block = pl.BlockSpec((tok, depth), lambda i: (0, i))
    full = lambda x: pl.BlockSpec(x.shape, lambda i: (0, 0))
    return pl.pallas_call(
        grad_pair_kernel,
        grid=(n_dp,),
        in_specs=[block, full(b), block, full(d), hbm()],
        out_specs=pl.BlockSpec((depth, cols), lambda i: (i, at // cols)),
        out_shape=jax.ShapeDtypeStruct(kept.shape, BF),
        input_output_aliases={4: 0},
        compiler_params=params(),
        cost_estimate=cost(13),
    )(a, b, c, d, kept)


def split_kernel(turned, g_ref, *outs):
    at = 0
    for i, out in enumerate(outs):
        if i in turned:
            cols = out.shape[0]
            out[...] = g_ref[:, at : at + cols].astype(F32).T
        else:
            cols = out.shape[1]
            out[...] = g_ref[:, at : at + cols].astype(F32)
        at += cols


def split_call(widths, turned, g):
    rows = g.shape[0]
    return pl.pallas_call(
        functools.partial(split_kernel, turned),
        in_specs=[whole()],
        out_specs=[whole()] * len(widths),
        out_shape=[
            jax.ShapeDtypeStruct((w, rows) if i in turned else (rows, w), F32) for i, w in enumerate(widths)
        ],
        compiler_params=params(),
        cost_estimate=cost(5),
    )(g)


def input_kernel(first, flag_ref, x_ref, t_ref, r_ref, gm_ref, gain_ref, *rest):
    out_ref, gain_out = rest[-2:]
    gn = jnp.where(flag_ref[0] == 1, r_ref[...], t_ref[...]).astype(F32)
    x = x_ref[...].astype(F32)
    r1 = rms_r(x)
    h = gn * gain_ref[...]
    out_ref[...] = gm_ref[...] + r1 * h - x * (r1 * r1 * r1 * jnp.mean(h * x, axis=-1, keepdims=True))
    gain_sum = jnp.sum(gn * x * r1, axis=0, keepdims=True)
    gain_out[...] = gain_sum if first else rest[0][...] + gain_sum


def input_call(c, flag, x, t, r, gm, gain, kept):
    tok, d = x.shape
    own = pl.BlockSpec((CHUNK, d), lambda i: (0, 0))
    one = pl.BlockSpec((1, d), lambda i: (0, 0))
    first = kept is None
    return pl.pallas_call(
        functools.partial(input_kernel, first),
        grid=(1,),
        in_specs=[smem(), chunk_block(c, d), own, own, own, one] + ([] if first else [one, hbm()]),
        out_specs=[chunk_block(c, d), one],
        out_shape=[jax.ShapeDtypeStruct((tok, d), F32), jax.ShapeDtypeStruct((1, d), F32)],
        input_output_aliases={} if first else {7: 0},
        compiler_params=params(),
        cost_estimate=cost(5),
    )(flag, x, t, r, gm, gain, *([] if first else [kept[1], kept[0]]))


def output_kernel(aliased, flag_ref, mid_ref, t_ref, r_ref, *rest):
    out_ref = rest[-1]
    down = jnp.where(flag_ref[0] == 1, r_ref[...], t_ref[...]).astype(F32)
    out_ref[...] = (mid_ref[...] + down).astype(BF)


def output_call(c, flag, mid, t, r, kept, tok):
    d = mid.shape[1]
    own = pl.BlockSpec((CHUNK, d), lambda i: (0, 0))
    first = kept is None
    return pl.pallas_call(
        functools.partial(output_kernel, not first),
        grid=(1,),
        in_specs=[smem(), own, own, own] + ([] if first else [hbm()]),
        out_specs=chunk_block(c, d),
        out_shape=jax.ShapeDtypeStruct((tok, d), BF),
        input_output_aliases={} if first else {4: 0},
        compiler_params=params(),
        cost_estimate=cost(3),
    )(flag, mid, t, r, *([] if first else [kept]))


def line_sum(line, x):
    n = lax.axis_size("mp")
    me = lax.axis_index("mp")
    half = n // 2
    for h in range(half - 1):
        r = lax.ppermute(x, "mp", [(h, h + 1), (n - 1 - h, n - 2 - h)])
        yield
        x = line(jnp.add, x, r)
    r = lax.ppermute(x, "mp", [(half - 1, half), (half, half - 1)])
    yield
    x = line(jnp.add, x, r)
    r = x
    for h in reversed(range(half - 1)):
        r = lax.ppermute(x, "mp", [(h + 1, h), (n - 2 - h, n - 1 - h)])
        if h:
            yield
            x = line(jnp.where, (me == h) | (me == n - 1 - h), r, x)
    return x, r


class Sum:
    def __init__(self, line, *args, kind=line_sum):
        self.steps = kind(line, *args)
        self.result = None
        self.step()

    def step(self):
        try:
            if self.result is None:
                next(self.steps)
        except StopIteration as done:
            self.result = done.value

    def total(self):
        while self.result is None:
            self.step()
        return self.result


class Stream:
    def __init__(self, line):
        self.line = line
        self.four = lax.axis_size("mp") == 4
        me = lax.axis_index("mp")
        self.end = (me == 0) | (me == 3)
        self.parts, self.sent, self.got, self.sums = [], [], [], {}

    def push(self, part=None):
        i = len(self.parts)
        self.parts.append(part)
        if not self.four:
            if part is not None:
                self.sums[i] = Sum(self.line, part).total()
            return i
        pairs = [(1, 0), (2, 3)] + ([] if part is None else [(0, 1), (3, 2)])
        if part is None:
            part = self.line(jnp.add, *self.sums[i - 2])
        elif i > 1:
            part = self.line(lambda end, p, a, b: jnp.where(end, p, a + b), self.end, part, *self.sums[i - 2])
        self.sent.append(part)
        self.got.append(lax.ppermute(part, "mp", pairs))
        return i

    def middle(self, i):
        if self.four:
            both = self.line(jnp.add, self.parts[i], self.got[i])
            self.sums[i] = both, lax.ppermute(both, "mp", [(1, 2), (2, 1)])

    def total(self, i):
        return (self.sent[i + 2], self.got[i + 2]) if self.four else self.sums[i]


class Line:
    def __init__(self):
        self.last = None

    def after(self, *args):
        if self.last is None:
            return args
        leaves, tree = jax.tree.flatten(args)
        leaves = lax.optimization_barrier((*leaves, self.last))[:-1]
        return jax.tree.unflatten(tree, leaves)

    def __call__(self, f, *args, **kw):
        out = f(*self.after(*args), **kw)
        self.last = jax.tree.leaves(out)[-1]
        return out


SWAP = [(0, 1), (1, 0)]
DP = ("chip", "core")


def behind(x, arrays):
    return lax.optimization_barrier((x, jax.tree.leaves(arrays)))[0]


class Gather:
    def __init__(self, x, low_first):
        self.n = lax.axis_size("chip")
        bits = [1 << b for b in range(self.n.bit_length() - 1)]
        self.bits = bits if low_first else bits[::-1]
        self.own = {0: x}
        self.swapped = {0: lax.ppermute(x, "core", SWAP)}
        self.level = 0

    def step(self):
        bit = self.bits[self.level]
        self.level += 1
        new = {
            r ^ bit: lax.ppermute(b, "chip", [(i, i ^ bit) for i in range(self.n)]) for r, b in self.own.items()
        }
        self.own |= new
        return list(new.values())

    def swap(self):
        for r, b in self.own.items():
            if r not in self.swapped:
                self.swapped[r] = lax.ppermute(b, "core", SWAP)

    def blocks(self):
        while self.level < len(self.bits):
            self.step()
        self.swap()
        return [b[r] for r in range(self.n) for b in (self.own, self.swapped)]


def in_order(stacked, index):
    n = stacked.shape[0]
    bit = 1
    while bit < n:
        parts = stacked.reshape(n // (2 * bit), 2, bit, *stacked.shape[1:])
        stacked = jnp.where(index & bit, parts[:, ::-1], parts).reshape(stacked.shape)
        bit *= 2
    return stacked


def swap_sum(line, x, axis):
    n = lax.axis_size(axis)
    step = 1
    while step < n:
        got = lax.ppermute(x, axis, [(i, i ^ step) for i in range(n)])
        yield
        x = line(jnp.add, x, got)
        step *= 2
    return x


def own_sum(line, rows, index):
    rows = in_order(rows, index)
    half = rows.shape[0] // 2
    while half:
        if half > 1:
            pairs = [(i, i ^ (half // 2)) for i in range(lax.axis_size("chip"))]
            got = lax.ppermute(rows[half:], "chip", pairs)
        else:
            got = lax.ppermute(rows[half:], "core", SWAP)
        yield
        rows = line(jnp.add, rows[:half], got)
        half //= 2
    return rows[0]


def on_device(
    hidden_in,
    cotangent,
    doc_lengths,
    w_query,
    w_key,
    w_value,
    w_out,
    w_gate,
    w_up,
    w_down,
    norm_attn,
    norm_mlp,
    norm_query,
    norm_key,
):
    chips = lax.axis_size("chip")
    n_dp = 2 * chips
    core_id = lax.axis_index("core")
    dp = 2 * lax.axis_index("chip") + core_id
    mp = lax.axis_index("mp")
    n_mp = lax.axis_size("mp")
    tok, d = hidden_in.shape
    nq = w_query.shape[1] // HD
    nk = w_key.shape[1] // HD
    depth = w_query.shape[0]
    small = norm_query.shape[0]
    flag = jnp.stack([((mp == 0) | (mp == n_mp - 1)).astype(jnp.int32), dp])

    wide = (2 * nq + 2 * nk) * HD
    widen = lambda v: jnp.pad(v, (0, wide - v.shape[0]))[None]
    placed = lambda v: widen(lax.dynamic_update_slice(jnp.zeros(HD, BF), v, (dp * small,)))
    gain_rows = jnp.concatenate([widen(norm_attn), widen(norm_mlp), placed(norm_query), placed(norm_key)])
    gain_rows = jnp.pad(gain_rows, ((0, 12), (0, 0)))
    w_attn = pack_call([w_query, w_key, w_value, w_out], gain_rows)
    halves = [Gather(w_attn[:, : wide // 2], True), Gather(w_attn[:, wide // 2 :], False)]
    while halves[0].level < len(halves[0].bits):
        arrived = [h.step() for h in halves]
    w_mlp = behind(pack_call([w_gate, w_up, w_down]), arrived)
    w_mlp = lax.all_gather(w_mlp, DP, axis=0)

    lengths = lax.dynamic_index_in_dim(doc_lengths, dp, 0, keepdims=False)
    ends = jnp.cumsum(lengths)
    ends = ends.astype(jnp.int32)
    token = jnp.arange(tok, dtype=jnp.int32)
    begin = jnp.max(jnp.where(token[:, None] >= ends[None, :], ends[None, :], 0), axis=1)
    position = token - begin
    inverse = ROPE_BASE ** (-(2.0 * jnp.arange(HD // 2, dtype=F32)) / HD)
    angles = position.astype(F32)[:, None] * inverse[None, :]
    cosine = jnp.cos(angles)
    sine = jnp.sin(angles)
    cosine = jnp.concatenate([cosine, cosine], axis=1)
    sine = jnp.concatenate([-sine, sine], axis=1)

    line = Line()

    normed, lin, rot, gain_attn, gain_mlp, gain_query, gain_key, w_attn = line(
        functools.partial(qkv_call, nq=nq, nk=nk), flag, hidden_in, cosine, sine, [h.blocks() for h in halves]
    )

    order = list(reversed(range(tok // CHUNK)))
    att = None
    lse, branch, mid, down, gnt, gn = {}, {}, {}, {}, {}, {}
    stream = Stream(line)
    for k, c in enumerate(order):
        att, lse[c], part = line(functools.partial(attn_call, c, nq=nq, nk=nk), ends, rot, w_attn, att)
        branch[c] = stream.push(part) if k < 2 else part

    c0, c1, c2, c3 = order
    state = {"mlp": None, "back": None, "carry": None, "input": None, "output": None}
    gm = {}
    ff = w_gate.shape[1]

    def run_mlp(c):
        t, r = stream.total(branch[c])
        mid[c], state["mlp"], down[c], gnt_part = line(
            functools.partial(mlp_call, c), flag, hidden_in, t, r, cotangent, gain_mlp,
            w_mlp, state["mlp"],
        )
        gnt[c] = gnt_part

    def run_back(c):
        t, r = stream.total(gnt[c])
        gm[c], state["back"], part, state["carry"] = line(
            functools.partial(back_call, c, nq=nq, nk=nk), flag, ends, mid[c], t, r, cotangent,
            gain_mlp, rot, lse[c], lin, cosine, sine, gain_query, gain_key, w_attn,
            state["back"], state["carry"],
        )
        gn[c] = part

    def run_input(c):
        t, r = stream.total(gn[c])
        state["input"] = line(
            functools.partial(input_call, c), flag, hidden_in, t, r, gm[c], gain_attn, state["input"]
        )

    def run_output(c):
        t, r = stream.total(down[c])
        state["output"] = line(functools.partial(output_call, c, tok=tok), flag, mid[c], t, r, state["output"])

    def push(of, c):
        of[c] = stream.push(line.after(of[c])[0])

    def grad(total, at, a, b, kept=None):
        return line(functools.partial(grad_call, n_dp, total, at), a, b, kept)

    def scatter(g):
        return lax.psum_scatter(line.after(g)[0], DP, scatter_dimension=0, tiled=True)

    stream.middle(branch[c0])
    stream.middle(branch[c1])
    push(branch, c2)
    push(branch, c3)
    stream.middle(branch[c2])
    run_mlp(c0)
    stream.middle(branch[c3])
    push(gnt, c0)
    run_mlp(c1)
    push(gnt, c1)
    stream.middle(gnt[c0])
    run_mlp(c2)
    stream.middle(gnt[c1])
    push(gnt, c2)
    run_mlp(c3)
    n2, prod, gg, gu = state["mlp"]
    push(gnt, c3)
    stream.middle(gnt[c2])
    run_back(c0)
    g_mlp = grad(3 * ff + wide, 0, n2, gg)
    stream.middle(gnt[c3])
    push(gn, c0)
    run_back(c1)
    g_mlp = grad(3 * ff + wide, ff, n2, gu, g_mlp)
    push(down, c0)
    stream.middle(gn[c0])
    run_back(c2)
    g_mlp = grad(3 * ff + wide, 2 * ff, cotangent, prod, g_mlp)
    push(gn, c1)
    stream.middle(down[c0])
    run_back(c3)
    gb, gqkv = state["back"]
    grads = line(functools.partial(grad_pair_call, n_dp, 3 * ff), normed, gqkv, gb, att, g_mlp)
    push(gn, c2)
    stream.middle(gn[c1])
    grads = scatter(grads)
    run_input(c0)
    push(gn, c3)
    stream.middle(gn[c2])
    run_output(c0)
    push(down, c1)
    stream.middle(gn[c3])
    run_input(c1)
    _, sum_mlp, sum_head = state["carry"]
    heads = Sum(line, sum_head, "mp", kind=swap_sum)
    push(down, c2)
    stream.middle(down[c1])
    run_input(c2)
    heads.step()
    push(down, c3)
    stream.middle(down[c2])
    run_input(c3)
    grad_input, sum_attn = state["input"]
    heads = heads.total()
    sums = jnp.concatenate(
        [sum_attn.reshape(n_dp, depth), sum_mlp.reshape(n_dp, depth)]
        + [heads[i].reshape(n_dp, small) for i in range(2)],
        axis=1,
    )
    sums = Sum(line, sums, dp, kind=own_sum)
    stream.push()
    stream.middle(down[c3])
    sums.step()
    run_output(c1)
    sums.step()
    stream.push()
    run_output(c2)
    sums = sums.total()
    widths = (ff, ff, ff, nq * HD, nk * HD, nk * HD, nq * HD)
    outs = line(functools.partial(split_call, widths, (2, 6)), grads)
    run_output(c3)

    return (
        state["output"],
        grad_input,
        *outs[3:6],
        outs[6],
        outs[0],
        outs[1],
        outs[2],
        sums[:depth],
        sums[depth : 2 * depth],
        sums[2 * depth : 2 * depth + small],
        sums[2 * depth + small :],
    )


def solution(mesh):
    n_dp, n_mp = mesh.devices.shape
    mesh = jax.sharding.Mesh(mesh.devices.reshape(n_dp // 2, 2, n_mp), ("chip", "core", "mp"))
    rows = P(DP, None)
    weight = P(DP, "mp")
    turned = P("mp", DP)
    gain = P(DP)
    return jax.shard_map(
        on_device,
        mesh=mesh,
        in_specs=(rows, rows, P(), weight, weight, weight, turned, weight, weight, turned, gain, gain, gain, gain),
        out_specs=(rows, rows, weight, weight, weight, turned, weight, weight, turned, gain, gain, gain, gain),
        check_vma=False,
    )
```

```python
import functools

import jax
import jax.numpy as jnp
from jax import lax
from jax.experimental import pallas as pl
from jax.experimental.pallas import tpu as pltpu
from jax.sharding import PartitionSpec as P

HD = 128
CHUNK = 256
EPSILON = 1e-06
ROPE_BASE = 1000000.0
SCALE = HD ** (-0.5)
BF = jnp.bfloat16
F32 = jnp.float32
VMEM_LIMIT = 56 * 1024 * 1024

NN = (((1,), (0,)), ((), ()))
NT = (((1,), (1,)), ((), ()))
TN = (((0,), (0,)), ((), ()))


def dot(a, b, dims=NN):
    return lax.dot_general(a, b, dims, preferred_element_type=F32)


def whole():
    return pl.BlockSpec(memory_space=pltpu.VMEM)


def smem():
    return pl.BlockSpec(memory_space=pltpu.SMEM)


def hbm():
    return pl.BlockSpec(memory_space=pl.ANY)


def params(**kw):
    return pltpu.CompilerParams(vmem_limit_bytes=VMEM_LIMIT, **kw)


def cost(us):
    return pl.CostEstimate(flops=0, bytes_accessed=3690000 * us, transcendentals=0)


def rms_r(values):
    return lax.rsqrt(jnp.mean(values * values, axis=-1, keepdims=True) + EPSILON)


def fetch(gathered, dest, sem, first):
    depth, cols = dest.shape[1:]
    return pltpu.make_async_copy(gathered.at[:, pl.ds(0, depth), pl.ds(first, cols)], dest, sem)


def start(copies):
    for copy in copies:
        copy.start()


def wait(copies):
    for copy in copies:
        copy.wait()


def joined(ref):
    a, b, n = ref.shape
    return ref[...].reshape(a * b, n)


def pack_kernel(n_rows, *refs):
    out_ref = refs[-1]
    weights = refs[: len(refs) - 1 - n_rows]
    depth = weights[0].shape[0]
    at = 0
    for ref in weights[:-1]:
        out_ref[:depth, at : at + ref.shape[1]] = ref[...]
        at += ref.shape[1]
    out_ref[:depth, at:] = weights[-1][...].astype(F32).T.astype(BF)
    if n_rows:
        out_ref[depth:, :] = refs[-2][...]


def pack_call(weights, rows=None):
    depth = weights[0].shape[0]
    cols = sum(w.shape[1] for w in weights[:-1]) + weights[-1].shape[0]
    extra = [] if rows is None else [rows]
    return pl.pallas_call(
        functools.partial(pack_kernel, len(extra)),
        in_specs=[whole()] * (len(weights) + len(extra)),
        out_specs=whole(),
        out_shape=jax.ShapeDtypeStruct((depth + (0 if rows is None else rows.shape[0]), cols), BF),
        compiler_params=params(),
        cost_estimate=cost(3),
    )(*weights, *extra)


def qkv_kernel(nq, nk, halves, flag_ref, x_ref, cos_ref, sin_ref, *rest):
    normed_ref, lin_ref, rot_ref, ga_ref, gm_ref, gq_ref, gk_ref, w_out, w, gains, sems, out_sem = rest[-12:]
    step = pl.program_id(0)
    n_dp, depth, half = w.shape[0], w.shape[1], w.shape[2] // halves
    save = pltpu.make_async_copy(w, w_out, out_sem)

    @pl.when(step == 0)
    def _():
        rows, copies = [], []
        for i in range(halves):
            for n in range(n_dp):
                block, place = rest[i * n_dp + n], flag_ref[1] ^ n
                cols = pl.ds(i * half, half)
                copies.append(
                    pltpu.make_async_copy(block.at[pl.ds(0, depth)], w.at[place, :, cols], sems.at[i, n])
                )
                if i == 0:
                    rows.append(pltpu.make_async_copy(block.at[pl.ds(depth, 16)], gains.at[place], sems.at[halves, n]))
        start(rows + copies)
        wait(rows)
        of_q = jnp.zeros((1, HD), F32)
        of_k = jnp.zeros((1, HD), F32)
        for p in range(n_dp):
            g = gains[p].astype(F32)
            ga_ref[:, p * depth : (p + 1) * depth] = g[0:1, :depth]
            gm_ref[:, p * depth : (p + 1) * depth] = g[1:2, :depth]
            of_q = of_q + g[2:3, :HD]
            of_k = of_k + g[3:4, :HD]
        gq_ref[...] = of_q
        gk_ref[...] = of_k
        wait(copies)
        save.start()

    x = x_ref[...].astype(F32)
    normed = (x * rms_r(x) * ga_ref[...]).astype(BF)
    normed_ref[...] = normed
    acc = dot(normed, w[:, :, : rot_ref.shape[1]].reshape(n_dp * depth, rot_ref.shape[1]))
    cosine = cos_ref[...]
    sine = sin_ref[...]
    for h in range(nq + nk):
        v = acc[:, h * HD : (h + 1) * HD]
        gain = gq_ref[...] if h < nq else gk_ref[...]
        n = v * rms_r(v) * gain
        rot_ref[:, h * HD : (h + 1) * HD] = (n * cosine + pltpu.roll(n, HD // 2, 1) * sine).astype(BF)
    lin_ref[...] = acc[:, : (nq + nk) * HD]
    rot_ref[:, (nq + nk) * HD :] = acc[:, (nq + nk) * HD :].astype(BF)

    @pl.when(step == pl.num_programs(0) - 1)
    def _():
        save.wait()


def qkv_call(flag, x, cosine, sine, halves, nq, nk):
    tok, d = x.shape
    n_dp = len(halves[0])
    wide = len(halves) * halves[0][0].shape[1]
    cols = (nq + 2 * nk) * HD
    blk = lambda n: pl.BlockSpec((CHUNK, n), lambda i: (i, 0))
    one = lambda n: pl.BlockSpec((1, n), lambda i: (0, 0))
    lin = (nq + nk) * HD
    return pl.pallas_call(
        functools.partial(qkv_kernel, nq, nk, len(halves)),
        grid=(tok // CHUNK,),
        in_specs=[smem(), blk(d), blk(HD), blk(HD)] + [hbm()] * (len(halves) * n_dp),
        out_specs=[blk(d), blk(lin), blk(cols), one(d), one(d), one(HD), one(HD), hbm()],
        out_shape=[
            jax.ShapeDtypeStruct((tok, d), BF),
            jax.ShapeDtypeStruct((tok, lin), F32),
            jax.ShapeDtypeStruct((tok, cols), BF),
            jax.ShapeDtypeStruct((1, d), F32),
            jax.ShapeDtypeStruct((1, d), F32),
            jax.ShapeDtypeStruct((1, HD), F32),
            jax.ShapeDtypeStruct((1, HD), F32),
            jax.ShapeDtypeStruct((n_dp, d // n_dp, wide), BF),
        ],
        scratch_shapes=[
            pltpu.VMEM((n_dp, d // n_dp, wide), BF),
            pltpu.VMEM((n_dp, 16, wide // len(halves)), BF),
            pltpu.SemaphoreType.DMA((len(halves) + 1, n_dp)),
            pltpu.SemaphoreType.DMA,
        ],
        compiler_params=params(),
        cost_estimate=cost(14),
    )(flag, x, cosine, sine, *[b for h in halves for b in h])


def band(c):
    lo = max(c - 1, 0) * CHUNK
    return lo, (c + 1) * CHUNK - lo


def doc_start(ends_ref, token):
    first = jnp.zeros_like(token)
    for j in range(ends_ref.shape[0]):
        first = jnp.maximum(first, jnp.where(token >= ends_ref[j], ends_ref[j], 0))
    return first


def allowed(c, ends_ref):
    lo, width = band(c)
    t = lax.broadcasted_iota(jnp.int32, (CHUNK, 1), 0) + c * CHUNK
    u = lax.broadcasted_iota(jnp.int32, (CHUNK, width), 1) + lo
    return (u <= t) & (u >= doc_start(ends_ref, t))


def attn_kernel(c, nq, nk, ends_ref, rot_ref, w_hbm, *rest):
    att_ref, lse_ref, part_ref, w, sem = rest[-5:]
    copies = [fetch(w_hbm, w, sem, (nq + 2 * nk) * HD)]
    start(copies)
    lo, width = band(c)
    mask = allowed(c, ends_ref)
    group = nq // nk
    heads = []
    lses = []
    for h in range(nq):
        q = rot_ref[c * CHUNK : (c + 1) * CHUNK, h * HD : (h + 1) * HD]
        j = h // group
        k = rot_ref[lo : lo + width, (nq + j) * HD : (nq + j + 1) * HD]
        v = rot_ref[lo : lo + width, (nq + nk + j) * HD : (nq + nk + j + 1) * HD]
        s = jnp.where(mask, dot(q, k, NT) * SCALE, -1e30)
        m = jnp.max(s, axis=-1, keepdims=True)
        e = jnp.exp(s - m)
        l = jnp.sum(e, axis=-1, keepdims=True)
        heads.append(dot((e / l).astype(BF), v).astype(BF))
        lses.append(m + jnp.log(l))
    att = jnp.concatenate(heads, axis=1)
    att_ref[...] = att
    lse_ref[...] = jnp.concatenate(lses, axis=1)
    wait(copies)
    part_ref[...] = dot(att, joined(w), NT).astype(BF)


def chunk_block(c, n):
    return pl.BlockSpec((CHUNK, n), lambda i: (c, 0))


def attn_call(c, ends, rot, w, att, nq, nk):
    tok = rot.shape[0]
    n_dp, depth = w.shape[:2]
    d = n_dp * depth
    first = att is None
    full = lambda a: pl.BlockSpec(a.shape, lambda i: (0,) * a.ndim)
    return pl.pallas_call(
        functools.partial(attn_kernel, c, nq, nk),
        grid=(1,),
        in_specs=[smem(), full(rot)] + [hbm()] * (1 if first else 2),
        out_specs=[
            chunk_block(c, nq * HD),
            pl.BlockSpec((CHUNK, nq), lambda i: (0, 0)),
            pl.BlockSpec((CHUNK, d), lambda i: (0, 0)),
        ],
        out_shape=[
            jax.ShapeDtypeStruct((tok, nq * HD), BF),
            jax.ShapeDtypeStruct((CHUNK, nq), F32),
            jax.ShapeDtypeStruct((CHUNK, d), BF),
        ],
        scratch_shapes=[pltpu.VMEM((n_dp, depth, nq * HD), BF), pltpu.SemaphoreType.DMA],
        input_output_aliases={} if first else {3: 0},
        compiler_params=params(),
        cost_estimate=cost(5),
    )(ends, rot, w, *([] if first else [att]))


def mlp_kernel(c, tiles, flag_ref, x_hbm, t_hbm, r_hbm, cot_hbm, gain_ref, w_hbm, *rest):
    outs, rest = rest[-22:-15], rest[-15:]
    x_ref, t_ref, r_ref, cot_ref, mid_ref, n2_ref, prod_ref, gg_ref, gu_ref, down_ref, gnt_ref, acc_d, acc_g, w, sems = rest
    mid_out, n2_out, prod_out, gg_out, gu_out, down_out, gnt_out = outs
    tile = w.shape[4]
    rows = pl.ds(c * CHUNK, CHUNK)
    copy = pltpu.make_async_copy
    first = [copy(t_hbm, t_ref, sems.at[0]), copy(r_hbm, r_ref, sems.at[1]), copy(x_hbm.at[rows], x_ref, sems.at[2])]
    cot_copy = [copy(cot_hbm.at[rows], cot_ref, sems.at[3])]
    copies = [
        [[fetch(w_hbm, w.at[j % 2, i], sems.at[4 + 3 * (j % 2) + i], (i * tiles + j) * tile)] for i in range(3)]
        for j in range(tiles)
    ]
    saves = [copy(mid_ref, mid_out, sems.at[10]), copy(n2_ref, n2_out.at[rows], sems.at[11])]
    start(first + copies[0][0] + copies[0][1] + cot_copy + copies[0][2])
    for j in range(1, min(tiles, 2)):
        for i in range(3):
            start(copies[j][i])
    wait(first)
    branch = jnp.where(flag_ref[0] == 1, r_ref[...], t_ref[...]).astype(F32)
    mid = x_ref[...].astype(F32) + branch
    mid_ref[...] = mid
    n2_ref[...] = (mid * rms_r(mid) * gain_ref[...]).astype(BF)
    start(saves)
    for j in range(tiles):
        wg, wu, wd = (w.at[j % 2, i] for i in range(3))
        cols = pl.ds(j * tile, tile)
        wait(copies[j][0])
        g = dot(n2_ref[...], joined(wg))
        wait(copies[j][1])
        u = dot(n2_ref[...], joined(wu))
        if j == 0:
            wait(cot_copy)
        wait(copies[j][2])
        gp = dot(cot_ref[...], joined(wd))
        s = 1.0 / (1.0 + jnp.exp(-g))
        gs = g * s
        prod = (gs * u).astype(BF)
        gg = (gp * u * s * (1.0 + g * (1.0 - s))).astype(BF)
        gu = (gp * gs).astype(BF)
        prod_ref[:, j * tile : (j + 1) * tile] = prod
        gg_ref[:, j * tile : (j + 1) * tile] = gg
        gu_ref[:, j * tile : (j + 1) * tile] = gu
        now = [
            copy(ref.at[:, cols], out.at[rows, cols], sems.at[12 + 3 * j + i])
            for i, (ref, out) in enumerate(((prod_ref, prod_out), (gg_ref, gg_out), (gu_ref, gu_out)))
        ]
        start(now)
        saves += now
        gnt = dot(gg, joined(wg), NT) + dot(gu, joined(wu), NT)
        if j:
            gnt = gnt + acc_g[...]
        if j < tiles - 1:
            acc_g[...] = gnt
        else:
            gnt_ref[...] = gnt.astype(BF)
            now = [copy(gnt_ref, gnt_out, sems.at[12 + 3 * tiles])]
            start(now)
            saves += now
        down = dot(prod, joined(wd), NT)
        if j:
            down = down + acc_d[...]
        if j < tiles - 1:
            acc_d[...] = down
        else:
            down_ref[...] = down.astype(BF)
            now = [copy(down_ref, down_out, sems.at[13 + 3 * tiles])]
            start(now)
            saves += now
        if j + 2 < tiles:
            for i in range(3):
                start(copies[j + 2][i])
    wait(saves)


MLP_TILES = 3


def mlp_call(c, flag, x, t, r, cot, gain, w, kept):
    tok, d = x.shape
    n_dp, depth, ff = w.shape[0], w.shape[1], w.shape[2] // 3
    tiles = MLP_TILES
    first = kept is None
    n_alias = 0 if first else 4
    chunk = lambda n, kind: pltpu.VMEM((CHUNK, n), kind)
    out = pl.pallas_call(
        functools.partial(mlp_kernel, c, tiles),
        in_specs=[smem(), hbm(), hbm(), hbm(), hbm(), whole(), hbm()] + [hbm()] * n_alias,
        out_specs=[hbm()] * 7,
        out_shape=[
            jax.ShapeDtypeStruct((CHUNK, d), F32),
            jax.ShapeDtypeStruct((tok, d), BF),
            jax.ShapeDtypeStruct((tok, ff), BF),
            jax.ShapeDtypeStruct((tok, ff), BF),
            jax.ShapeDtypeStruct((tok, ff), BF),
            jax.ShapeDtypeStruct((CHUNK, d), BF),
            jax.ShapeDtypeStruct((CHUNK, d), BF),
        ],
        scratch_shapes=[chunk(d, BF)] * 4
        + [chunk(d, F32), chunk(d, BF)]
        + [chunk(ff, BF)] * 3
        + [chunk(d, BF)] * 2
        + [chunk(d, F32)] * 2
        + [pltpu.VMEM((2, 3, n_dp, depth, ff // tiles), BF), pltpu.SemaphoreType.DMA((14 + 3 * tiles,))],
        input_output_aliases={} if first else {7: 1, 8: 2, 9: 3, 10: 4},
        compiler_params=params(),
        cost_estimate=cost(19),
    )(flag, x, t, r, cot, gain, w, *([] if first else kept))
    return out[0], out[1:5], out[5], out[6]


def back_kernel(
    c, nq, nk, first, flag_ref, ends_ref, mid_ref, t_ref, r_ref, cot_ref, gain_ref, rot_hbm,
    lse_ref, lin_hbm, cos_ref, sin_ref, gq_ref, gk_ref, w_hbm, *rest,
):
    gm_out, gb_out, gqkv_ref, part_ref, gain_out, head_out, carry_out = rest[-16:-9]
    gm_ref, gb_ref, rot_ref, lin_ref, wo, w, sems, late_sems, save_sems = rest[-9:]
    lo, width = band(c)
    rows = pl.ds(c * CHUNK, CHUNK)
    late = [
        pltpu.make_async_copy(rot_hbm.at[pl.ds(lo, width)], rot_ref, late_sems.at[0]),
        pltpu.make_async_copy(lin_hbm.at[rows], lin_ref, late_sems.at[1]),
    ]
    saves = [
        pltpu.make_async_copy(gm_ref, gm_out, save_sems.at[0]),
        pltpu.make_async_copy(gb_ref, gb_out.at[rows], save_sems.at[1]),
    ]
    if not first:
        carry_ref, gain_in, head_in = rest[:3]
    out_copies = [fetch(w_hbm, wo, sems.at[0], (nq + 2 * nk) * HD)]
    in_copies = [fetch(w_hbm, w, sems.at[1], 0)]
    start(out_copies + late + in_copies)
    gnt = jnp.where(flag_ref[0] == 1, r_ref[...], t_ref[...]).astype(F32)
    mid = mid_ref[...]
    r2 = rms_r(mid)
    h = gnt * gain_ref[...]
    gm = (
        cot_ref[...].astype(F32)
        + r2 * h
        - mid * (r2 * r2 * r2 * jnp.mean(h * mid, axis=-1, keepdims=True))
    )
    gain_sum = jnp.sum(gnt * mid * r2, axis=0, keepdims=True)
    gain_out[...] = gain_sum if first else gain_in[...] + gain_sum
    gm_ref[...] = gm
    gb = gm.astype(BF)
    gb_ref[...] = gb
    start(saves)
    wait(out_copies)
    ga = dot(gb, joined(wo)).astype(BF)
    wait(late)
    mask = allowed(c, ends_ref)
    group = nq // nk
    cosine = cos_ref[...]
    sine = -sin_ref[...]

    def unrope(grad, lin, gain):
        gr = grad * cosine + pltpu.roll(grad, HD // 2, 1) * sine
        rr = rms_r(lin)
        hh = gr * gain
        out = rr * hh - lin * (rr * rr * rr * jnp.mean(hh * lin, axis=-1, keepdims=True))
        return out.astype(BF), jnp.sum(gr * lin * rr, axis=0, keepdims=True)

    sum_q = jnp.zeros((1, HD), F32) if first else head_in[0:1, :]
    sum_k = jnp.zeros((1, HD), F32) if first else head_in[1:2, :]
    outs = [None] * (nq + 2 * nk)
    for j in range(nk):
        k = rot_ref[:, (nq + j) * HD : (nq + j + 1) * HD]
        v = rot_ref[:, (nq + nk + j) * HD : (nq + nk + j + 1) * HD]
        dk = jnp.zeros((width, HD), F32)
        dv = jnp.zeros((width, HD), F32)
        for g in range(group):
            i = j * group + g
            q = rot_ref[width - CHUNK :, i * HD : (i + 1) * HD]
            gah = ga[:, i * HD : (i + 1) * HD]
            s = jnp.where(mask, dot(q, k, NT) * SCALE, -1e30)
            p = jnp.exp(s - lse_ref[:, i : i + 1])
            gw = dot(gah, v, NT)
            delta = jnp.sum(p * gw, axis=-1, keepdims=True)
            gs = (p * (gw - delta)).astype(BF)
            dq = (dot(gs, k) * SCALE).astype(BF).astype(F32)
            dk = dk + dot(gs, q, TN)
            dv = dv + dot(p.astype(BF), gah, TN)
            outs[i], part = unrope(dq, lin_ref[:, i * HD : (i + 1) * HD], gq_ref[...])
            sum_q = sum_q + part
        dk_own, dv_own = dk[width - CHUNK :], dv[width - CHUNK :]
        if not first:
            dk_own = dk_own + carry_ref[:, j * HD : (j + 1) * HD]
            dv_own = dv_own + carry_ref[:, (nk + j) * HD : (nk + j + 1) * HD]
        carry_out[:, j * HD : (j + 1) * HD] = dk[:CHUNK]
        carry_out[:, (nk + j) * HD : (nk + j + 1) * HD] = dv[:CHUNK]
        dk_own = (dk_own * SCALE).astype(BF).astype(F32)
        outs[nq + j], part = unrope(dk_own, lin_ref[:, (nq + j) * HD : (nq + j + 1) * HD], gk_ref[...])
        sum_k = sum_k + part
        outs[nq + nk + j] = dv_own.astype(BF)
    gqkv = jnp.concatenate(outs, axis=1)
    gqkv_ref[...] = gqkv
    head_out[0:1, :] = sum_q
    head_out[1:2, :] = sum_k
    wait(in_copies)
    part_ref[...] = dot(gqkv, joined(w), NT).astype(BF)
    wait(saves)


def back_call(
    c, flag, ends, mid, t, r, cot, gain, rot, lse, lin, cosine, sine, gq, gk, w, kept, carry, nq, nk
):
    tok, d = cot.shape
    first = carry is None
    full = lambda a: pl.BlockSpec(a.shape, lambda i: (0,) * a.ndim)
    args = [flag, ends, mid, t, r, cot, gain, rot, lse, lin, cosine, sine, gq, gk]
    specs = [smem(), smem()] + [full(a) for a in args[2:]]
    specs[5] = chunk_block(c, d)
    specs[7] = hbm()
    specs[9] = hbm()
    specs[10] = chunk_block(c, HD)
    specs[11] = chunk_block(c, HD)
    args.append(w)
    specs.append(hbm())
    if not first:
        args += [*carry, *kept]
        specs += [full(a) for a in carry] + [hbm(), hbm()]
    own = lambda n: pl.BlockSpec((CHUNK, n), lambda i: (0, 0))
    cols = (nq + 2 * nk) * HD
    n_dp = w.shape[0]
    depth = d // n_dp
    out = pl.pallas_call(
        functools.partial(back_kernel, c, nq, nk, first),
        grid=(1,),
        in_specs=specs,
        out_specs=[
            hbm(),
            hbm(),
            chunk_block(c, cols),
            own(d),
            pl.BlockSpec((1, d), lambda i: (0, 0)),
            pl.BlockSpec((2, HD), lambda i: (0, 0)),
            own(2 * nk * HD),
        ],
        out_shape=[
            jax.ShapeDtypeStruct((CHUNK, d), F32),
            jax.ShapeDtypeStruct((tok, d), BF),
            jax.ShapeDtypeStruct((tok, cols), BF),
            jax.ShapeDtypeStruct((CHUNK, d), BF),
            jax.ShapeDtypeStruct((1, d), F32),
            jax.ShapeDtypeStruct((2, HD), F32),
            jax.ShapeDtypeStruct((CHUNK, 2 * nk * HD), F32),
        ],
        scratch_shapes=[
            pltpu.VMEM((CHUNK, d), F32),
            pltpu.VMEM((CHUNK, d), BF),
            pltpu.VMEM((band(c)[1], cols), BF),
            pltpu.VMEM((CHUNK, lin.shape[1]), F32),
            pltpu.VMEM((n_dp, depth, nq * HD), BF),
            pltpu.VMEM((n_dp, depth, cols), BF),
            pltpu.SemaphoreType.DMA((2,)),
            pltpu.SemaphoreType.DMA((2,)),
            pltpu.SemaphoreType.DMA((2,)),
        ],
        input_output_aliases={} if first else {18: 1, 19: 2},
        compiler_params=params(),
        cost_estimate=cost(12),
    )(*args)
    return out[0], out[1:3], out[3], (out[6], out[4], out[5])


def grad_kernel(a_ref, b_ref, *rest):
    rest[-1][...] = dot(a_ref[...], b_ref[...], TN).astype(BF)


def grad_call(n_dp, total, at, a, b, kept):
    tok, d = a.shape
    depth = 2 * d // n_dp
    cols = b.shape[1]
    first = kept is None
    return pl.pallas_call(
        grad_kernel,
        grid=(n_dp // 2,),
        in_specs=[pl.BlockSpec((tok, depth), lambda i: (0, i)), pl.BlockSpec(b.shape, lambda i: (0, 0))]
        + ([] if first else [hbm()]),
        out_specs=pl.BlockSpec((depth, cols), lambda i: (i, at // cols)),
        out_shape=jax.ShapeDtypeStruct((d, total), BF),
        input_output_aliases={} if first else {2: 0},
        compiler_params=params(),
        cost_estimate=cost(2 + cols // 185),
    )(a, b, *([] if first else [kept]))


def grad_pair_kernel(a_ref, b_ref, c_ref, d_ref, kept_ref, out_ref):
    cols = b_ref.shape[1]
    out_ref[:, :cols] = dot(a_ref[...], b_ref[...], TN).astype(BF)
    out_ref[:, cols:] = dot(c_ref[...], d_ref[...], TN).astype(BF)


def grad_pair_call(n_dp, at, a, b, c, d, kept):
    tok, rows = a.shape
    depth = 2 * rows // n_dp
    cols = b.shape[1] + d.shape[1]
    block = pl.BlockSpec((tok, depth), lambda i: (0, i))
    full = lambda x: pl.BlockSpec(x.shape, lambda i: (0, 0))
    return pl.pallas_call(
        grad_pair_kernel,
        grid=(n_dp // 2,),
        in_specs=[block, full(b), block, full(d), hbm()],
        out_specs=pl.BlockSpec((depth, cols), lambda i: (i, at // cols)),
        out_shape=jax.ShapeDtypeStruct(kept.shape, BF),
        input_output_aliases={4: 0},
        compiler_params=params(),
        cost_estimate=cost(13),
    )(a, b, c, d, kept)


def split_kernel(turned, g_ref, *outs):
    at = 0
    for i, out in enumerate(outs):
        if i in turned:
            cols = out.shape[0]
            out[...] = g_ref[:, at : at + cols].astype(F32).T
        else:
            cols = out.shape[1]
            out[...] = g_ref[:, at : at + cols].astype(F32)
        at += cols


def split_call(widths, turned, g):
    rows = g.shape[0]
    return pl.pallas_call(
        functools.partial(split_kernel, turned),
        in_specs=[whole()],
        out_specs=[whole()] * len(widths),
        out_shape=[
            jax.ShapeDtypeStruct((w, rows) if i in turned else (rows, w), F32) for i, w in enumerate(widths)
        ],
        compiler_params=params(),
        cost_estimate=cost(5),
    )(g)


def input_kernel(first, flag_ref, x_ref, t_ref, r_ref, gm_ref, gain_ref, *rest):
    out_ref, gain_out = rest[-2:]
    gn = jnp.where(flag_ref[0] == 1, r_ref[...], t_ref[...]).astype(F32)
    x = x_ref[...].astype(F32)
    r1 = rms_r(x)
    h = gn * gain_ref[...]
    out_ref[...] = gm_ref[...] + r1 * h - x * (r1 * r1 * r1 * jnp.mean(h * x, axis=-1, keepdims=True))
    gain_sum = jnp.sum(gn * x * r1, axis=0, keepdims=True)
    gain_out[...] = gain_sum if first else rest[0][...] + gain_sum


def input_call(c, flag, x, t, r, gm, gain, kept):
    tok, d = x.shape
    own = pl.BlockSpec((CHUNK, d), lambda i: (0, 0))
    one = pl.BlockSpec((1, d), lambda i: (0, 0))
    first = kept is None
    return pl.pallas_call(
        functools.partial(input_kernel, first),
        grid=(1,),
        in_specs=[smem(), chunk_block(c, d), own, own, own, one] + ([] if first else [one, hbm()]),
        out_specs=[chunk_block(c, d), one],
        out_shape=[jax.ShapeDtypeStruct((tok, d), F32), jax.ShapeDtypeStruct((1, d), F32)],
        input_output_aliases={} if first else {7: 0},
        compiler_params=params(),
        cost_estimate=cost(5),
    )(flag, x, t, r, gm, gain, *([] if first else [kept[1], kept[0]]))


def output_kernel(aliased, flag_ref, mid_ref, t_ref, r_ref, *rest):
    out_ref = rest[-1]
    down = jnp.where(flag_ref[0] == 1, r_ref[...], t_ref[...]).astype(F32)
    out_ref[...] = (mid_ref[...] + down).astype(BF)


def output_call(c, flag, mid, t, r, kept, tok):
    d = mid.shape[1]
    own = pl.BlockSpec((CHUNK, d), lambda i: (0, 0))
    first = kept is None
    return pl.pallas_call(
        functools.partial(output_kernel, not first),
        grid=(1,),
        in_specs=[smem(), own, own, own] + ([] if first else [hbm()]),
        out_specs=chunk_block(c, d),
        out_shape=jax.ShapeDtypeStruct((tok, d), BF),
        input_output_aliases={} if first else {4: 0},
        compiler_params=params(),
        cost_estimate=cost(3),
    )(flag, mid, t, r, *([] if first else [kept]))


def line_sum(line, x):
    n = lax.axis_size("mp")
    me = lax.axis_index("mp")
    half = n // 2
    for h in range(half - 1):
        r = lax.ppermute(x, "mp", [(h, h + 1), (n - 1 - h, n - 2 - h)])
        yield
        x = line(jnp.add, x, r)
    r = lax.ppermute(x, "mp", [(half - 1, half), (half, half - 1)])
    yield
    x = line(jnp.add, x, r)
    r = x
    for h in reversed(range(half - 1)):
        r = lax.ppermute(x, "mp", [(h + 1, h), (n - 2 - h, n - 1 - h)])
        if h:
            yield
            x = line(jnp.where, (me == h) | (me == n - 1 - h), r, x)
    return x, r


class Sum:
    def __init__(self, line, *args, kind=line_sum):
        self.steps = kind(line, *args)
        self.result = None
        self.step()

    def step(self):
        try:
            if self.result is None:
                next(self.steps)
        except StopIteration as done:
            self.result = done.value

    def total(self):
        while self.result is None:
            self.step()
        return self.result


class Stream:
    def __init__(self, line):
        self.line = line
        self.four = lax.axis_size("mp") == 4
        me = lax.axis_index("mp")
        self.end = (me == 0) | (me == 3)
        self.parts, self.sent, self.got, self.sums = [], [], [], {}

    def push(self, part=None):
        i = len(self.parts)
        self.parts.append(part)
        if not self.four:
            if part is not None:
                self.sums[i] = Sum(self.line, part).total()
            return i
        pairs = [(1, 0), (2, 3)] + ([] if part is None else [(0, 1), (3, 2)])
        if part is None:
            part = self.line(jnp.add, *self.sums[i - 2])
        elif i > 1:
            part = self.line(lambda end, p, a, b: jnp.where(end, p, a + b), self.end, part, *self.sums[i - 2])
        self.sent.append(part)
        self.got.append(lax.ppermute(part, "mp", pairs))
        return i

    def middle(self, i):
        if self.four:
            both = self.line(jnp.add, self.parts[i], self.got[i])
            self.sums[i] = both, lax.ppermute(both, "mp", [(1, 2), (2, 1)])

    def total(self, i):
        return (self.sent[i + 2], self.got[i + 2]) if self.four else self.sums[i]


class Line:
    def __init__(self):
        self.last = None

    def after(self, *args):
        if self.last is None:
            return args
        leaves, tree = jax.tree.flatten(args)
        leaves = lax.optimization_barrier((*leaves, self.last))[:-1]
        return jax.tree.unflatten(tree, leaves)

    def __call__(self, f, *args, **kw):
        out = f(*self.after(*args), **kw)
        self.last = jax.tree.leaves(out)[-1]
        return out


SWAP = [(0, 1), (1, 0)]
DP = ("chip", "core")


def behind(x, arrays):
    return lax.optimization_barrier((x, jax.tree.leaves(arrays)))[0]


class Gather:
    def __init__(self, x, low_first):
        self.n = lax.axis_size("chip")
        bits = [1 << b for b in range(self.n.bit_length() - 1)]
        self.bits = bits if low_first else bits[::-1]
        self.own = {0: x}
        self.swapped = {0: lax.ppermute(x, "core", SWAP)}
        self.level = 0

    def step(self):
        bit = self.bits[self.level]
        self.level += 1
        new = {
            r ^ bit: lax.ppermute(b, "chip", [(i, i ^ bit) for i in range(self.n)]) for r, b in self.own.items()
        }
        self.own |= new
        return list(new.values())

    def swap(self):
        for r, b in self.own.items():
            if r not in self.swapped:
                self.swapped[r] = lax.ppermute(b, "core", SWAP)

    def blocks(self):
        while self.level < len(self.bits):
            self.step()
        self.swap()
        return [b[r] for r in range(self.n) for b in (self.own, self.swapped)]


def in_order(stacked, index):
    n = stacked.shape[0]
    bit = 1
    while bit < n:
        parts = stacked.reshape(n // (2 * bit), 2, bit, *stacked.shape[1:])
        stacked = jnp.where(index & bit, parts[:, ::-1], parts).reshape(stacked.shape)
        bit *= 2
    return stacked


def swap_sum(line, x, axis):
    n = lax.axis_size(axis)
    step = 1
    while step < n:
        got = lax.ppermute(x, axis, [(i, i ^ step) for i in range(n)])
        yield
        x = line(jnp.add, x, got)
        step *= 2
    return x


def own_sum(line, rows, index):
    rows = in_order(rows, index)
    half = rows.shape[0] // 2
    while half:
        if half > 1:
            pairs = [(i, i ^ (half // 2)) for i in range(lax.axis_size("chip"))]
            got = lax.ppermute(rows[half:], "chip", pairs)
        else:
            got = lax.ppermute(rows[half:], "core", SWAP)
        yield
        rows = line(jnp.add, rows[:half], got)
        half //= 2
    return rows[0]


def on_device(
    hidden_in,
    cotangent,
    doc_lengths,
    w_query,
    w_key,
    w_value,
    w_out,
    w_gate,
    w_up,
    w_down,
    norm_attn,
    norm_mlp,
    norm_query,
    norm_key,
):
    chips = lax.axis_size("chip")
    n_dp = 2 * chips
    core_id = lax.axis_index("core")
    dp = 2 * lax.axis_index("chip") + core_id
    mp = lax.axis_index("mp")
    n_mp = lax.axis_size("mp")
    tok, d = hidden_in.shape
    nq = w_query.shape[1] // HD
    nk = w_key.shape[1] // HD
    depth = w_query.shape[0]
    small = norm_query.shape[0]
    flag = jnp.stack([((mp == 0) | (mp == n_mp - 1)).astype(jnp.int32), dp])

    wide = (2 * nq + 2 * nk) * HD
    widen = lambda v: jnp.pad(v, (0, wide - v.shape[0]))[None]
    placed = lambda v: widen(lax.dynamic_update_slice(jnp.zeros(HD, BF), v, (dp * small,)))
    gain_rows = jnp.concatenate([widen(norm_attn), widen(norm_mlp), placed(norm_query), placed(norm_key)])
    gain_rows = jnp.pad(gain_rows, ((0, 12), (0, 0)))
    w_attn = pack_call([w_query, w_key, w_value, w_out], gain_rows)
    halves = [Gather(w_attn[:, : wide // 2], True), Gather(w_attn[:, wide // 2 :], False)]
    while halves[0].level < len(halves[0].bits):
        arrived = [h.step() for h in halves]
    w_mlp = behind(pack_call([w_gate, w_up, w_down]), arrived)
    w_mlp = lax.all_gather(w_mlp, DP, axis=0)

    lengths = lax.dynamic_index_in_dim(doc_lengths, dp, 0, keepdims=False)
    ends = jnp.cumsum(lengths)
    ends = ends.astype(jnp.int32)
    token = jnp.arange(tok, dtype=jnp.int32)
    begin = jnp.max(jnp.where(token[:, None] >= ends[None, :], ends[None, :], 0), axis=1)
    position = token - begin
    inverse = ROPE_BASE ** (-(2.0 * jnp.arange(HD // 2, dtype=F32)) / HD)
    angles = position.astype(F32)[:, None] * inverse[None, :]
    cosine = jnp.cos(angles)
    sine = jnp.sin(angles)
    cosine = jnp.concatenate([cosine, cosine], axis=1)
    sine = jnp.concatenate([-sine, sine], axis=1)

    line = Line()

    normed, lin, rot, gain_attn, gain_mlp, gain_query, gain_key, w_attn = line(
        functools.partial(qkv_call, nq=nq, nk=nk), flag, hidden_in, cosine, sine, [h.blocks() for h in halves]
    )

    order = list(reversed(range(tok // CHUNK)))
    att = None
    lse, branch, mid, down, gnt, gn = {}, {}, {}, {}, {}, {}
    stream = Stream(line)
    for k, c in enumerate(order):
        att, lse[c], part = line(functools.partial(attn_call, c, nq=nq, nk=nk), ends, rot, w_attn, att)
        branch[c] = stream.push(part) if k < 2 else part

    c0, c1, c2, c3 = order
    state = {"mlp": None, "back": None, "carry": None, "input": None, "output": None}
    gm = {}
    ff = w_gate.shape[1]

    def run_mlp(c):
        t, r = stream.total(branch[c])
        mid[c], state["mlp"], down[c], gnt_part = line(
            functools.partial(mlp_call, c), flag, hidden_in, t, r, cotangent, gain_mlp,
            w_mlp, state["mlp"],
        )
        gnt[c] = gnt_part

    def run_back(c):
        t, r = stream.total(gnt[c])
        gm[c], state["back"], part, state["carry"] = line(
            functools.partial(back_call, c, nq=nq, nk=nk), flag, ends, mid[c], t, r, cotangent,
            gain_mlp, rot, lse[c], lin, cosine, sine, gain_query, gain_key, w_attn,
            state["back"], state["carry"],
        )
        gn[c] = part

    def run_input(c):
        t, r = stream.total(gn[c])
        state["input"] = line(
            functools.partial(input_call, c), flag, hidden_in, t, r, gm[c], gain_attn, state["input"]
        )

    def run_output(c):
        t, r = stream.total(down[c])
        state["output"] = line(functools.partial(output_call, c, tok=tok), flag, mid[c], t, r, state["output"])

    def push(of, c):
        of[c] = stream.push(line.after(of[c])[0])

    def grad(total, at, a, b, kept=None):
        return line(functools.partial(grad_call, n_dp, total, at), a, b, kept)

    def scatter(g):
        return lax.psum_scatter(line.after(g)[0], DP, scatter_dimension=0, tiled=True)

    stream.middle(branch[c0])
    stream.middle(branch[c1])
    push(branch, c2)
    push(branch, c3)
    stream.middle(branch[c2])
    run_mlp(c0)
    stream.middle(branch[c3])
    push(gnt, c0)
    run_mlp(c1)
    push(gnt, c1)
    stream.middle(gnt[c0])
    run_mlp(c2)
    stream.middle(gnt[c1])
    push(gnt, c2)
    run_mlp(c3)
    n2, prod, gg, gu = state["mlp"]
    push(gnt, c3)
    stream.middle(gnt[c2])
    run_back(c0)
    g_mlp = grad(3 * ff + wide, 0, n2, gg)
    stream.middle(gnt[c3])
    push(gn, c0)
    run_back(c1)
    g_mlp = grad(3 * ff + wide, ff, n2, gu, g_mlp)
    push(down, c0)
    stream.middle(gn[c0])
    run_back(c2)
    g_mlp = grad(3 * ff + wide, 2 * ff, cotangent, prod, g_mlp)
    push(gn, c1)
    stream.middle(down[c0])
    run_back(c3)
    gb, gqkv = state["back"]
    grads = line(functools.partial(grad_pair_call, n_dp, 3 * ff), normed, gqkv, gb, att, g_mlp)
    push(gn, c2)
    stream.middle(gn[c1])
    grads = scatter(grads)
    run_input(c0)
    push(gn, c3)
    stream.middle(gn[c2])
    run_output(c0)
    push(down, c1)
    stream.middle(gn[c3])
    run_input(c1)
    _, sum_mlp, sum_head = state["carry"]
    heads = Sum(line, sum_head, "mp", kind=swap_sum)
    push(down, c2)
    stream.middle(down[c1])
    run_input(c2)
    heads.step()
    push(down, c3)
    stream.middle(down[c2])
    run_input(c3)
    grad_input, sum_attn = state["input"]
    heads = heads.total()
    sums = jnp.concatenate(
        [sum_attn.reshape(n_dp, depth), sum_mlp.reshape(n_dp, depth)]
        + [heads[i].reshape(n_dp, small) for i in range(2)],
        axis=1,
    )
    sums = Sum(line, sums, dp, kind=own_sum)
    stream.push()
    stream.middle(down[c3])
    sums.step()
    run_output(c1)
    sums.step()
    stream.push()
    run_output(c2)
    sums = sums.total()
    widths = (ff, ff, ff, nq * HD, nk * HD, nk * HD, nq * HD)
    outs = line(functools.partial(split_call, widths, (2, 6)), grads)
    run_output(c3)

    return (
        state["output"],
        grad_input,
        *outs[3:6],
        outs[6],
        outs[0],
        outs[1],
        outs[2],
        sums[:depth],
        sums[depth : 2 * depth],
        sums[2 * depth : 2 * depth + small],
        sums[2 * depth + small :],
    )


def solution(mesh):
    n_dp, n_mp = mesh.devices.shape
    mesh = jax.sharding.Mesh(mesh.devices.reshape(n_dp // 2, 2, n_mp), ("chip", "core", "mp"))
    rows = P(DP, None)
    weight = P(DP, "mp")
    turned = P("mp", DP)
    gain = P(DP)
    return jax.shard_map(
        on_device,
        mesh=mesh,
        in_specs=(rows, rows, P(), weight, weight, weight, turned, weight, weight, turned, gain, gain, gain, gain),
        out_specs=(rows, rows, weight, weight, weight, turned, weight, weight, turned, gain, gain, gain, gain),
        check_vma=False,
    )
```
